512 devices in a mesh: gx: 16 (over z), gy: 8 (over y, core), gz: 4 (over x).
Axes of the slice: x: 4, y: 4, z: 16, core: 2. Of those that a mesh axis runs over, the one named last changes fastest.
Arguments:
- right_side: float32 [256, 128, 512], P('gx', 'gy', 'gz'), may hold values from -6 to 6
- conductivity: float32 [256, 128, 512], P('gx', 'gy', 'gz'), may hold values from 0.2 to 5
Outputs:
- solution_field: float32 [256, 128, 512], P('gx', 'gy', 'gz')
The draws below stay inside these ranges and needn't reach their ends.
All inputs are finite; a program needn't handle non-finite values.
Results may differ from the reference program's by a relative error of at most 0.00012.
Values sent between devices are 32-bit elements; how exact they have to be, the bound alone decides.
A program may use at most 128 MiB of HBM per device.

```python
import math
import jax
import jax.numpy as jnp

LEVELS = 4
CG_ITERS = 8
NX = 256
NY = 128
NZ = 512


def shard_levels(stream_key, shape, cuts, smallest, high):
    def one(position, blocks):
        draws = jax.random.uniform(jax.random.fold_in(jax.random.fold_in(stream_key, 6), position), (blocks,), jnp.float32, smallest / len(cuts), high / len(cuts))
        return jnp.repeat(jnp.exp(draws), shape[position] // blocks).reshape((-1,) + (1,) * (len(shape) - position - 1))

    gain = one(*cuts[0])
    for cut in cuts[1:]:
        gain = gain * one(*cut)
    return gain


def centred(stream_key, shape, width, reach, shards=(), dtype=jnp.bfloat16):
    values = width * jax.random.normal(stream_key, shape, jnp.float32)
    if shards:
        values = values * shard_levels(stream_key, shape, shards, -0.22, 0.18)
    return jnp.clip(values, -reach, reach).astype(dtype)


def setup_inputs(seed: int = 0) -> dict:
    seeds = jax.random.split(jax.random.key(seed), 3)
    return {
        "right_side": centred(seeds[0], (NX, NY, NZ), 1.0, 6.0, ((0, 16), (1, 8), (2, 4)), jnp.float32),
        "conductivity": jnp.clip(jnp.exp(math.log(5.0) - 3.218876 * jax.random.uniform(seeds[1], (NX, NY, NZ), jnp.float32) ** shard_levels(seeds[1], (NX, NY, NZ), ((0, 16), (1, 8), (2, 4)), -0.2, 0.2)), 0.2, 5.0),
    }


THETA = 1.125
DELTA = 0.875


def cheb_table():
    sigma = THETA / DELTA
    rho_now = 1.0 / sigma
    table = []
    for sweep in range(3):
        rho_next = 1.0 / (2.0 * sigma - rho_now)
        table.append((rho_next * rho_now, 2.0 * rho_next / DELTA))
        rho_now = rho_next
    return table


def shifted(padded):
    return [padded[2:, 1:-1, 1:-1], padded[:-2, 1:-1, 1:-1], padded[1:-1, 2:, 1:-1],
            padded[1:-1, :-2, 1:-1], padded[1:-1, 1:-1, 2:], padded[1:-1, 1:-1, :-2]]


def total_of(terms):
    running = terms[0]
    for other in terms[1:]:
        running = running + other
    return running


def face_weights(coef_pad, scale):
    centre = coef_pad[1:-1, 1:-1, 1:-1]
    return [(0.5 * scale) * (centre + other) for other in shifted(coef_pad)]


def operate(padded, weights, diagonal):
    return diagonal * padded[1:-1, 1:-1, 1:-1] - total_of([w_face * near for w_face, near in zip(weights, shifted(padded))])


def coarsen(field):
    size_a, size_b, size_c = field.shape
    return jnp.mean(field.reshape(size_a // 2, 2, size_b // 2, 2, size_c // 2, 2), axis=(1, 3, 5))


def refine(field):
    size_a, size_b, size_c = field.shape
    spread = jnp.broadcast_to(field[:, None, :, None, :, None], (size_a, 2, size_b, 2, size_c, 2))
    return spread.reshape(2 * size_a, 2 * size_b, 2 * size_c)


def level_parts(conductivity, scale):
    weights = face_weights(jnp.pad(conductivity, 1), scale)
    diagonal = total_of(weights)
    return weights, diagonal, 1.0 / diagonal


def presmooth(source, parts):
    weights, diagonal, inverse = parts
    table = cheb_table()
    solution = jnp.zeros_like(source)
    residual = source
    step_dir = inverse * residual / THETA
    for sweep in range(4):
        solution = solution + step_dir
        residual = residual - operate(jnp.pad(step_dir, 1), weights, diagonal)
        if sweep < 3:
            step_dir = table[sweep][0] * step_dir + table[sweep][1] * (inverse * residual)
    return solution, residual


def postsmooth(source, solution, parts):
    weights, diagonal, inverse = parts
    table = cheb_table()
    residual = source - operate(jnp.pad(solution, 1), weights, diagonal)
    step_dir = inverse * residual / THETA
    for sweep in range(4):
        solution = solution + step_dir
        if sweep < 3:
            residual = residual - operate(jnp.pad(step_dir, 1), weights, diagonal)
            step_dir = table[sweep][0] * step_dir + table[sweep][1] * (inverse * residual)
    return solution


def bottom_solve(source, conductivity, scale):
    weights, diagonal, inverse = level_parts(conductivity, scale)
    solution = jnp.zeros_like(source)
    residual = source
    direction = source
    norm_now = jnp.sum(residual * residual)
    for sweep in range(CG_ITERS):
        image = operate(jnp.pad(direction, 1), weights, diagonal)
        alpha = norm_now / jnp.sum(direction * image)
        solution = solution + alpha * direction
        residual = residual - alpha * image
        norm_next = jnp.sum(residual * residual)
        direction = residual + (norm_next / norm_now) * direction
        norm_now = norm_next
    return solution


def cycle(source, conductivity, level):
    scale = 0.25 ** level
    if level == LEVELS:
        return bottom_solve(source, conductivity, scale)
    parts = level_parts(conductivity, scale)
    solution, residual = presmooth(source, parts)
    correction = cycle(coarsen(residual), coarsen(conductivity), level + 1)
    solution = solution + refine(correction)
    return postsmooth(source, solution, parts)


def reference(right_side, conductivity):
    return cycle(right_side, conductivity, 0)
```

```python
import functools

import jax
import jax.numpy as jnp
from jax import lax
from jax.experimental import pallas as pl
from jax.experimental.pallas import tpu as pltpu
from jax.sharding import PartitionSpec as P

F32 = jnp.float32
MESH = pl.DeviceIdType.MESH
CG_ITERS = 8
THETA = 1.125
DELTA = 0.875

H0, H0R = 5, 3
H1K, H1F, H1R = 6, 4, 5


def cheb_table():
    sigma = THETA / DELTA
    rho_now = 1.0 / sigma
    table = []
    for _ in range(3):
        rho_next = 1.0 / (2.0 * sigma - rho_now)
        table.append((rho_next * rho_now, 2.0 * rho_next / DELTA))
        rho_now = rho_next
    return table


TABLE = cheb_table()


def mm(a, b):
    return jnp.dot(a, b, precision=lax.Precision.HIGHEST, preferred_element_type=F32)


def iota(shape, dim):
    return lax.broadcasted_iota(jnp.int32, shape, dim)


def flat(v):
    return v.reshape(v.shape[0] * v.shape[1], v.shape[2])


def up(v, dim, step=1):
    return pltpu.roll(v, v.shape[dim] - step, dim)


def down(v, dim, step=1):
    return pltpu.roll(v, step, dim)


def planes_loop(lo, hi, group, fn):
    count = (hi - lo) // group
    if count > 1:
        def body(i, carry):
            fn(lo + i * group, group)
            return carry

        lax.fori_loop(0, count, body, 0)
    elif count == 1:
        fn(lo, group)
    rest = hi - lo - count * group
    if rest:
        fn(lo + count * group, rest)


def weights(lev, lo, hi, h, whole, group):
    K = lev["K"]
    rows, lanes = K.shape[1], K.shape[2]

    def one(p, g):
        n = g * rows
        k = flat(K[pl.ds(p, g)])
        kxu = flat(K[pl.ds(p + 1, g)])
        kxd = flat(K[pl.ds(p - 1, g)])
        kyu, kyd, kzu, kzd = up(k, 0), down(k, 0), up(k, 1), down(k, 1)
        if whole:
            row = iota((n, lanes), 0) & (rows - 1)
            lane = iota((n, lanes), 1)
            kyu = jnp.where(row == rows - 1, 0.0, kyu)
            kyd = jnp.where(row == 0, 0.0, kyd)
            kzu = jnp.where(lane == lanes - 1, 0.0, kzu)
            kzd = jnp.where(lane == 0, 0.0, kzd)
        wy, wz = h * (k + kyu), h * (k + kzu)
        diag = h * (6.0 * k + ((kxu + kxd) + (kyu + kyd) + (kzu + kzd)))
        if whole:
            wy = jnp.where(row == rows - 1, 0.0, wy)
            wz = jnp.where(lane == lanes - 1, 0.0, wz)
        shape = (g, rows, lanes)
        lev["WX"][pl.ds(p, g)] = (h * (k + kxu)).reshape(shape)
        lev["WY"][pl.ds(p, g)] = wy.reshape(shape)
        lev["WZ"][pl.ds(p, g)] = wz.reshape(shape)
        lev["DG"][pl.ds(p, g)] = diag.reshape(shape)
        lev["IV"][pl.ds(p, g)] = jnp.where(k > 0.0, 1.0 / diag, 0.0).reshape(shape)

    lev["WX"][lo - 1] = h * (K[lo - 1] + K[lo])
    planes_loop(lo, hi, group, one)


def sweep(lev, R, X, src, dst, lo, hi, a, b, group, first=False, want_dir=True):
    Vi, Vo = lev[src], lev[dst]
    rows, lanes = Vi.shape[1], Vi.shape[2]

    def one(p, g):
        here = pl.ds(p, g)
        shape = (g, rows, lanes)
        v = flat(Vi[here])
        total = flat(lev["WX"][here]) * flat(Vi[pl.ds(p + 1, g)])
        total = total + flat(lev["WX"][pl.ds(p - 1, g)]) * flat(Vi[pl.ds(p - 1, g)])
        wy, wz = flat(lev["WY"][here]), flat(lev["WZ"][here])
        total = total + (wy * up(v, 0) + down(wy * v, 0))
        total = total + (wz * up(v, 1) + down(wz * v, 1))
        r = flat(R[here]) - (flat(lev["DG"][here]) * v - total)
        R[here] = r.reshape(shape)
        if first:
            X[here] = v.reshape(shape)
        else:
            X[here] = X[here] + v.reshape(shape)
        if want_dir:
            d = b * (flat(lev["IV"][here]) * r)
            if a:
                d = d + a * v
            Vo[here] = d.reshape(shape)

    planes_loop(lo, hi, group, one)


def presmooth(lev, R, X, halos, base, own, group, whole=False):
    h = 0 if whole else halos[0] + 1
    lo, hi = base - h, base + own + h

    def start(p, g):
        here = pl.ds(p, g)
        lev["Va"][here] = (lev["IV"][here] * R[here]) * (1.0 / THETA)

    planes_loop(lo, hi, group, start)
    names = ("Va", "Vb")
    for j in range(4):
        a, b = TABLE[j] if j < 3 else (0.0, 0.0)
        lo, hi = base - halos[j], base + own + halos[j]
        sweep(lev, R, X, names[j % 2], names[1 - j % 2], lo, hi, a, b, group,
              first=(j == 0), want_dir=(j < 3))


def postsmooth(lev, R, X, halos, base, own, group):
    names = ("Va", "Vb")
    for j in range(4):
        a, b = TABLE[j - 1] if j > 0 else (0.0, 1.0 / THETA)
        lo, hi = base - halos[j], base + own + halos[j]
        sweep(lev, R, X, names[j % 2], names[1 - j % 2], lo, hi, a, b, group)


def kernel(sizes, names, *refs):
    f_ref, k_ref, out_ref = refs[:3]
    S = dict(zip(names, refs[3:]))
    ss, rs = S["ss"], S["rs"]
    NGX, NGY, NGZ = sizes
    NYC = NGY // 2
    NX0, NY0, NZ0 = 16 * NGX, 16 * NGY, 128 * NGZ
    NX1, NY1, NZ1 = NX0 // 2, NY0 // 2, NZ0 // 2
    NX3 = 2 * NGX
    gx, gy, gz = lax.axis_index("gx"), lax.axis_index("gy"), lax.axis_index("gz")
    core, chip = gy % 2, gy // 2

    def at(dx=0, dy=0, dz=0):
        return ((gx + dx + NGX) % NGX, (gy + dy + NGY) % NGY, (gz + dz + NGZ) % NGZ)

    pair_peers = [(c, dz) for c in (0, 1) for dz in range(NGZ) if (c, dz) != (0, 0)]

    def pair_dev(c, dz):
        return (gx, chip * 2 + (core + c) % 2, (gz + dz) % NGZ)

    def chip_dev(dy):
        return (gx, ((chip + dy) % NYC) * 2 + core, gz)

    sides = [(dx, dy) for dx in (-1, 0, 1) for dy in (-1, 0, 1) if (dx, dy) != (0, 0)]

    barrier = pltpu.get_barrier_semaphore()
    greeted = [pair_dev(c, dz) for c, dz in pair_peers]
    greeted += [chip_dev(dy) for dy in range(1, NYC)]
    greeted += [at(dx=d) for d in range(1, NGX)]
    greeted += [at(dx=dx, dy=dy) for dx, dy in sides if dy != 0]
    for dev in greeted:
        pl.semaphore_signal(barrier, inc=1, device_id=dev, device_id_type=MESH)

    counter = [0]

    def remote(src, dst, dev):
        i = counter[0]
        counter[0] += 1
        return pltpu.make_async_remote_copy(
            src_ref=src, dst_ref=dst, send_sem=ss.at[i], recv_sem=rs.at[i],
            device_id=dev, device_id_type=MESH,
        )

    def begin(copies):
        for c in copies:
            c.start()
        return copies

    def finish(copies):
        for c in copies:
            c.wait()

    def z_copies(buf, from_left, from_right):
        return [remote(buf, from_left, at(dz=1)), remote(buf, from_right, at(dz=-1))]

    def xy_copies(buf, base, own, h, rows):
        fields = slice(None)
        xs = {1: (base + own - h, base - h, h), -1: (base, base + own, h), 0: (base, base, own)}
        ys = {1: (rows, 0, 8), -1: (8, 8 + rows, 8), 0: (8, 8, rows)}
        out = []
        for dx, dy in sides:
            (sx, tx, nx), (sy, ty, ny) = xs[dx], ys[dy]
            out.append(remote(
                buf.at[fields, pl.ds(sx, nx), pl.ds(sy, ny)],
                buf.at[fields, pl.ds(tx, nx), pl.ds(ty, ny)],
                at(dx=dx, dy=dy)))
        return out

    def x_copies(buf, n1, n2):
        out = []
        for d, n in ((1, n1), (2, n2)):
            if n:
                out.append(remote(buf.at[:, pl.ds(11 - n, n)],
                                  buf.at[:, pl.ds(7 - 4 * (d - 1) - n, n)], at(dx=d)))
                out.append(remote(buf.at[:, pl.ds(7, n)],
                                  buf.at[:, pl.ds(11 + 4 * (d - 1), n)], at(dx=-d)))
        return out

    def pair_copies(buf, slots):
        return [remote(buf, slots.at[i], pair_dev(c, dz)) for i, (c, dz) in enumerate(pair_peers)]

    def chip_copies(buf):
        mine = buf.at[0, pl.ds(7, 4), pl.ds(pl.multiple_of(chip * 8, 8), 8)]
        return [remote(mine, mine, chip_dev(dy)) for dy in range(1, NYC)]

    def gather_copies(buf):
        return [remote(buf.at[gx], buf.at[gx], at(dx=d)) for d in range(1, NGX)]

    lane16 = iota((16, 128), 1)
    lane8 = iota((8, 128), 1)

    def sel(shape, cond, value):
        return jnp.where(cond(iota(shape, 0), iota(shape, 1)), value, 0.0).astype(F32)

    def coarse_0(r):
        c = sel((64, 256), lambda r, c: ((c >> 5) == (r >> 3)) & (((c & 15) >> 1) == (r & 7)), 0.25)
        z = sel((128, 128), lambda l, c: (l >> 1) == (c & 63), 0.5)
        return mm(mm(c, r), z)

    def coarse_1(r):
        c = sel((32, 64), lambda r, c: ((c >> 4) == (r >> 3)) & (((c & 7) >> 1) == (r & 7) - 4 * core), 0.25)
        z = sel((128, 128), lambda l, c: (l < 64) & (c == 32 * gz + (l >> 1)), 0.5)
        return mm(mm(c, r), z)

    def coarse_2(r):
        c = sel((32, 128), lambda r, c: ((c >> 6) == (r >> 4)) & (((c & 31) >> 1) == (r & 15)), 0.25)
        z = sel((128, 128), lambda l, c: (l >> 1) == (c & 63), 0.5)
        t = mm(mm(c, r), z)
        return jnp.where(lane16 < 64, t[0:16], t[16:32])

    def coarse_3(r):
        n = r.shape[0]
        c = sel((n // 4, n), lambda r, c: ((c >> 5) == (r >> 3)) & (((c & 15) >> 1) == (r & 7)), 0.25)
        z = sel((128, 128), lambda l, c: (l < 64) & ((l >> 1) == c), 0.5)
        return mm(mm(c, r), z)

    def fine_3(e):
        n = e.shape[0]
        u = sel((4 * n, n), lambda r, c: ((r >> 5) == (c >> 3)) & (((r & 15) >> 1) == (c & 7)), 1.0)
        z = sel((128, 128), lambda c, l: (l < 64) & ((l >> 1) == c), 1.0)
        return mm(u, mm(e, z))

    def pack0(field):
        out = []
        for g in range(2):
            acc = None
            for j in range(8):
                t = pltpu.roll(field(8 * g + j), 16 * j + 8, 1)
                acc = t if acc is None else jnp.where((lane16 >> 4) == j, t, acc)
            out.append(acc)
        return out

    def centre0(buf, fld, h, field, from_left, from_right):
        base = h + 1
        for g, m in ((0, base), (1, base + 17)):
            buf[fld, m, 8:24] = jnp.where((lane16 & 15) >= 8, from_right[fld, g], from_left[fld, g])

    def body0(buf, fld, h, ref):
        base = h + 1
        buf[fld, base + 1:base + 17, 8:24] = ref[...]

    def unpack0(buf, fld, h, lo, hi, put):
        for x in range(lo, hi):
            if x < 0:
                main, m, j = x + h, h, x + 8
            elif x < 16:
                main, m, j = h + 2 + x, (h + 1 if x < 8 else h + 18), x % 8
            else:
                main, m, j = h + 20 + x - 16, h + 19, x - 16
            put(x, buf[fld, main], pltpu.roll(buf[fld, m], (120 - 16 * j) % 128, 1))

    def double1(v):
        n = v.shape[0]
        return jnp.where(iota((n, 128), 1) < 64, v, pltpu.roll(v, 64, 1))

    def centre1(buf, fld, own, left, right, i):
        lane = iota((64, 128), 1)
        t = jnp.where(lane < 64, flat(own[i]), jnp.where(lane < 96, flat(right[i]), flat(left[i])))
        buf[fld, 6:14, 8:16] = t.reshape(8, 8, 128)

    def inside(n_rows, n_lanes, row0, lane_of, ny, nz):
        y = iota((n_rows, n_lanes), 0) + row0
        z = lane_of(iota((n_rows, n_lanes), 1))
        return jnp.where((y >= 0) & (y < ny) & (z >= 0) & (z < nz), 1.0, 0.0).astype(F32)

    def xin(x, n):
        return jnp.where((x >= 0) & (x < n), 1.0, 0.0).astype(F32)

    L0 = {n: S[n + "0"] for n in ("K", "WX", "WY", "WZ", "DG", "IV", "Va", "Vb")}
    L1 = {n: S[n + "1"] for n in ("WX", "WY", "WZ", "DG", "IV", "Va", "Vb")}
    L1["K"] = S["K1"].at[0]
    L2 = {n: S[n + "2"] for n in ("WX", "WY", "WZ", "DG", "IV", "Va", "Vb")}
    L2["K"] = S["K2"].at[0]
    L3 = {n: S[n + "3"] for n in ("K", "WX", "WY", "WZ", "DG", "IV", "Va", "Vb")}
    R0, X0 = S["R0"], S["X0"]
    F1, X1 = S["F1"].at[0], S["X1"]
    F2, X2 = S["F2"].at[0], S["X2"]
    F3, X3 = S["F3"], S["X3"]

    E0, E0r = S["E0"], S["E0r"]
    for fld, ref in ((0, f_ref), (1, k_ref)):
        for g, t in enumerate(pack0(lambda x: ref[x])):
            S["P0"][fld, g] = t
        body0(E0, fld, H0, ref)
    k1 = coarse_0(k_ref[...].reshape(256, 128))
    S["T1k"][0] = k1.reshape(8, 8, 128)
    S["B2k"][...] = coarse_1(k1).reshape(4, 8, 128)

    pl.semaphore_wait(barrier, len(greeted))
    z0 = begin(z_copies(S["P0"], S["P0L"], S["P0R"]))
    z1k = begin(z_copies(S["T1k"], S["T1kL"], S["T1kR"]))
    p2k = begin(pair_copies(S["B2k"], S["B2kS"]))

    finish(z0)
    for fld in (0, 1):
        centre0(E0, fld, H0, None, S["P0L"], S["P0R"])
    xy0 = begin(xy_copies(E0, H0 + 1, 18, H0 + 1, 16))
    finish(z1k)
    centre1(S["K1"], 0, S["T1k"], S["T1kL"], S["T1kR"], 0)
    xy1k = begin(xy_copies(S["K1"], 6, 8, H1K, 8))
    finish(p2k)

    def pair_sum(own, slots):
        total = own[...]
        for i in range(len(pair_peers)):
            total = total + slots[i]
        return total

    my_rows = pl.ds(pl.multiple_of(chip * 8, 8), 8)
    if NYC * 8 < 32:
        S["K2"][...] = jnp.zeros(S["K2"].shape, F32)
        S["F2"][...] = jnp.zeros(S["F2"].shape, F32)
    S["K2"][0, 7:11, my_rows] = pair_sum(S["B2k"], S["B2kS"])
    c2k = begin(chip_copies(S["K2"]))

    finish(xy0)

    def lane0(l):
        return 128 * gz + jnp.where(l < 192, l, l - 256)

    in0 = inside(32, 256, 16 * gy - 8, lane0, NY0, NZ0)

    def put_k(x, main, halo):
        w = xin(16 * gx + x, NX0)
        L0["K"][x + 5, :, 0:128] = main * (in0[:, 0:128] * w)
        L0["K"][x + 5, :, 128:256] = halo * (in0[:, 128:256] * w)

    def put_r(x, main, halo):
        R0[x + 5, :, 0:128] = main
        R0[x + 5, :, 128:256] = halo

    unpack0(E0, 1, H0, -5, 21, put_k)
    unpack0(E0, 0, H0, -4, 20, put_r)
    weights(L0, 1, 25, 0.5, False, 1)

    finish(c2k)
    xx2k = begin(x_copies(S["K2"], 4, 3))
    S["G3k"][gx] = coarse_2(S["K2"][0, 7:11].reshape(128, 128))
    g3k = begin(gather_copies(S["G3k"]))

    presmooth(L0, R0, X0, (3, 2, 1, 0), 5, 16, 1)

    own0 = R0[5:21, 8:24, 0:128]
    S["T1f"][0] = coarse_0(own0.reshape(256, 128)).reshape(8, 8, 128)
    z1f = begin(z_copies(S["T1f"], S["T1fL"], S["T1fR"]))
    for g, t in enumerate(pack0(lambda x: R0[5 + x, 8:24, 0:128])):
        S["P0r"][0, g] = t
    E0r[0, H0R + 2:H0R + 18, 8:24] = own0
    z0r = begin(z_copies(S["P0r"], S["P0rL"], S["P0rR"]))

    finish(xy1k)

    def lane1(l):
        return 64 * gz + jnp.where(l < 96, l, l - 128)

    in1 = inside(24, 128, 8 * gy - 8, lane1, NY1, NZ1)
    for p in range(20):
        L1["K"][p] = L1["K"][p] * (in1 * xin(8 * gx + p - 6, NX1))
    weights(L1, 1, 19, 0.5 * 0.25, False, 2)

    finish(z1f)
    centre1(S["F1"], 0, S["T1f"], S["T1fL"], S["T1fR"], 0)
    xy1f = begin(xy_copies(S["F1"], 6, 8, H1F, 8))
    finish(z0r)
    centre0(E0r, 0, H0R, None, S["P0rL"], S["P0rR"])
    xy0r = begin(xy_copies(E0r, H0R + 1, 18, H0R + 1, 16))
    finish(xy1f)
    presmooth(L1, F1, X1, (3, 2, 1, 0), 6, 8, 2)

    r1 = F1[6:14, 8:16]
    S["B2f"][...] = coarse_1(r1.reshape(64, 128)).reshape(4, 8, 128)
    p2f = begin(pair_copies(S["B2f"], S["B2fS"]))
    S["T1r"][0] = double1(r1.reshape(64, 128)).reshape(8, 8, 128)
    S["T1r"][1] = double1(X1[6:14, 8:16].reshape(64, 128)).reshape(8, 8, 128)
    z1r = begin(z_copies(S["T1r"], S["T1rL"], S["T1rR"]))

    finish(xx2k)
    for p in range(18):
        if p < 7 or p > 10:
            L2["K"][p] = L2["K"][p] * xin(4 * gx + p - 7, NX1 // 2)
    weights(L2, 1, 17, 0.5 * 0.25 ** 2, True, 2)

    finish(p2f)
    S["F2"][0, 7:11, my_rows] = pair_sum(S["B2f"], S["B2fS"])
    c2f = begin(chip_copies(S["F2"]))
    finish(z1r)
    for i in (0, 1):
        centre1(S["RX1"], i, S["T1r"], S["T1rL"], S["T1rR"], i)
    finish(c2f)
    xx2f = begin(x_copies(S["F2"], 4, 0))
    xy1r = begin(xy_copies(S["RX1"], 6, 8, H1R, 8))

    finish(g3k)

    def unpack3(slots, dst):
        for s in range(NGX):
            t = slots[s]
            dst[5 + 2 * s] = jnp.where(lane16 < 64, t, 0.0)
            dst[6 + 2 * s] = jnp.where(lane16 < 64, pltpu.roll(t, 64, 1), 0.0)

    unpack3(S["G3k"], L3["K"])
    zero3 = jnp.zeros((5, 16, 128), F32)
    for ref in (L3["K"], L3["Va"], L3["Vb"], X3):
        ref[0:5] = zero3
        ref[5 + NX3:10 + NX3] = zero3
    weights(L3, 5, 5 + NX3, 0.5 * 0.25 ** 3, True, 4)

    finish(xx2f)
    presmooth(L2, F2, X2, (3, 2, 1, 0), 7, 4, 2)

    S["G3f"][gx] = coarse_2(F2[7:11].reshape(128, 128))
    g3f = begin(gather_copies(S["G3f"]))
    S["RX2"][0, 7:11] = F2[7:11]
    S["RX2"][1, 7:11] = X2[7:11]
    xx2r = begin(x_copies(S["RX2"], 4, 2))

    n4 = 8 * (NX3 // 2)
    h4 = 0.5 * 0.25 ** 4
    k4 = coarse_3(L3["K"][5:5 + NX3].reshape(16 * NX3, 128))
    row4 = iota((n4, 128), 0)
    plane_end = (row4 & 7) == 7
    last_plane = row4 >= n4 - 8
    first_plane = row4 < 8
    k4xu = jnp.where(last_plane, 0.0, up(k4, 0, 8))
    k4xd = jnp.where(first_plane, 0.0, down(k4, 0, 8))
    k4yu = jnp.where(plane_end, 0.0, up(k4, 0))
    k4yd = jnp.where((row4 & 7) == 0, 0.0, down(k4, 0))
    k4zu, k4zd = up(k4, 1), down(k4, 1)
    wx4 = jnp.where(last_plane, 0.0, h4 * (k4 + k4xu))
    wy4 = jnp.where(plane_end, 0.0, h4 * (k4 + k4yu))
    wz4 = h4 * (k4 + k4zu)
    dg4 = h4 * (6.0 * k4 + ((k4xu + k4xd) + (k4yu + k4yd) + (k4zu + k4zd)))

    finish(g3f)
    unpack3(S["G3f"], F3)
    presmooth(L3, F3, X3, (0, 0, 0, 0), 5, NX3, 4, whole=True)

    f4 = coarse_3(F3[5:5 + NX3].reshape(16 * NX3, 128))
    f4 = jnp.where(k4 > 0.0, f4, 0.0)
    x4 = jnp.zeros_like(f4)
    r4 = p4 = f4
    rr = jnp.sum(r4 * r4, keepdims=True)
    for _ in range(CG_ITERS):
        q4 = dg4 * p4 - (
            (wx4 * up(p4, 0, 8) + down(wx4 * p4, 0, 8))
            + (wy4 * up(p4, 0) + down(wy4 * p4, 0))
            + (wz4 * up(p4, 1) + down(wz4 * p4, 1)))
        q4 = jnp.where(k4 > 0.0, q4, 0.0)
        alpha = rr / jnp.sum(p4 * q4, keepdims=True)
        x4 = x4 + alpha * p4
        r4 = r4 - alpha * q4
        rn = jnp.sum(r4 * r4, keepdims=True)
        p4 = r4 + (rn / rr) * p4
        rr = rn

    L3["Va"][5:5 + NX3] = fine_3(x4).reshape(NX3, 16, 128)
    postsmooth(L3, F3, X3, (0, 0, 0, 0), 5, NX3, 4)
    X3[5:5 + NX3] = X3[5:5 + NX3] + L3["Va"][5:5 + NX3]

    finish(xx2r)
    z3 = sel((128, 128), lambda c, l: (l >> 1) == c, 1.0)
    y3 = sel((32, 16), lambda r, c: (r >> 1) == c, 1.0)
    t = mm(X3[pl.ds(2 * gx + 1, 10)].reshape(160, 128), z3)
    for q in range(10):
        e = mm(y3, t[16 * q:16 * q + 16])
        for p in (2 * q - 1, 2 * q):
            if 0 <= p < 18:
                L2["Va"][p] = e
    R2b, X2b = S["RX2"].at[0], S["RX2"].at[1]
    postsmooth(L2, R2b, X2b, (6, 5, 4, 3), 7, 4, 2)
    X2b[4:14] = X2b[4:14] + L2["Va"][4:14]

    finish(xy1r)
    z2 = sel((128, 128), lambda c, l: ((lane1(l) >> 1) == c) & (lane1(l) >= 0) & (lane1(l) < NZ1), 1.0)

    def yrow(r):
        return 8 * gy + r - 8

    y2 = sel((24, 32), lambda r, c: ((yrow(r) >> 1) == c) & (yrow(r) >= 0) & (yrow(r) < NY1), 1.0)
    t = mm(X2b[4:14].reshape(320, 128), z2)
    for q in range(10):
        e = mm(y2, t[32 * q:32 * q + 32])
        e = e * xin(4 * gx + q - 3, NX1 // 2)
        L1["Va"][2 * q] = e
        L1["Va"][2 * q + 1] = e
    R1b, X1b = S["RX1"].at[0], S["RX1"].at[1]
    postsmooth(L1, R1b, X1b, (5, 4, 3, 2), 6, 8, 2)
    X1b[4:16] = X1b[4:16] + L1["Va"][4:16]

    finish(xy0r)
    unpack0(E0r, 0, H0R, -3, 19, put_r)

    def zfine(c, l):
        z = jnp.where(l < 192, l, l - 256)
        g = 128 * gz + z
        return (((z >> 1) & 127) == c) & (g >= 0) & (g < NZ0)

    def yfine(r, c):
        g = 16 * gy + r - 8
        return (((r - 8) >> 1) + 8 == c) & (g >= 0) & (g < NY0)

    z1 = sel((128, 256), zfine, 1.0)
    y1 = sel((32, 24), yfine, 1.0)
    t = mm(X1b[4:16].reshape(288, 128), z1)
    for q in range(12):
        e = mm(y1, t[24 * q:24 * q + 24])
        e = e * xin(8 * gx + q - 2, NX1)
        L0["Va"][1 + 2 * q] = e
        L0["Va"][2 + 2 * q] = e
    postsmooth(L0, R0, X0, (3, 2, 1, 0), 5, 16, 1)
    out_ref[...] = X0[5:21, 8:24, 0:128] + L0["Va"][5:21, 8:24, 0:128]


def scratch(sizes):
    ngx, ngy, ngz = sizes
    n_pair = 2 * ngz - 1
    shapes = {
        "P0": (2, 2, 16, 128), "P0L": (2, 2, 16, 128), "P0R": (2, 2, 16, 128),
        "E0": (2, 18 + 2 * (H0 + 1), 32, 128),
        "P0r": (1, 2, 16, 128), "P0rL": (1, 2, 16, 128), "P0rR": (1, 2, 16, 128),
        "E0r": (1, 18 + 2 * (H0R + 1), 32, 128),
        "R0": (26, 32, 256), "X0": (26, 32, 256), "K0": (26, 32, 256),
        "T1r": (2, 8, 8, 128), "T1rL": (2, 8, 8, 128), "T1rR": (2, 8, 8, 128),
        "K1": (1, 20, 24, 128), "F1": (1, 20, 24, 128), "RX1": (2, 20, 24, 128), "X1": (20, 24, 128),
        "K2": (1, 18, 32, 128), "F2": (1, 18, 32, 128), "RX2": (2, 18, 32, 128), "X2": (18, 32, 128),
        "B2k": (4, 8, 128), "B2kS": (n_pair, 4, 8, 128),
        "B2f": (4, 8, 128), "B2fS": (n_pair, 4, 8, 128),
        "G3k": (ngx, 16, 128), "G3f": (ngx, 16, 128),
        "K3": (2 * ngx + 10, 16, 128), "F3": (2 * ngx + 10, 16, 128), "X3": (2 * ngx + 10, 16, 128),
    }
    for n in ("T1k", "T1f"):
        for side in ("", "L", "R"):
            shapes[n + side] = (1, 8, 8, 128)
    for n in ("WX", "WY", "WZ", "DG", "IV", "Va", "Vb"):
        shapes[n + "0"] = (26, 32, 256)
        shapes[n + "1"] = (20, 24, 128)
        shapes[n + "2"] = (18, 32, 128)
        shapes[n + "3"] = (2 * ngx + 10, 16, 128)
    names = list(shapes) + ["ss", "rs"]
    n_sem = 4 * 10 + 10 + 2 * (n_pair + max(ngy // 2 - 1, 0)) + 4 + 2 + 4 + 2 * (ngx - 1)
    kinds = [pltpu.VMEM(shapes[n], F32) for n in shapes]
    kinds += [pltpu.SemaphoreType.DMA((n_sem,)), pltpu.SemaphoreType.DMA((n_sem,))]
    return names, kinds


def solution(mesh):
    sizes = (mesh.shape["gx"], mesh.shape["gy"], mesh.shape["gz"])
    names, kinds = scratch(sizes)
    spec = P("gx", "gy", "gz")

    def local(right_side, conductivity):
        return pl.pallas_call(
            functools.partial(kernel, sizes, names),
            out_shape=jax.ShapeDtypeStruct(right_side.shape, F32),
            in_specs=[pl.BlockSpec(memory_space=pltpu.VMEM)] * 2,
            out_specs=pl.BlockSpec(memory_space=pltpu.VMEM),
            scratch_shapes=kinds,
            compiler_params=pltpu.CompilerParams(
                collective_id=0, has_side_effects=True, vmem_limit_bytes=48 * 1024 * 1024
            ),
        )(right_side, conductivity)

    return jax.shard_map(local, mesh=mesh, in_specs=(spec, spec), out_specs=spec, check_vma=False)
```

```python
import functools

import jax
import jax.numpy as jnp
from jax import lax
from jax.experimental import pallas as pl
from jax.experimental.pallas import tpu as pltpu
from jax.sharding import PartitionSpec as P

F32 = jnp.float32
MESH = pl.DeviceIdType.MESH
CG_ITERS = 8
THETA = 1.125
DELTA = 0.875

H0, H0R = 5, 3
H1K, H1F, H1R = 6, 4, 5

G0, G1, G2, G3 = 4, 8, 8, 16
OWN0 = (slice(8, 24), slice(0, 128))


def cheb_table():
    sigma = THETA / DELTA
    rho_now = 1.0 / sigma
    table = []
    for _ in range(3):
        rho_next = 1.0 / (2.0 * sigma - rho_now)
        table.append((rho_next * rho_now, 2.0 * rho_next / DELTA))
        rho_now = rho_next
    return table


TABLE = cheb_table()


def mm(a, b):
    return jnp.dot(a, b, precision=lax.Precision.HIGHEST, preferred_element_type=F32)


def iota(shape, dim):
    return lax.broadcasted_iota(jnp.int32, shape, dim)


def flat(v):
    return v.reshape(v.shape[0] * v.shape[1], v.shape[2])


def up(v, dim, step=1):
    return pltpu.roll(v, v.shape[dim] - step, dim)


def down(v, dim, step=1):
    return pltpu.roll(v, step, dim)


def planes_loop(lo, hi, group, fn):
    count = (hi - lo) // group
    if count > 1:
        def body(i, carry):
            fn(lo + i * group, group)
            return carry

        lax.fori_loop(0, count, body, 0)
    elif count == 1:
        fn(lo, group)
    rest = hi - lo - count * group
    if rest:
        fn(lo + count * group, rest)


def weights(lev, lo, hi, h, whole, group):
    K = lev["K"]
    rows, lanes = K.shape[1], K.shape[2]

    def one(p, g):
        n = g * rows
        k = flat(K[pl.ds(p, g)])
        kxu = flat(K[pl.ds(p + 1, g)])
        kxd = flat(K[pl.ds(p - 1, g)])
        kyu, kyd, kzu, kzd = up(k, 0), down(k, 0), up(k, 1), down(k, 1)
        if whole:
            row = iota((n, lanes), 0) & (rows - 1)
            lane = iota((n, lanes), 1)
            kyu = jnp.where(row == rows - 1, 0.0, kyu)
            kyd = jnp.where(row == 0, 0.0, kyd)
            kzu = jnp.where(lane == lanes - 1, 0.0, kzu)
            kzd = jnp.where(lane == 0, 0.0, kzd)
        wy, wz = h * (k + kyu), h * (k + kzu)
        diag = h * (6.0 * k + ((kxu + kxd) + (kyu + kyd) + (kzu + kzd)))
        if whole:
            wy = jnp.where(row == rows - 1, 0.0, wy)
            wz = jnp.where(lane == lanes - 1, 0.0, wz)
        shape = (g, rows, lanes)
        lev["WX"][pl.ds(p, g)] = (h * (k + kxu)).reshape(shape)
        lev["WY"][pl.ds(p, g)] = wy.reshape(shape)
        lev["WZ"][pl.ds(p, g)] = wz.reshape(shape)
        lev["DG"][pl.ds(p, g)] = diag.reshape(shape)
        lev["IV"][pl.ds(p, g)] = jnp.where(k > 0.0, 1.0 / diag, 0.0).reshape(shape)

    lev["WX"][lo - 1] = h * (K[lo - 1] + K[lo])
    planes_loop(lo, hi, group, one)


def sweep(lev, R, X, src, dst, lo, hi, a, b, group, first=False, want_dir=True, part=None):
    Vi, Vo = lev[src], lev[dst]

    def one(p, g):
        v = [Vi[p - 1 + i] for i in range(g + 2)]
        wx = [lev["WX"][p - 1 + i] for i in range(g + 1)]
        for i in range(g):
            c = v[i + 1]
            wy, wz = lev["WY"][p + i], lev["WZ"][p + i]
            total = wx[i + 1] * v[i + 2] + wx[i] * v[i]
            total = total + (wy * up(c, 0) + down(wy * c, 0))
            total = total + (wz * up(c, 1) + down(wz * c, 1))
            r = R[p + i] - (lev["DG"][p + i] * c - total)
            R[p + i] = r
            own = c if part is None else c[part[0], part[1]]
            X[p + i] = own if first else X[p + i] + own
            if want_dir:
                d = b * (lev["IV"][p + i] * r)
                Vo[p + i] = d + a * c if a else d

    planes_loop(lo, hi, group, one)


def presmooth(lev, R, X, halos, base, own, group, whole=False, part=None, after=None):
    h = 0 if whole else halos[0] + 1
    lo, hi = base - h, base + own + h

    def start(p, g):
        here = pl.ds(p, g)
        lev["Va"][here] = (lev["IV"][here] * R[here]) * (1.0 / THETA)

    planes_loop(lo, hi, group, start)
    names = ("Va", "Vb")
    for j in range(4):
        a, b = TABLE[j] if j < 3 else (0.0, 0.0)
        lo, hi = base - halos[j], base + own + halos[j]
        sweep(lev, R, X, names[j % 2], names[1 - j % 2], lo, hi, a, b, group,
              first=(j == 0), want_dir=(j < 3), part=part)
        if after:
            after(j)


def postsmooth(lev, R, X, halos, base, own, group, part=None):
    names = ("Va", "Vb")
    for j in range(4):
        a, b = TABLE[j - 1] if j > 0 else (0.0, 1.0 / THETA)
        lo, hi = base - halos[j], base + own + halos[j]
        sweep(lev, R, X, names[j % 2], names[1 - j % 2], lo, hi, a, b, group, part=part)


def kernel(sizes, names, *refs):
    f_hbm, k_hbm, out_ref = refs[:3]
    S = dict(zip(names, refs[3:]))
    f_ref, k_ref = S["FI"], S["KI"]
    loads = [pltpu.make_async_copy(src, dst, S["ls"].at[i])
             for i, (src, dst) in enumerate(((f_hbm, f_ref), (k_hbm, k_ref)))]
    for c in loads:
        c.start()
    ss, rs = S["ss"], S["rs"]
    NGX, NGY, NGZ = sizes
    NYC = NGY // 2
    NX0, NY0, NZ0 = 16 * NGX, 16 * NGY, 128 * NGZ
    NX1, NY1, NZ1 = NX0 // 2, NY0 // 2, NZ0 // 2
    NX3 = 2 * NGX
    gx, gy, gz = lax.axis_index("gx"), lax.axis_index("gy"), lax.axis_index("gz")
    core, chip = gy % 2, gy // 2

    def at(dx=0, dy=0, dz=0):
        return ((gx + dx + NGX) % NGX, (gy + dy + NGY) % NGY, (gz + dz + NGZ) % NGZ)

    pair_peers = [(c, dz) for c in (0, 1) for dz in range(NGZ) if (c, dz) != (0, 0)]

    def pair_dev(c, dz):
        return (gx, chip * 2 + (core + c) % 2, (gz + dz) % NGZ)

    def chip_dev(dy):
        return (gx, ((chip + dy) % NYC) * 2 + core, gz)

    sides = [(dx, dy) for dx in (-1, 0, 1) for dy in (-1, 0, 1) if (dx, dy) != (0, 0)]

    barrier = pltpu.get_barrier_semaphore()
    greeted = [pair_dev(c, dz) for c, dz in pair_peers]
    greeted += [chip_dev(dy) for dy in range(1, NYC)]
    greeted += [at(dx=dx, dy=dy) for dx, dy in sides]
    for dev in greeted:
        pl.semaphore_signal(barrier, inc=1, device_id=dev, device_id_type=MESH)

    def pass_on(i):
        for d in (2 ** i, -(2 ** i)):
            pl.semaphore_signal(S["dis"].at[i], inc=1, device_id=at(dx=d), device_id_type=MESH)

    def heard(i):
        pl.semaphore_wait(S["dis"].at[i], 2)

    counter = [0]

    def remote(src, dst, dev):
        i = counter[0]
        counter[0] += 1
        return pltpu.make_async_remote_copy(
            src_ref=src, dst_ref=dst, send_sem=ss.at[i], recv_sem=rs.at[i],
            device_id=dev, device_id_type=MESH,
        )

    def begin(copies):
        for c in copies:
            c.start()
        return copies

    def finish(copies):
        for c in copies:
            c.wait()

    def z_copies(buf, from_left, from_right):
        return [remote(buf, from_left, at(dz=1)), remote(buf, from_right, at(dz=-1))]

    def xy_copies(buf, base, own, h, rows):
        fields = slice(None)
        xs = {1: (base + own - h, base - h, h), -1: (base, base + own, h), 0: (base, base, own)}
        ys = {1: (rows, 0, 8), -1: (8, 8 + rows, 8), 0: (8, 8, rows)}
        out = []
        for dx, dy in sides:
            (sx, tx, nx), (sy, ty, ny) = xs[dx], ys[dy]
            out.append(remote(
                buf.at[fields, pl.ds(sx, nx), pl.ds(sy, ny)],
                buf.at[fields, pl.ds(tx, nx), pl.ds(ty, ny)],
                at(dx=dx, dy=dy)))
        return out

    def x_copies(buf, n1, n2):
        out = []
        for d, n in ((1, n1), (2, n2)):
            if n:
                fld = slice(None) if d == 1 else slice(0, 1)
                out.append(remote(buf.at[fld, pl.ds(11 - n, n)],
                                  buf.at[fld, pl.ds(7 - 4 * (d - 1) - n, n)], at(dx=d)))
                out.append(remote(buf.at[fld, pl.ds(7, n)],
                                  buf.at[fld, pl.ds(11 + 4 * (d - 1), n)], at(dx=-d)))
        return out

    def pair_copies(buf, slots):
        return [remote(buf, slots.at[i], pair_dev(c, dz)) for i, (c, dz) in enumerate(pair_peers)]

    def chip_copies(buf):
        mine = buf.at[0, pl.ds(7, 4), pl.ds(pl.multiple_of(chip * 8, 8), 8)]
        return [remote(mine, mine, chip_dev(dy)) for dy in range(1, NYC)]

    lane16 = iota((16, 128), 1)
    lane8 = iota((8, 128), 1)

    def sel(shape, cond, value):
        return jnp.where(cond(iota(shape, 0), iota(shape, 1)), value, 0.0).astype(F32)

    def coarse_0(r):
        c = sel((64, 256), lambda r, c: ((c >> 5) == (r >> 3)) & (((c & 15) >> 1) == (r & 7)), 0.25)
        z = sel((128, 128), lambda l, c: (l >> 1) == (c & 63), 0.5)
        return mm(mm(c, r), z)

    def coarse_1(r):
        c = sel((32, 64), lambda r, c: ((c >> 4) == (r >> 3)) & (((c & 7) >> 1) == (r & 7) - 4 * core), 0.25)
        z = sel((128, 128), lambda l, c: (l < 64) & (c == 32 * gz + (l >> 1)), 0.5)
        return mm(mm(c, r), z)

    def coarse_2(r):
        c = sel((32, 128), lambda r, c: ((c >> 6) == (r >> 4)) & (((c & 31) >> 1) == (r & 15)), 0.25)
        z = sel((128, 128), lambda l, c: (l >> 1) == (c & 63), 0.5)
        t = mm(mm(c, r), z)
        return jnp.where(lane16 < 64, t[0:16], t[16:32])

    def coarse_3(r):
        n = r.shape[0]
        c = sel((n // 4, n), lambda r, c: ((c >> 5) == (r >> 3)) & (((c & 15) >> 1) == (r & 7)), 0.25)
        z = sel((128, 128), lambda l, c: (l < 64) & ((l >> 1) == c), 0.5)
        return mm(mm(c, r), z)

    def fine_3(e):
        n = e.shape[0]
        u = sel((4 * n, n), lambda r, c: ((r >> 5) == (c >> 3)) & (((r & 15) >> 1) == (c & 7)), 1.0)
        z = sel((128, 128), lambda c, l: (l < 64) & ((l >> 1) == c), 1.0)
        return mm(u, mm(e, z))

    def pack0(field):
        out = []
        for g in range(2):
            acc = None
            for j in range(8):
                t = pltpu.roll(field(8 * g + j), 16 * j + 8, 1)
                acc = t if acc is None else jnp.where((lane16 >> 4) == j, t, acc)
            out.append(acc)
        return out

    def centre0(buf, fld, h, field, from_left, from_right):
        base = h + 1
        for g, m in ((0, base), (1, base + 17)):
            buf[fld, m, 8:24] = jnp.where((lane16 & 15) >= 8, from_right[fld, g], from_left[fld, g])

    def body0(buf, fld, h, ref):
        base = h + 1
        buf[fld, base + 1:base + 17, 8:24] = ref[...]

    def unpack0(buf, fld, h, lo, hi, put):
        for x in range(lo, hi):
            if x < 0:
                main, m, j = x + h, h, x + 8
            elif x < 16:
                main, m, j = h + 2 + x, (h + 1 if x < 8 else h + 18), x % 8
            else:
                main, m, j = h + 20 + x - 16, h + 19, x - 16
            put(x, buf[fld, main], pltpu.roll(buf[fld, m], (120 - 16 * j) % 128, 1))

    def double1(v):
        n = v.shape[0]
        return jnp.where(iota((n, 128), 1) < 64, v, pltpu.roll(v, 64, 1))

    def centre1(buf, fld, own, left, right, i):
        lane = iota((64, 128), 1)
        t = jnp.where(lane < 64, flat(own[i]), jnp.where(lane < 96, flat(right[i]), flat(left[i])))
        buf[fld, 6:14, 8:16] = t.reshape(8, 8, 128)

    def inside(n_rows, n_lanes, row0, lane_of, ny, nz):
        y = iota((n_rows, n_lanes), 0) + row0
        z = lane_of(iota((n_rows, n_lanes), 1))
        return jnp.where((y >= 0) & (y < ny) & (z >= 0) & (z < nz), 1.0, 0.0).astype(F32)

    def xin(x, n):
        return jnp.where((x >= 0) & (x < n), 1.0, 0.0).astype(F32)

    L0 = {n: S[n + "0"] for n in ("K", "WX", "WY", "WZ", "DG", "IV", "Va", "Vb")}
    L1 = {n: S[n + "1"] for n in ("WX", "WY", "WZ", "DG", "IV", "Va", "Vb")}
    L1["K"] = S["K1"].at[0]
    L2 = {n: S[n + "2"] for n in ("WX", "WY", "WZ", "DG", "IV", "Va", "Vb")}
    L2["K"] = S["K2"].at[0]
    L3 = {n: S[n + "3"] for n in ("K", "WX", "WY", "WZ", "DG", "IV", "Va", "Vb")}
    R0, X0 = S["R0"], S["X0"]
    F1, X1 = S["F1"].at[0], S["X1"]
    F2, X2 = S["F2"].at[0], S["X2"]
    F3, X3 = S["F3"], S["X3"]

    for c in loads:
        c.wait()
    E0, E0r = S["E0"], S["E0r"]
    for fld, ref in ((0, f_ref), (1, k_ref)):
        for g, t in enumerate(pack0(lambda x: ref[x])):
            S["P0"][fld, g] = t
        body0(E0, fld, H0, ref)

    pl.semaphore_wait(barrier, len(greeted))
    z0 = begin(z_copies(S["P0"], S["P0L"], S["P0R"]))
    pass_on(0)
    finish(z0)
    for fld in (0, 1):
        centre0(E0, fld, H0, None, S["P0L"], S["P0R"])
    xy0 = begin(xy_copies(E0, H0 + 1, 18, H0 + 1, 16))

    k1 = coarse_0(k_ref[...].reshape(256, 128))
    S["T1k"][0] = k1.reshape(8, 8, 128)
    S["B2k"][...] = coarse_1(k1).reshape(4, 8, 128)
    z1k = begin(z_copies(S["T1k"], S["T1kL"], S["T1kR"]))
    p2k = begin(pair_copies(S["B2k"], S["B2kS"]))
    heard(0)
    pass_on(1)

    def pair_sum(own, slots):
        total = own[...]
        for i in range(len(pair_peers)):
            total = total + slots[i]
        return total

    my_rows = pl.ds(pl.multiple_of(chip * 8, 8), 8)
    my_half = pl.ds(pl.multiple_of(core * 8, 8), 8)

    def gather_start(v, buf):
        S["C3"][...] = v
        buf[gx, my_half] = S["C3"][my_half]
        mine = buf.at[gx, my_half]
        return begin([remote(mine, mine, at(dx=d)) for d in range(1, NGX)])

    def swap_start(buf):
        mine = buf.at[:, my_half]
        return begin([remote(mine, mine, pair_dev(1, 0))])

    finish(z1k)
    centre1(S["K1"], 0, S["T1k"], S["T1kL"], S["T1kR"], 0)
    finish(p2k)
    S["K2"][0, 7:11, my_rows] = pair_sum(S["B2k"], S["B2kS"])

    finish(xy0)
    xy1k = begin(xy_copies(S["K1"], 6, 8, H1K, 8))
    c2k = begin(chip_copies(S["K2"]))
    heard(1)
    pass_on(2)

    def lane0(l):
        return 128 * gz + jnp.where(l < 192, l, l - 256)

    in0 = inside(32, 256, 16 * gy - 8, lane0, NY0, NZ0)

    def put_k(x, main, halo):
        w = xin(16 * gx + x, NX0)
        L0["K"][x + 5, :, 0:128] = main * (in0[:, 0:128] * w)
        L0["K"][x + 5, :, 128:256] = halo * (in0[:, 128:256] * w)

    def put_r(x, main, halo):
        R0[x + 5, :, 0:128] = main
        R0[x + 5, :, 128:256] = halo

    unpack0(E0, 1, H0, -5, 21, put_k)
    unpack0(E0, 0, H0, -4, 20, put_r)
    weights(L0, 1, 25, 0.5, False, 1)

    coef = {}

    def after_sweep(j):
        if j == 1:
            finish(c2k)
            coef["x"] = begin(x_copies(S["K2"], 4, 3))
            heard(2)
            coef["g"] = gather_start(coarse_2(S["K2"][0, 7:11].reshape(128, 128)), S["G3k"])

    presmooth(L0, R0, X0, (3, 2, 1, 0), 5, 16, G0, part=OWN0, after=after_sweep)

    own0 = R0[5:21, 8:24, 0:128]
    S["T1f"][0] = coarse_0(own0.reshape(256, 128)).reshape(8, 8, 128)
    z1f = begin(z_copies(S["T1f"], S["T1fL"], S["T1fR"]))
    for g, t in enumerate(pack0(lambda x: R0[5 + x, 8:24, 0:128])):
        S["P0r"][0, g] = t
    E0r[0, H0R + 2:H0R + 18, 8:24] = own0
    finish(xy1k)

    def lane1(l):
        return 64 * gz + jnp.where(l < 96, l, l - 128)

    in1 = inside(24, 128, 8 * gy - 8, lane1, NY1, NZ1)
    for p in range(20):
        L1["K"][p] = L1["K"][p] * (in1 * xin(8 * gx + p - 6, NX1))
    weights(L1, 1, 19, 0.5 * 0.25, False, 2)

    finish(z1f)
    centre1(S["F1"], 0, S["T1f"], S["T1fL"], S["T1fR"], 0)
    xy1f = begin(xy_copies(S["F1"], 6, 8, H1F, 8))
    z0r = begin(z_copies(S["P0r"], S["P0rL"], S["P0rR"]))
    finish(xy1f)
    finish(z0r)
    centre0(E0r, 0, H0R, None, S["P0rL"], S["P0rR"])
    xy0r = begin(xy_copies(E0r, H0R + 1, 18, H0R + 1, 16))
    presmooth(L1, F1, X1, (3, 2, 1, 0), 6, 8, G1)

    r1 = F1[6:14, 8:16]
    S["B2f"][...] = coarse_1(r1.reshape(64, 128)).reshape(4, 8, 128)
    p2f = begin(pair_copies(S["B2f"], S["B2fS"]))
    S["T1r"][0] = double1(r1.reshape(64, 128)).reshape(8, 8, 128)
    S["T1r"][1] = double1(X1[6:14, 8:16].reshape(64, 128)).reshape(8, 8, 128)
    z1r = begin(z_copies(S["T1r"], S["T1rL"], S["T1rR"]))

    finish(coef["x"])
    for p in range(18):
        if p < 7 or p > 10:
            L2["K"][p] = L2["K"][p] * xin(4 * gx + p - 7, NX1 // 2)
    weights(L2, 1, 17, 0.5 * 0.25 ** 2, True, 2)

    finish(p2f)
    S["F2"][0, 7:11, my_rows] = pair_sum(S["B2f"], S["B2fS"])
    c2f = begin(chip_copies(S["F2"]))
    finish(z1r)
    for i in (0, 1):
        centre1(S["RX1"], i, S["T1r"], S["T1rL"], S["T1rR"], i)
    finish(c2f)
    xx2f = begin(x_copies(S["F2"], 4, 0))
    xy1r = begin(xy_copies(S["RX1"], 6, 8, H1R, 8))

    finish(coef["g"])
    finish(swap_start(S["G3k"]))

    def unpack3(slots, dst):
        for s in range(NGX):
            t = slots[s]
            dst[5 + 2 * s] = jnp.where(lane16 < 64, t, 0.0)
            dst[6 + 2 * s] = jnp.where(lane16 < 64, pltpu.roll(t, 64, 1), 0.0)

    unpack3(S["G3k"], L3["K"])
    zero3 = jnp.zeros((5, 16, 128), F32)
    for ref in (L3["K"], L3["Va"], L3["Vb"], X3):
        ref[0:5] = zero3
        ref[5 + NX3:10 + NX3] = zero3
    weights(L3, 5, 5 + NX3, 0.5 * 0.25 ** 3, True, 4)

    finish(xx2f)
    presmooth(L2, F2, X2, (3, 2, 1, 0), 7, 4, G2)

    g3f = gather_start(coarse_2(F2[7:11].reshape(128, 128)), S["G3f"])
    S["RX2"][0, 7:11] = F2[7:11]
    S["RX2"][1, 7:11] = X2[7:11]
    xx2r = begin(x_copies(S["RX2"], 4, 2))

    n4 = 8 * (NX3 // 2)
    h4 = 0.5 * 0.25 ** 4
    k4 = coarse_3(L3["K"][5:5 + NX3].reshape(16 * NX3, 128))
    row4 = iota((n4, 128), 0)
    plane_end = (row4 & 7) == 7
    last_plane = row4 >= n4 - 8
    first_plane = row4 < 8
    k4xu = jnp.where(last_plane, 0.0, up(k4, 0, 8))
    k4xd = jnp.where(first_plane, 0.0, down(k4, 0, 8))
    k4yu = jnp.where(plane_end, 0.0, up(k4, 0))
    k4yd = jnp.where((row4 & 7) == 0, 0.0, down(k4, 0))
    k4zu, k4zd = up(k4, 1), down(k4, 1)
    wx4 = jnp.where(last_plane, 0.0, h4 * (k4 + k4xu))
    wy4 = jnp.where(plane_end, 0.0, h4 * (k4 + k4yu))
    wz4 = h4 * (k4 + k4zu)
    dg4 = h4 * (6.0 * k4 + ((k4xu + k4xd) + (k4yu + k4yd) + (k4zu + k4zd)))

    finish(g3f)
    finish(swap_start(S["G3f"]))
    unpack3(S["G3f"], F3)
    presmooth(L3, F3, X3, (0, 0, 0, 0), 5, NX3, G3, whole=True)

    f4 = coarse_3(F3[5:5 + NX3].reshape(16 * NX3, 128))
    f4 = jnp.where(k4 > 0.0, f4, 0.0)
    x4 = jnp.zeros_like(f4)
    r4 = p4 = f4
    rr = jnp.sum(r4 * r4, keepdims=True)
    for _ in range(CG_ITERS):
        q4 = dg4 * p4 - (
            (wx4 * up(p4, 0, 8) + down(wx4 * p4, 0, 8))
            + (wy4 * up(p4, 0) + down(wy4 * p4, 0))
            + (wz4 * up(p4, 1) + down(wz4 * p4, 1)))
        q4 = jnp.where(k4 > 0.0, q4, 0.0)
        alpha = rr / jnp.sum(p4 * q4, keepdims=True)
        x4 = x4 + alpha * p4
        r4 = r4 - alpha * q4
        rn = jnp.sum(r4 * r4, keepdims=True)
        p4 = r4 + (rn / rr) * p4
        rr = rn

    L3["Va"][5:5 + NX3] = fine_3(x4).reshape(NX3, 16, 128)
    postsmooth(L3, F3, X3, (0, 0, 0, 0), 5, NX3, G3)
    X3[5:5 + NX3] = X3[5:5 + NX3] + L3["Va"][5:5 + NX3]

    finish(xx2r)
    z3 = sel((128, 128), lambda c, l: (l >> 1) == c, 1.0)
    y3 = sel((32, 16), lambda r, c: (r >> 1) == c, 1.0)
    t = mm(X3[pl.ds(2 * gx + 1, 10)].reshape(160, 128), z3)
    for q in range(10):
        e = mm(y3, t[16 * q:16 * q + 16])
        for p in (2 * q - 1, 2 * q):
            if 0 <= p < 18:
                L2["Va"][p] = e
    R2b, X2b = S["RX2"].at[0], S["RX2"].at[1]
    postsmooth(L2, R2b, X2b, (6, 5, 4, 3), 7, 4, G2)
    X2b[4:14] = X2b[4:14] + L2["Va"][4:14]

    finish(xy1r)
    z2 = sel((128, 128), lambda c, l: ((lane1(l) >> 1) == c) & (lane1(l) >= 0) & (lane1(l) < NZ1), 1.0)

    def yrow(r):
        return 8 * gy + r - 8

    y2 = sel((24, 32), lambda r, c: ((yrow(r) >> 1) == c) & (yrow(r) >= 0) & (yrow(r) < NY1), 1.0)
    t = mm(X2b[4:14].reshape(320, 128), z2)
    for q in range(10):
        e = mm(y2, t[32 * q:32 * q + 32])
        e = e * xin(4 * gx + q - 3, NX1 // 2)
        L1["Va"][2 * q] = e
        L1["Va"][2 * q + 1] = e
    R1b, X1b = S["RX1"].at[0], S["RX1"].at[1]
    postsmooth(L1, R1b, X1b, (5, 4, 3, 2), 6, 8, G1)
    X1b[4:16] = X1b[4:16] + L1["Va"][4:16]

    finish(xy0r)
    unpack0(E0r, 0, H0R, -3, 19, put_r)

    def zfine(c, l):
        z = jnp.where(l < 192, l, l - 256)
        g = 128 * gz + z
        return (((z >> 1) & 127) == c) & (g >= 0) & (g < NZ0)

    def yfine(r, c):
        g = 16 * gy + r - 8
        return (((r - 8) >> 1) + 8 == c) & (g >= 0) & (g < NY0)

    z1 = sel((128, 256), zfine, 1.0)
    y1 = sel((32, 24), yfine, 1.0)
    t = mm(X1b[4:16].reshape(288, 128), z1)
    for q in range(12):
        e = mm(y1, t[24 * q:24 * q + 24])
        e = e * xin(8 * gx + q - 2, NX1)
        L0["Va"][1 + 2 * q] = e
        L0["Va"][2 + 2 * q] = e
    postsmooth(L0, R0, X0, (3, 2, 1, 0), 5, 16, G0, part=OWN0)
    out_ref[...] = X0[5:21] + L0["Va"][5:21, 8:24, 0:128]


def scratch(sizes):
    ngx, ngy, ngz = sizes
    n_pair = 2 * ngz - 1
    shapes = {
        "FI": (16, 16, 128), "KI": (16, 16, 128), "C3": (16, 128),
        "P0": (2, 2, 16, 128), "P0L": (2, 2, 16, 128), "P0R": (2, 2, 16, 128),
        "E0": (2, 18 + 2 * (H0 + 1), 32, 128),
        "P0r": (1, 2, 16, 128), "P0rL": (1, 2, 16, 128), "P0rR": (1, 2, 16, 128),
        "E0r": (1, 18 + 2 * (H0R + 1), 32, 128),
        "R0": (26, 32, 256), "X0": (26, 16, 128), "K0": (26, 32, 256),
        "T1r": (2, 8, 8, 128), "T1rL": (2, 8, 8, 128), "T1rR": (2, 8, 8, 128),
        "K1": (1, 20, 24, 128), "F1": (1, 20, 24, 128), "RX1": (2, 20, 24, 128), "X1": (20, 24, 128),
        "K2": (1, 18, 32, 128), "F2": (1, 18, 32, 128), "RX2": (2, 18, 32, 128), "X2": (18, 32, 128),
        "B2k": (4, 8, 128), "B2kS": (n_pair, 4, 8, 128),
        "B2f": (4, 8, 128), "B2fS": (n_pair, 4, 8, 128),
        "G3k": (ngx, 16, 128), "G3f": (ngx, 16, 128),
        "K3": (2 * ngx + 10, 16, 128), "F3": (2 * ngx + 10, 16, 128), "X3": (2 * ngx + 10, 16, 128),
    }
    for n in ("T1k", "T1f"):
        for side in ("", "L", "R"):
            shapes[n + side] = (1, 8, 8, 128)
    for n in ("WX", "WY", "WZ", "DG", "IV", "Va", "Vb"):
        shapes[n + "0"] = (26, 32, 256)
        shapes[n + "1"] = (20, 24, 128)
        shapes[n + "2"] = (18, 32, 128)
        shapes[n + "3"] = (2 * ngx + 10, 16, 128)
    names = list(shapes) + ["ss", "rs", "ls", "dis"]
    n_sem = 4 * 10 + 10 + 2 * (n_pair + max(ngy // 2 - 1, 0)) + 4 + 2 + 4 + 2 * ngx
    kinds = [pltpu.VMEM(shapes[n], F32) for n in shapes]
    kinds += [pltpu.SemaphoreType.DMA((n_sem,)), pltpu.SemaphoreType.DMA((n_sem,))]
    kinds += [pltpu.SemaphoreType.DMA((2,)), pltpu.SemaphoreType.REGULAR((3,))]
    return names, kinds


def solution(mesh):
    sizes = (mesh.shape["gx"], mesh.shape["gy"], mesh.shape["gz"])
    names, kinds = scratch(sizes)
    spec = P("gx", "gy", "gz")

    def local(right_side, conductivity):
        return pl.pallas_call(
            functools.partial(kernel, sizes, names),
            out_shape=jax.ShapeDtypeStruct(right_side.shape, F32),
            in_specs=[pl.BlockSpec(memory_space=pl.ANY)] * 2,
            out_specs=pl.BlockSpec(memory_space=pltpu.VMEM),
            scratch_shapes=kinds,
            compiler_params=pltpu.CompilerParams(
                collective_id=0, has_side_effects=True, vmem_limit_bytes=48 * 1024 * 1024
            ),
        )(right_side, conductivity)

    return jax.shard_map(local, mesh=mesh, in_specs=(spec, spec), out_specs=spec, check_vma=False)
```

```python
import functools

import jax
import jax.numpy as jnp
from jax import lax
from jax.experimental import pallas as pl
from jax.experimental.pallas import tpu as pltpu
from jax.sharding import PartitionSpec as P

F32 = jnp.float32
MESH = pl.DeviceIdType.MESH
CG_ITERS = 8
THETA = 1.125
DELTA = 0.875

H0, H0R = 5, 3
H1K, H1F, H1R = 6, 4, 5

G0, G1, G2, G3 = 8, 20, 20, 32
OWN0 = (slice(8, 24), slice(0, 128))


def cheb_table():
    sigma = THETA / DELTA
    rho_now = 1.0 / sigma
    table = []
    for _ in range(3):
        rho_next = 1.0 / (2.0 * sigma - rho_now)
        table.append((rho_next * rho_now, 2.0 * rho_next / DELTA))
        rho_now = rho_next
    return table


TABLE = cheb_table()


def parts_of(v):
    high = v.astype(jnp.bfloat16)
    rest = v - high.astype(F32)
    mid = rest.astype(jnp.bfloat16)
    return high, mid, (rest - mid.astype(F32)).astype(jnp.bfloat16)


def dot(a, b):
    return jnp.dot(a, b, preferred_element_type=F32)


def mml(m, v):
    m = m.astype(jnp.bfloat16)
    high, mid, low = parts_of(v)
    return dot(m, high) + (dot(m, mid) + dot(m, low))


def mmr(v, m):
    m = m.astype(jnp.bfloat16)
    high, mid, low = parts_of(v)
    return dot(high, m) + (dot(mid, m) + dot(low, m))


def iota(shape, dim):
    return lax.broadcasted_iota(jnp.int32, shape, dim)


def flat(v):
    return v.reshape(v.shape[0] * v.shape[1], v.shape[2])


def up(v, dim, step=1):
    return pltpu.roll(v, v.shape[dim] - step, dim)


def down(v, dim, step=1):
    return pltpu.roll(v, step, dim)


def planes_loop(lo, hi, group, fn):
    count = (hi - lo) // group
    if count > 1:
        def body(i, carry):
            fn(lo + i * group, group)
            return carry

        lax.fori_loop(0, count, body, 0)
    elif count == 1:
        fn(lo, group)
    rest = hi - lo - count * group
    if rest:
        fn(lo + count * group, rest)


def weights(lev, lo, hi, h, whole, group):
    K = lev["K"]
    rows, lanes = K.shape[1], K.shape[2]

    def one(p, g):
        n = g * rows
        k = flat(K[pl.ds(p, g)])
        kxu = flat(K[pl.ds(p + 1, g)])
        kxd = flat(K[pl.ds(p - 1, g)])
        kyu, kyd, kzu, kzd = up(k, 0), down(k, 0), up(k, 1), down(k, 1)
        if whole:
            row = iota((n, lanes), 0) & (rows - 1)
            lane = iota((n, lanes), 1)
            kyu = jnp.where(row == rows - 1, 0.0, kyu)
            kyd = jnp.where(row == 0, 0.0, kyd)
            kzu = jnp.where(lane == lanes - 1, 0.0, kzu)
            kzd = jnp.where(lane == 0, 0.0, kzd)
        wy, wz = h * (k + kyu), h * (k + kzu)
        diag = h * (6.0 * k + ((kxu + kxd) + (kyu + kyd) + (kzu + kzd)))
        if whole:
            wy = jnp.where(row == rows - 1, 0.0, wy)
            wz = jnp.where(lane == lanes - 1, 0.0, wz)
        shape = (g, rows, lanes)
        lev["WX"][pl.ds(p, g)] = (h * (k + kxu)).reshape(shape)
        lev["WY"][pl.ds(p, g)] = wy.reshape(shape)
        lev["WZ"][pl.ds(p, g)] = wz.reshape(shape)
        lev["DG"][pl.ds(p, g)] = diag.reshape(shape)
        lev["IV"][pl.ds(p, g)] = jnp.where(k > 0.0, 1.0 / diag, 0.0).reshape(shape)

    lev["WX"][lo - 1] = h * (K[lo - 1] + K[lo])
    planes_loop(lo, hi, group, one)


def sweep(lev, R, X, src, dst, lo, hi, a, b, group, first=False, want_dir=True, part=None):
    Vi, Vo = lev[src], lev[dst]

    def one(p, g):
        v = [Vi[p - 1 + i] for i in range(g + 2)]
        wx = [lev["WX"][p - 1 + i] for i in range(g + 1)]
        for i in range(g):
            c = v[i + 1]
            wy, wz = lev["WY"][p + i], lev["WZ"][p + i]
            total = wx[i + 1] * v[i + 2] + wx[i] * v[i]
            total = total + (wy * up(c, 0) + down(wy * c, 0))
            total = total + (wz * up(c, 1) + down(wz * c, 1))
            r = R[p + i] - (lev["DG"][p + i] * c - total)
            R[p + i] = r
            own = c if part is None else c[part[0], part[1]]
            X[p + i] = own if first else X[p + i] + own
            if want_dir:
                d = b * (lev["IV"][p + i] * r)
                Vo[p + i] = d + a * c if a else d

    planes_loop(lo, hi, group, one)


def presmooth(lev, R, X, halos, base, own, group, whole=False, part=None, after=None):
    h = 0 if whole else halos[0] + 1
    lo, hi = base - h, base + own + h

    def start(p, g):
        here = pl.ds(p, g)
        lev["Va"][here] = (lev["IV"][here] * R[here]) * (1.0 / THETA)

    planes_loop(lo, hi, group, start)
    names = ("Va", "Vb")
    for j in range(4):
        a, b = TABLE[j] if j < 3 else (0.0, 0.0)
        lo, hi = base - halos[j], base + own + halos[j]
        sweep(lev, R, X, names[j % 2], names[1 - j % 2], lo, hi, a, b, group,
              first=(j == 0), want_dir=(j < 3), part=part)
        if after:
            after(j)


def postsmooth(lev, R, X, halos, base, own, group, part=None):
    names = ("Va", "Vb")
    for j in range(4):
        a, b = TABLE[j - 1] if j > 0 else (0.0, 1.0 / THETA)
        lo, hi = base - halos[j], base + own + halos[j]
        sweep(lev, R, X, names[j % 2], names[1 - j % 2], lo, hi, a, b, group, part=part)


def kernel(sizes, names, *refs):
    f_hbm, k_hbm, out_ref = refs[:3]
    S = dict(zip(names, refs[3:]))
    E0 = S["E0"]
    loads = [pltpu.make_async_copy(src, E0.at[i, pl.ds(H0, 16), pl.ds(8, 16)], S["ls"].at[i])
             for i, src in enumerate((f_hbm, k_hbm))]
    for c in loads:
        c.start()
    ss, rs = S["ss"], S["rs"]
    NGX, NGY, NGZ = sizes
    NYC = NGY // 2
    NX0, NY0, NZ0 = 16 * NGX, 16 * NGY, 128 * NGZ
    NX1, NY1, NZ1 = NX0 // 2, NY0 // 2, NZ0 // 2
    NX3 = 2 * NGX
    gx, gy, gz = lax.axis_index("gx"), lax.axis_index("gy"), lax.axis_index("gz")
    core, chip = gy % 2, gy // 2

    def at(dx=0, dy=0, dz=0):
        return ((gx + dx + NGX) % NGX, (gy + dy + NGY) % NGY, (gz + dz + NGZ) % NGZ)

    pair_peers = [(c, dz) for c in (0, 1) for dz in range(NGZ) if (c, dz) != (0, 0)]

    def pair_dev(c, dz):
        return (gx, chip * 2 + (core + c) % 2, (gz + dz) % NGZ)

    def chip_dev(dy, dx=0):
        return ((gx + dx + NGX) % NGX, ((chip + dy) % NYC) * 2 + core, gz)

    sides = [(dx, dy) for dx in (-1, 0, 1) for dy in (-1, 0, 1) if (dx, dy) != (0, 0)]

    barrier = pltpu.get_barrier_semaphore()
    greeted = [pair_dev(c, dz) for c, dz in pair_peers]
    greeted += [chip_dev(dy, dx) for dx in (-1, 0, 1) for dy in range(1, NYC)]
    greeted += [at(dx=dx, dy=dy) for dx, dy in sides]
    for dev in greeted:
        pl.semaphore_signal(barrier, inc=1, device_id=dev, device_id_type=MESH)

    def pass_on(i):
        for d in (2 ** i, -(2 ** i)):
            pl.semaphore_signal(S["dis"].at[i], inc=1, device_id=at(dx=d), device_id_type=MESH)

    def heard(i):
        pl.semaphore_wait(S["dis"].at[i], 2)

    counter = [0]

    def remote(src, dst, dev):
        i = counter[0]
        counter[0] += 1
        return pltpu.make_async_remote_copy(
            src_ref=src, dst_ref=dst, send_sem=ss.at[i], recv_sem=rs.at[i],
            device_id=dev, device_id_type=MESH,
        )

    def begin(copies):
        for c in copies:
            c.start()
        return copies

    def finish(copies):
        for c in copies:
            c.wait()

    def z_copies(buf, from_left, from_right):
        return [remote(buf, from_left, at(dz=1)), remote(buf, from_right, at(dz=-1))]

    def xy_copies(buf, base, own, h, rows):
        fields = slice(None)
        xs = {1: (base + own - h, base - h, h), -1: (base, base + own, h), 0: (base, base, own)}
        ys = {1: (rows, 0, 8), -1: (8, 8 + rows, 8), 0: (8, 8, rows)}
        out = []
        for dx, dy in sides:
            (sx, tx, nx), (sy, ty, ny) = xs[dx], ys[dy]
            out.append(remote(
                buf.at[fields, pl.ds(sx, nx), pl.ds(sy, ny)],
                buf.at[fields, pl.ds(tx, nx), pl.ds(ty, ny)],
                at(dx=dx, dy=dy)))
        return out

    def x_copies(buf, n1, n2):
        out = []
        for d, n in ((1, n1), (2, n2)):
            if n:
                fld = slice(None) if d == 1 else slice(0, 1)
                out.append(remote(buf.at[fld, pl.ds(11 - n, n)],
                                  buf.at[fld, pl.ds(7 - 4 * (d - 1) - n, n)], at(dx=d)))
                out.append(remote(buf.at[fld, pl.ds(7, n)],
                                  buf.at[fld, pl.ds(11 + 4 * (d - 1), n)], at(dx=-d)))
        return out

    def pair_copies(buf, slots):
        return [remote(buf, slots.at[i], pair_dev(c, dz)) for i, (c, dz) in enumerate(pair_peers)]

    column = [(dx, dy) for dx in (-1, 0, 1) for dy in range(NYC) if (dx, dy) != (0, 0)]

    def column_copies(buf):
        rows = pl.ds(pl.multiple_of(chip * 8, 8), 8)
        mine = buf.at[0, pl.ds(7, 4), rows]
        return [remote(mine, buf.at[0, pl.ds(7 - 4 * dx, 4), rows], chip_dev(dy, dx)) for dx, dy in column]

    lane16 = iota((16, 128), 1)
    lane8 = iota((8, 128), 1)

    def sel(shape, cond, value):
        return jnp.where(cond(iota(shape, 0), iota(shape, 1)), value, 0.0).astype(F32)

    def coarse_0(r):
        c = sel((64, 256), lambda r, c: ((c >> 5) == (r >> 3)) & (((c & 15) >> 1) == (r & 7)), 0.25)
        z = sel((128, 128), lambda l, c: (l >> 1) == (c & 63), 0.5)
        return mmr(mml(c, r), z)

    def coarse_1(r):
        c = sel((32, 64), lambda r, c: ((c >> 4) == (r >> 3)) & (((c & 7) >> 1) == (r & 7) - 4 * core), 0.25)
        z = sel((128, 128), lambda l, c: (l < 64) & (c == (l >> 1)), 0.5)
        t = mmr(mml(c, r), z)
        return (t[0:8] + pltpu.roll(t[8:16], 32, 1)) + (pltpu.roll(t[16:24], 64, 1) + pltpu.roll(t[24:32], 96, 1))

    def coarse_2(r):
        c = sel((32, 128), lambda r, c: ((c >> 6) == (r >> 4)) & (((c & 31) >> 1) == (r & 15)), 0.25)
        z = sel((128, 128), lambda l, c: (l >> 1) == (c & 63), 0.5)
        t = mmr(mml(c, r), z)
        return jnp.where(lane16 < 64, t[0:16], t[16:32])

    def coarse_3(r):
        n = r.shape[0]
        c = sel((n // 4, n), lambda r, c: ((c >> 5) == (r >> 3)) & (((c & 15) >> 1) == (r & 7)), 0.25)
        z = sel((128, 128), lambda l, c: (l < 64) & ((l >> 1) == c), 0.5)
        return mmr(mml(c, r), z)

    def fine_3(e):
        n = e.shape[0]
        u = sel((4 * n, n), lambda r, c: ((r >> 5) == (c >> 3)) & (((r & 15) >> 1) == (c & 7)), 1.0)
        z = sel((128, 128), lambda c, l: (l < 64) & ((l >> 1) == c), 1.0)
        return mml(u, mmr(e, z))

    def pack0(field):
        out = []
        for g in range(2):
            acc = None
            for j in range(8):
                t = pltpu.roll(field(8 * g + j), 16 * j + 8, 1)
                acc = t if acc is None else jnp.where((lane16 >> 4) == j, t, acc)
            out.append(acc)
        return out

    def merge0(from_left, from_right):
        return jnp.where((lane16 & 15) >= 8, from_right, from_left)

    def centre0(buf, fld, h, from_left, from_right):
        for g, m in ((0, h + 1), (1, h + 18)):
            buf[fld, m, 8:24] = merge0(from_left[fld, g], from_right[fld, g])

    def open0(fld, lo, hi, put):
        for x in range(lo, hi):
            g, j = (x + 8) // 8, x % 8
            put(x, E0[fld, H0 + x], pltpu.roll(M0[fld, g], (120 - 16 * j) % 128, 1))

    def unpack0(buf, fld, h, lo, hi, put):
        for x in range(lo, hi):
            if x < 0:
                main, m, j = x + h, h, x + 8
            elif x < 16:
                main, m, j = h + 2 + x, (h + 1 if x < 8 else h + 18), x % 8
            else:
                main, m, j = h + 20 + x - 16, h + 19, x - 16
            put(x, buf[fld, main], pltpu.roll(buf[fld, m], (120 - 16 * j) % 128, 1))

    def pack1(v):
        acc = None
        for j in range(8):
            t = v[8 * j:8 * j + 8]
            low = pltpu.roll(t, 8 * j, 1) if j else t
            high = pltpu.roll(t, 8 * j + 8, 1)
            acc = low if acc is None else jnp.where((lane8 >> 3) == j, low, acc)
            acc = jnp.where((lane8 >> 3) == 8 + j, high, acc)
        return acc

    def corner_copies(pack, from_left, from_right):
        out = []
        for dz, buf in ((1, from_left), (-1, from_right)):
            for dx in (-1, 0, 1):
                for dy in (-1, 0, 1):
                    out.append(remote(pack, buf.at[pl.ds(1 - dx, 1), pl.ds(8 - 8 * dy, 8)], at(dx, dy, dz)))
        return out

    def double1(v):
        n = v.shape[0]
        return jnp.where(iota((n, 128), 1) < 64, v, pltpu.roll(v, 64, 1))

    def centre1(buf, fld, own, left, right, i):
        lane = iota((64, 128), 1)
        t = jnp.where(lane < 64, flat(own[i]), jnp.where(lane < 96, flat(right[i]), flat(left[i])))
        buf[fld, 6:14, 8:16] = t.reshape(8, 8, 128)

    def inside(n_rows, n_lanes, row0, lane_of, ny, nz):
        y = iota((n_rows, n_lanes), 0) + row0
        z = lane_of(iota((n_rows, n_lanes), 1))
        return jnp.where((y >= 0) & (y < ny) & (z >= 0) & (z < nz), 1.0, 0.0).astype(F32)

    def xin(x, n):
        return jnp.where((x >= 0) & (x < n), 1.0, 0.0).astype(F32)

    L0 = {n: S[n + "0"] for n in ("K", "WX", "WY", "WZ", "DG", "IV", "Va", "Vb")}
    L1 = {n: S[n + "1"] for n in ("WX", "WY", "WZ", "DG", "IV", "Va", "Vb")}
    L1["K"] = S["K1"].at[0]
    L2 = {n: S[n + "2"] for n in ("WX", "WY", "WZ", "DG", "IV", "Va", "Vb")}
    L2["K"] = S["K2"].at[0]
    L3 = {n: S[n + "3"] for n in ("K", "WX", "WY", "WZ", "DG", "IV", "Va", "Vb")}
    R0, X0 = S["R0"], S["X0"]
    F1, X1 = S["F1"].at[0], S["X1"]
    F2, X2 = S["F2"].at[0], S["X2"]
    F3, X3 = S["F3"], S["X3"]

    for c in loads:
        c.wait()
    E0r, M0 = S["E0r"], S["M0"]
    pl.semaphore_wait(barrier, len(greeted))
    xy0 = begin(xy_copies(E0, H0, 16, H0, 16))
    for fld in (0, 1):
        for g, t in enumerate(pack0(lambda x: E0[fld, H0 + x, 8:24])):
            S["P0"][fld, g] = t
    z0 = begin(z_copies(S["P0"], S["P0L"], S["P0R"]))
    pass_on(0)
    finish(z0)
    for fld in (0, 1):
        for g in (0, 1):
            M0[fld, 1 + g, 8:24] = merge0(S["P0L"][fld, g], S["P0R"][fld, g])
    xy0 += begin(xy_copies(M0, 1, 2, 1, 16))

    k1 = coarse_0(E0[1, H0:H0 + 16, 8:24].reshape(256, 128))
    S["T1k"][0] = k1.reshape(8, 8, 128)
    S["B2k"][...] = coarse_1(k1)
    z1k = begin(z_copies(S["T1k"], S["T1kL"], S["T1kR"]))
    p2k = begin(pair_copies(S["B2k"], S["B2kS"]))
    heard(0)
    pass_on(1)

    def pair_rows(own, slots):
        blocks = [[] for _ in range(NGZ)]
        blocks[0].append(own[...])
        for i, (_, dz) in enumerate(pair_peers):
            blocks[dz].append(slots[i])
        rows = [jnp.zeros((8, 128), F32)] * 4
        for dz in range(NGZ):
            g = (gz - dz + NGZ) % NGZ
            t = pltpu.roll(sum(blocks[dz][1:], blocks[dz][0]), 32 * g, 1)
            here = (lane8 >> 5) == g
            for x in range(4):
                rows[x] = jnp.where(here, t if x == 0 else pltpu.roll(t, 128 - 32 * x, 1), rows[x])
        return rows

    def put_rows(buf, rows):
        for x in range(4):
            buf[0, 7 + x, my_rows] = rows[x]

    my_rows = pl.ds(pl.multiple_of(chip * 8, 8), 8)
    my_half = pl.ds(pl.multiple_of(core * 8, 8), 8)

    def gather_start(v, buf):
        S["C3"][...] = v
        buf[gx, my_half] = S["C3"][my_half]
        mine = buf.at[gx, my_half]
        return begin([remote(mine, mine, at(dx=d)) for d in range(1, NGX)])

    def swap_start(buf):
        mine = buf.at[:, my_half]
        return begin([remote(mine, mine, pair_dev(1, 0))])

    finish(z1k)
    centre1(S["K1"], 0, S["T1k"], S["T1kL"], S["T1kR"], 0)
    finish(p2k)
    put_rows(S["K2"], pair_rows(S["B2k"], S["B2kS"]))

    finish(xy0)
    xy1k = begin(xy_copies(S["K1"], 6, 8, H1K, 8))
    c2k = begin(column_copies(S["K2"]))
    heard(1)
    pass_on(2)

    def lane0(l):
        return 128 * gz + jnp.where(l < 192, l, l - 256)

    in0 = inside(32, 256, 16 * gy - 8, lane0, NY0, NZ0)

    def put_k(x, main, halo):
        w = xin(16 * gx + x, NX0)
        L0["K"][x + 5, :, 0:128] = main * (in0[:, 0:128] * w)
        L0["K"][x + 5, :, 128:256] = halo * (in0[:, 128:256] * w)

    def put_r(x, main, halo):
        R0[x + 5, :, 0:128] = main
        R0[x + 5, :, 128:256] = halo

    open0(1, -5, 21, put_k)
    open0(0, -4, 20, put_r)
    weights(L0, 1, 25, 0.5, False, 1)

    presmooth(L0, R0, X0, (3, 2, 1, 0), 5, 16, G0, part=OWN0)

    own0 = R0[5:21, 8:24, 0:128]
    f1 = coarse_0(own0.reshape(256, 128))
    S["F1"][0, 6:14, 8:16] = f1.reshape(8, 8, 128)
    S["P1"][0] = pack1(f1)
    xy1f = begin(xy_copies(S["F1"], 6, 8, H1F, 8) + corner_copies(S["P1"], S["Z1L"], S["Z1R"]))
    for g, t in enumerate(pack0(lambda x: R0[5 + x, 8:24, 0:128])):
        S["P0r"][0, g] = t
    E0r[0, H0R + 2:H0R + 18, 8:24] = own0
    finish(c2k)
    xx2k = begin(x_copies(S["K2"], 0, 3))
    finish(xy1k)

    def lane1(l):
        return 64 * gz + jnp.where(l < 96, l, l - 128)

    in1 = inside(24, 128, 8 * gy - 8, lane1, NY1, NZ1)
    for p in range(20):
        L1["K"][p] = L1["K"][p] * (in1 * xin(8 * gx + p - 6, NX1))
    weights(L1, 1, 19, 0.5 * 0.25, False, 2)

    z0r = begin(z_copies(S["P0r"], S["P0rL"], S["P0rR"]))
    finish(xy1f)
    edges = [jnp.where(iota((24, 128), 1) < 64, S["Z1R"][g], S["Z1L"][g]) for g in range(3)]
    lane24 = iota((24, 128), 1)
    for x in range(-H1F, 8 + H1F):
        g, j = (x + 8) // 8, x % 8
        right = pltpu.roll(edges[g], (64 - 8 * j) % 128, 1)
        left = pltpu.roll(edges[g], (56 - 8 * j) % 128, 1)
        F1[6 + x] = jnp.where(lane24 < 64, F1[6 + x], jnp.where(lane24 < 96, right, left))
    finish(z0r)
    centre0(E0r, 0, H0R, S["P0rL"], S["P0rR"])
    xy0r = begin(xy_copies(E0r, H0R + 1, 18, H0R + 1, 16))
    heard(2)
    g3k = gather_start(coarse_2(S["K2"][0, 7:11].reshape(128, 128)), S["G3k"])
    presmooth(L1, F1, X1, (3, 2, 1, 0), 6, 8, G1)

    r1 = F1[6:14, 8:16]
    S["B2f"][...] = coarse_1(r1.reshape(64, 128))
    p2f = begin(pair_copies(S["B2f"], S["B2fS"]))
    S["T1r"][0] = double1(r1.reshape(64, 128)).reshape(8, 8, 128)
    S["T1r"][1] = double1(X1[6:14, 8:16].reshape(64, 128)).reshape(8, 8, 128)
    z1r = begin(z_copies(S["T1r"], S["T1rL"], S["T1rR"]))

    finish(xx2k)
    for p in range(18):
        if p < 7 or p > 10:
            L2["K"][p] = L2["K"][p] * xin(4 * gx + p - 7, NX1 // 2)
    weights(L2, 1, 17, 0.5 * 0.25 ** 2, True, 2)

    finish(p2f)
    put_rows(S["F2"], pair_rows(S["B2f"], S["B2fS"]))
    c2f = begin(column_copies(S["F2"]))
    finish(z1r)
    for i in (0, 1):
        centre1(S["RX1"], i, S["T1r"], S["T1rL"], S["T1rR"], i)

    finish(c2f)
    presmooth(L2, F2, X2, (3, 2, 1, 0), 7, 4, G2)

    g3f = gather_start(coarse_2(F2[7:11].reshape(128, 128)), S["G3f"])
    S["RX2"][0, 7:11] = F2[7:11]
    S["RX2"][1, 7:11] = X2[7:11]

    finish(g3k)
    finish(swap_start(S["G3k"]))

    def unpack3(slots, dst):
        for s in range(NGX):
            t = slots[s]
            dst[5 + 2 * s] = jnp.where(lane16 < 64, t, 0.0)
            dst[6 + 2 * s] = jnp.where(lane16 < 64, pltpu.roll(t, 64, 1), 0.0)

    unpack3(S["G3k"], L3["K"])
    zero3 = jnp.zeros((5, 16, 128), F32)
    for ref in (L3["K"], L3["Va"], L3["Vb"], X3):
        ref[0:5] = zero3
        ref[5 + NX3:10 + NX3] = zero3
    weights(L3, 5, 5 + NX3, 0.5 * 0.25 ** 3, True, 4)


    def compact4(v):
        v = v.reshape(4, 32, 128)
        return (v[0] + pltpu.roll(v[1], 32, 1)) + (pltpu.roll(v[2], 64, 1) + pltpu.roll(v[3], 96, 1))

    def spread4(v):
        return jnp.concatenate([v] + [pltpu.roll(v, 128 - 32 * c, 1) for c in (1, 2, 3)], axis=0)

    h4 = 0.5 * 0.25 ** 4
    k4 = coarse_3(L3["K"][5:5 + NX3].reshape(16 * NX3, 128))
    k4 = compact4(k4)
    row4, lane4 = iota((32, 128), 0), iota((32, 128), 1)
    x_first, x_last = (row4 < 8) & (lane4 < 32), (row4 >= 24) & (lane4 >= 96)
    y_first, y_last = (row4 & 7) == 0, (row4 & 7) == 7
    z_first, z_last = (lane4 & 31) == 0, (lane4 & 31) == 31

    def xup(v):
        return jnp.concatenate([v[8:32], pltpu.roll(v[0:8], 96, 1)], axis=0)

    def xdown(v):
        return jnp.concatenate([pltpu.roll(v[24:32], 32, 1), v[0:24]], axis=0)

    k4xu, k4xd = jnp.where(x_last, 0.0, xup(k4)), jnp.where(x_first, 0.0, xdown(k4))
    k4yu, k4yd = jnp.where(y_last, 0.0, up(k4, 0)), jnp.where(y_first, 0.0, down(k4, 0))
    k4zu, k4zd = jnp.where(z_last, 0.0, up(k4, 1)), jnp.where(z_first, 0.0, down(k4, 1))
    wx4 = jnp.where(x_last, 0.0, h4 * (k4 + k4xu))
    wy4 = jnp.where(y_last, 0.0, h4 * (k4 + k4yu))
    wz4 = jnp.where(z_last, 0.0, h4 * (k4 + k4zu))
    dg4 = h4 * (6.0 * k4 + ((k4xu + k4xd) + (k4yu + k4yd) + (k4zu + k4zd)))

    finish(g3f)
    xx2r = begin(x_copies(S["RX2"], 4, 2))
    xy1r = begin(xy_copies(S["RX1"], 6, 8, H1R, 8))
    finish(swap_start(S["G3f"]))
    unpack3(S["G3f"], F3)
    presmooth(L3, F3, X3, (0, 0, 0, 0), 5, NX3, G3, whole=True)

    f4 = coarse_3(F3[5:5 + NX3].reshape(16 * NX3, 128))
    f4 = compact4(f4)
    x4 = jnp.zeros_like(f4)
    r4 = p4 = f4

    def total4(v):
        t = (v[0:8] + v[8:16]) + (v[16:24] + v[24:32])
        t = jnp.broadcast_to(jnp.sum(t, axis=1, keepdims=True), (8, 128))
        for step in (4, 2, 1):
            t = t + pltpu.roll(t, step, 0)
        return t

    def times4(c, v):
        return (c[None] * v.reshape(4, 8, 128)).reshape(32, 128)

    rr = total4(r4 * r4)
    for _ in range(CG_ITERS):
        q4 = dg4 * p4 - (
            (wx4 * xup(p4) + xdown(wx4 * p4))
            + (wy4 * up(p4, 0) + down(wy4 * p4, 0))
            + (wz4 * up(p4, 1) + down(wz4 * p4, 1)))
        alpha = rr / total4(p4 * q4)
        x4 = x4 + times4(alpha, p4)
        r4 = r4 - times4(alpha, q4)
        rn = total4(r4 * r4)
        p4 = r4 + times4(rn / rr, p4)
        rr = rn

    L3["Va"][5:5 + NX3] = fine_3(spread4(x4)).reshape(NX3, 16, 128)
    postsmooth(L3, F3, X3, (0, 0, 0, 0), 5, NX3, G3)
    X3[5:5 + NX3] = X3[5:5 + NX3] + L3["Va"][5:5 + NX3]

    finish(xx2r)
    z3 = sel((128, 128), lambda c, l: (l >> 1) == c, 1.0)
    y3 = sel((32, 16), lambda r, c: (r >> 1) == c, 1.0)
    t = mmr(X3[pl.ds(2 * gx + 1, 10)].reshape(160, 128), z3)
    for q in range(10):
        e = mml(y3, t[16 * q:16 * q + 16])
        for p in (2 * q - 1, 2 * q):
            if 0 <= p < 18:
                L2["Va"][p] = e
    R2b, X2b = S["RX2"].at[0], S["RX2"].at[1]
    postsmooth(L2, R2b, X2b, (6, 5, 4, 3), 7, 4, G2)
    X2b[4:14] = X2b[4:14] + L2["Va"][4:14]

    finish(xy1r)
    z2 = sel((128, 128), lambda c, l: ((lane1(l) >> 1) == c) & (lane1(l) >= 0) & (lane1(l) < NZ1), 1.0)

    def yrow(r):
        return 8 * gy + r - 8

    y2 = sel((24, 32), lambda r, c: ((yrow(r) >> 1) == c) & (yrow(r) >= 0) & (yrow(r) < NY1), 1.0)
    t = mmr(X2b[4:14].reshape(320, 128), z2)
    for q in range(10):
        e = mml(y2, t[32 * q:32 * q + 32])
        e = e * xin(4 * gx + q - 3, NX1 // 2)
        L1["Va"][2 * q] = e
        L1["Va"][2 * q + 1] = e
    R1b, X1b = S["RX1"].at[0], S["RX1"].at[1]
    postsmooth(L1, R1b, X1b, (5, 4, 3, 2), 6, 8, G1)
    X1b[4:16] = X1b[4:16] + L1["Va"][4:16]

    finish(xy0r)
    unpack0(E0r, 0, H0R, -3, 19, put_r)

    def zfine(c, l):
        z = jnp.where(l < 192, l, l - 256)
        g = 128 * gz + z
        return (((z >> 1) & 127) == c) & (g >= 0) & (g < NZ0)

    def yfine(r, c):
        g = 16 * gy + r - 8
        return (((r - 8) >> 1) + 8 == c) & (g >= 0) & (g < NY0)

    z1 = sel((128, 256), zfine, 1.0)
    y1 = sel((32, 24), yfine, 1.0)
    t = mmr(X1b[4:16].reshape(288, 128), z1)
    for q in range(12):
        e = mml(y1, t[24 * q:24 * q + 24])
        e = e * xin(8 * gx + q - 2, NX1)
        L0["Va"][1 + 2 * q] = e
        L0["Va"][2 + 2 * q] = e
    postsmooth(L0, R0, X0, (3, 2, 1, 0), 5, 16, G0, part=OWN0)
    out_ref[...] = X0[5:21] + L0["Va"][5:21, 8:24, 0:128]


def scratch(sizes):
    ngx, ngy, ngz = sizes
    n_pair = 2 * ngz - 1
    shapes = {
        "C3": (16, 128), "M0": (2, 4, 32, 128),
        "P1": (1, 8, 128), "Z1L": (3, 24, 128), "Z1R": (3, 24, 128),
        "P0": (2, 2, 16, 128), "P0L": (2, 2, 16, 128), "P0R": (2, 2, 16, 128),
        "E0": (2, 16 + 2 * H0, 32, 128),
        "P0r": (1, 2, 16, 128), "P0rL": (1, 2, 16, 128), "P0rR": (1, 2, 16, 128),
        "E0r": (1, 18 + 2 * (H0R + 1), 32, 128),
        "R0": (26, 32, 256), "X0": (26, 16, 128), "K0": (26, 32, 256),
        "T1r": (2, 8, 8, 128), "T1rL": (2, 8, 8, 128), "T1rR": (2, 8, 8, 128),
        "K1": (1, 20, 24, 128), "F1": (1, 20, 24, 128), "RX1": (2, 20, 24, 128), "X1": (20, 24, 128),
        "K2": (1, 18, 32, 128), "F2": (1, 18, 32, 128), "RX2": (2, 18, 32, 128), "X2": (18, 32, 128),
        "B2k": (8, 128), "B2kS": (n_pair, 8, 128),
        "B2f": (8, 128), "B2fS": (n_pair, 8, 128),
        "G3k": (ngx, 16, 128), "G3f": (ngx, 16, 128),
        "K3": (2 * ngx + 10, 16, 128), "F3": (2 * ngx + 10, 16, 128), "X3": (2 * ngx + 10, 16, 128),
    }
    for n in ("T1k", "T1f"):
        for side in ("", "L", "R"):
            shapes[n + side] = (1, 8, 8, 128)
    for n in ("WX", "WY", "WZ", "DG", "IV", "Va", "Vb"):
        shapes[n + "0"] = (26, 32, 256)
        shapes[n + "1"] = (20, 24, 128)
        shapes[n + "2"] = (18, 32, 128)
        shapes[n + "3"] = (2 * ngx + 10, 16, 128)
    names = list(shapes) + ["ss", "rs", "ls", "dis"]
    n_sem = 74 + 2 * (n_pair + 3 * (ngy // 2) - 1) + 2 + 4 + 2 * ngx
    kinds = [pltpu.VMEM(shapes[n], F32) for n in shapes]
    kinds += [pltpu.SemaphoreType.DMA((n_sem,)), pltpu.SemaphoreType.DMA((n_sem,))]
    kinds += [pltpu.SemaphoreType.DMA((2,)), pltpu.SemaphoreType.REGULAR((3,))]
    return names, kinds


def solution(mesh):
    sizes = (mesh.shape["gx"], mesh.shape["gy"], mesh.shape["gz"])
    names, kinds = scratch(sizes)
    spec = P("gx", "gy", "gz")

    def local(right_side, conductivity):
        return pl.pallas_call(
            functools.partial(kernel, sizes, names),
            out_shape=jax.ShapeDtypeStruct(right_side.shape, F32),
            in_specs=[pl.BlockSpec(memory_space=pl.ANY)] * 2,
            out_specs=pl.BlockSpec(memory_space=pltpu.VMEM),
            scratch_shapes=kinds,
            compiler_params=pltpu.CompilerParams(
                collective_id=0, has_side_effects=True, vmem_limit_bytes=48 * 1024 * 1024
            ),
        )(right_side, conductivity)

    return jax.shard_map(local, mesh=mesh, in_specs=(spec, spec), out_specs=spec, check_vma=False)
```

```python
import functools

import jax
import jax.numpy as jnp
from jax import lax
from jax.experimental import pallas as pl
from jax.experimental.pallas import tpu as pltpu
from jax.sharding import PartitionSpec as P

F32 = jnp.float32
MESH = pl.DeviceIdType.MESH
CG_ITERS = 8
THETA = 1.125
DELTA = 0.875

H0, H0R = 5, 3
H1K, H1F, H1R = 6, 4, 5

G0, G1, G2, G3 = 8, 20, 20, 32
OWN0 = (slice(8, 24), slice(0, 128))


def cheb_table():
    sigma = THETA / DELTA
    rho_now = 1.0 / sigma
    table = []
    for _ in range(3):
        rho_next = 1.0 / (2.0 * sigma - rho_now)
        table.append((rho_next * rho_now, 2.0 * rho_next / DELTA))
        rho_now = rho_next
    return table


TABLE = cheb_table()


def parts_of(v):
    high = v.astype(jnp.bfloat16)
    rest = v - high.astype(F32)
    mid = rest.astype(jnp.bfloat16)
    return high, mid, (rest - mid.astype(F32)).astype(jnp.bfloat16)


def dot(a, b):
    return jnp.dot(a, b, preferred_element_type=F32)


def mml(m, v):
    m = m.astype(jnp.bfloat16)
    high, mid, low = parts_of(v)
    return dot(m, high) + (dot(m, mid) + dot(m, low))


def mmr(v, m):
    m = m.astype(jnp.bfloat16)
    high, mid, low = parts_of(v)
    return dot(high, m) + (dot(mid, m) + dot(low, m))


def iota(shape, dim):
    return lax.broadcasted_iota(jnp.int32, shape, dim)


def flat(v):
    return v.reshape(v.shape[0] * v.shape[1], v.shape[2])


def up(v, dim, step=1):
    return pltpu.roll(v, v.shape[dim] - step, dim)


def down(v, dim, step=1):
    return pltpu.roll(v, step, dim)


def planes_loop(lo, hi, group, fn):
    count = (hi - lo) // group
    if count > 1:
        def body(i, carry):
            fn(lo + i * group, group)
            return carry

        lax.fori_loop(0, count, body, 0)
    elif count == 1:
        fn(lo, group)
    rest = hi - lo - count * group
    if rest:
        fn(lo + count * group, rest)


def weights(lev, lo, hi, h, whole, group):
    K = lev["K"]
    rows, lanes = K.shape[1], K.shape[2]

    def one(p, g):
        n = g * rows
        k = flat(K[pl.ds(p, g)])
        kxu = flat(K[pl.ds(p + 1, g)])
        kxd = flat(K[pl.ds(p - 1, g)])
        kyu, kyd, kzu, kzd = up(k, 0), down(k, 0), up(k, 1), down(k, 1)
        if whole:
            row = iota((n, lanes), 0) & (rows - 1)
            lane = iota((n, lanes), 1)
            kyu = jnp.where(row == rows - 1, 0.0, kyu)
            kyd = jnp.where(row == 0, 0.0, kyd)
            kzu = jnp.where(lane == lanes - 1, 0.0, kzu)
            kzd = jnp.where(lane == 0, 0.0, kzd)
        wy, wz = h * (k + kyu), h * (k + kzu)
        diag = h * (6.0 * k + ((kxu + kxd) + (kyu + kyd) + (kzu + kzd)))
        if whole:
            wy = jnp.where(row == rows - 1, 0.0, wy)
            wz = jnp.where(lane == lanes - 1, 0.0, wz)
        shape = (g, rows, lanes)
        lev["WX"][pl.ds(p, g)] = (h * (k + kxu)).reshape(shape)
        lev["WY"][pl.ds(p, g)] = wy.reshape(shape)
        lev["WZ"][pl.ds(p, g)] = wz.reshape(shape)
        lev["DG"][pl.ds(p, g)] = diag.reshape(shape)
        lev["IV"][pl.ds(p, g)] = jnp.where(k > 0.0, 1.0 / diag, 0.0).reshape(shape)

    lev["WX"][lo - 1] = h * (K[lo - 1] + K[lo])
    planes_loop(lo, hi, group, one)


def sweep(lev, R, X, src, dst, lo, hi, a, b, group, first=False, want_dir=True, part=None,
          fold=False, out=None):
    Vi, Vo = lev[src], lev[dst]

    def one(p, g):
        v = [Vi[p - 1 + i] for i in range(g + 2)]
        wx = [lev["WX"][p - 1 + i] for i in range(g + 1)]
        for i in range(g):
            c = v[i + 1]
            wy, wz = lev["WY"][p + i], lev["WZ"][p + i]
            total = wx[i + 1] * v[i + 2] + wx[i] * v[i]
            total = total + (wy * up(c, 0) + down(wy * c, 0))
            total = total + (wz * up(c, 1) + down(wz * c, 1))
            r = R[p + i] - (lev["DG"][p + i] * c - total)
            if want_dir:
                d = b * (lev["IV"][p + i] * r)
                d = d + a * c if a else d
            step = c + d if fold else c
            own = step if part is None else step[part[0], part[1]]
            x = own if first else X[p + i] + own
            if out is None:
                X[p + i] = x
            else:
                out[p + i - lo] = x
            if not fold:
                R[p + i] = r
            if want_dir and not fold:
                Vo[p + i] = d

    planes_loop(lo, hi, group, one)


def presmooth(lev, R, X, halos, base, own, group, whole=False, part=None, after=None):
    h = 0 if whole else halos[0] + 1
    lo, hi = base - h, base + own + h

    def start(p, g):
        here = pl.ds(p, g)
        lev["Va"][here] = (lev["IV"][here] * R[here]) * (1.0 / THETA)

    planes_loop(lo, hi, group, start)
    names = ("Va", "Vb")
    for j in range(4):
        a, b = TABLE[j] if j < 3 else (0.0, 0.0)
        lo, hi = base - halos[j], base + own + halos[j]
        sweep(lev, R, X, names[j % 2], names[1 - j % 2], lo, hi, a, b, group,
              first=(j == 0), want_dir=(j < 3), part=part)
        if after:
            after(j)


def postsmooth(lev, R, X, halos, base, own, group, part=None, out=None):
    names = ("Va", "Vb")
    for j in range(4):
        a, b = TABLE[j - 1] if j > 0 else (0.0, 1.0 / THETA)
        lo, hi = base - halos[j], base + own + halos[j]
        sweep(lev, R, X, names[j % 2], names[1 - j % 2], lo, hi, a, b, group, part=part,
              fold=(j == 3), out=out if j == 3 else None)


def kernel(sizes, names, *refs):
    f_hbm, k_hbm, out_ref = refs[:3]
    S = dict(zip(names, refs[3:]))
    E0 = S["E0"]
    loads = [pltpu.make_async_copy(src, E0.at[i, pl.ds(H0, 16), pl.ds(8, 16)], S["ls"].at[i])
             for i, src in enumerate((f_hbm, k_hbm))]
    for c in loads:
        c.start()
    ss, rs = S["ss"], S["rs"]
    NGX, NGY, NGZ = sizes
    NYC = NGY // 2
    NX0, NY0, NZ0 = 16 * NGX, 16 * NGY, 128 * NGZ
    NX1, NY1, NZ1 = NX0 // 2, NY0 // 2, NZ0 // 2
    NX3 = 2 * NGX
    gx, gy, gz = lax.axis_index("gx"), lax.axis_index("gy"), lax.axis_index("gz")
    core, chip = gy % 2, gy // 2

    def at(dx=0, dy=0, dz=0):
        return ((gx + dx + NGX) % NGX, (gy + dy + NGY) % NGY, (gz + dz + NGZ) % NGZ)

    pair_peers = [(c, dz) for c in (0, 1) for dz in range(NGZ) if (c, dz) != (0, 0)]

    def pair_dev(c, dz):
        return (gx, chip * 2 + (core + c) % 2, (gz + dz) % NGZ)

    def chip_dev(dy, dx=0):
        return ((gx + dx + NGX) % NGX, ((chip + dy) % NYC) * 2 + core, gz)

    sides = [(dx, dy) for dx in (-1, 0, 1) for dy in (-1, 0, 1) if (dx, dy) != (0, 0)]

    barrier = pltpu.get_barrier_semaphore()
    greeted = [pair_dev(c, dz) for c, dz in pair_peers]
    greeted += [chip_dev(dy, dx) for dx in (-1, 0, 1) for dy in range(1, NYC)]
    greeted += [at(dx=dx, dy=dy) for dx, dy in sides]
    for dev in greeted:
        pl.semaphore_signal(barrier, inc=1, device_id=dev, device_id_type=MESH)

    def pass_on(i):
        for d in (2 ** i, -(2 ** i)):
            pl.semaphore_signal(S["dis"].at[i], inc=1, device_id=at(dx=d), device_id_type=MESH)

    def heard(i):
        pl.semaphore_wait(S["dis"].at[i], 2)

    counter = [0]

    def remote(src, dst, dev):
        i = counter[0]
        counter[0] += 1
        return pltpu.make_async_remote_copy(
            src_ref=src, dst_ref=dst, send_sem=ss.at[i], recv_sem=rs.at[i],
            device_id=dev, device_id_type=MESH,
        )

    def begin(copies):
        for c in copies:
            c.start()
        return copies

    def finish(copies):
        for c in copies:
            c.wait()

    def z_copies(buf, from_left, from_right):
        return [remote(buf, from_left, at(dz=1)), remote(buf, from_right, at(dz=-1))]

    def xy_copies(buf, base, own, h, rows):
        fields = slice(None)
        xs = {1: (base + own - h, base - h, h), -1: (base, base + own, h), 0: (base, base, own)}
        ys = {1: (rows, 0, 8), -1: (8, 8 + rows, 8), 0: (8, 8, rows)}
        out = []
        for dx, dy in sides:
            (sx, tx, nx), (sy, ty, ny) = xs[dx], ys[dy]
            out.append(remote(
                buf.at[fields, pl.ds(sx, nx), pl.ds(sy, ny)],
                buf.at[fields, pl.ds(tx, nx), pl.ds(ty, ny)],
                at(dx=dx, dy=dy)))
        return out

    def x_copies(buf, n1, n2):
        out = []
        for d, n in ((1, n1), (2, n2)):
            if n:
                fld = slice(None) if d == 1 else slice(0, 1)
                out.append(remote(buf.at[fld, pl.ds(11 - n, n)],
                                  buf.at[fld, pl.ds(7 - 4 * (d - 1) - n, n)], at(dx=d)))
                out.append(remote(buf.at[fld, pl.ds(7, n)],
                                  buf.at[fld, pl.ds(11 + 4 * (d - 1), n)], at(dx=-d)))
        return out

    def pair_copies(buf, slots):
        return [remote(buf, slots.at[i], pair_dev(c, dz)) for i, (c, dz) in enumerate(pair_peers)]

    column = [(dx, dy) for dx in (-1, 0, 1) for dy in range(NYC) if (dx, dy) != (0, 0)]

    def column_copies(buf):
        rows = pl.ds(pl.multiple_of(chip * 8, 8), 8)
        mine = buf.at[0, pl.ds(7, 4), rows]
        return [remote(mine, buf.at[0, pl.ds(7 - 4 * dx, 4), rows], chip_dev(dy, dx)) for dx, dy in column]

    lane16 = iota((16, 128), 1)
    lane8 = iota((8, 128), 1)

    def sel(shape, cond, value):
        return jnp.where(cond(iota(shape, 0), iota(shape, 1)), value, 0.0).astype(F32)

    def coarse_0(r):
        c = sel((64, 256), lambda r, c: ((c >> 5) == (r >> 3)) & (((c & 15) >> 1) == (r & 7)), 0.25)
        z = sel((128, 128), lambda l, c: (l >> 1) == (c & 63), 0.5)
        return mmr(mml(c, r), z)

    def coarse_1(r):
        c = sel((32, 64), lambda r, c: ((c >> 4) == (r >> 3)) & (((c & 7) >> 1) == (r & 7) - 4 * core), 0.25)
        z = sel((128, 128), lambda l, c: (l < 64) & (c == (l >> 1)), 0.5)
        t = mmr(mml(c, r), z)
        return (t[0:8] + pltpu.roll(t[8:16], 32, 1)) + (pltpu.roll(t[16:24], 64, 1) + pltpu.roll(t[24:32], 96, 1))

    def coarse_2(r):
        c = sel((32, 128), lambda r, c: ((c >> 6) == (r >> 4)) & (((c & 31) >> 1) == (r & 15)), 0.25)
        z = sel((128, 128), lambda l, c: (l >> 1) == (c & 63), 0.5)
        t = mmr(mml(c, r), z)
        return jnp.where(lane16 < 64, t[0:16], t[16:32])

    def coarse_3(r):
        n = r.shape[0]
        c = sel((n // 4, n), lambda r, c: ((c >> 5) == (r >> 3)) & (((c & 15) >> 1) == (r & 7)), 0.25)
        z = sel((128, 128), lambda l, c: (l < 64) & ((l >> 1) == c), 0.5)
        return mmr(mml(c, r), z)

    def fine_3(e):
        n = e.shape[0]
        u = sel((4 * n, n), lambda r, c: ((r >> 5) == (c >> 3)) & (((r & 15) >> 1) == (c & 7)), 1.0)
        z = sel((128, 128), lambda c, l: (l < 64) & ((l >> 1) == c), 1.0)
        return mml(u, mmr(e, z))

    def pack0(field):
        out = []
        for g in range(2):
            acc = None
            for j in range(8):
                t = pltpu.roll(field(8 * g + j), 16 * j + 8, 1)
                acc = t if acc is None else jnp.where((lane16 >> 4) == j, t, acc)
            out.append(acc)
        return out

    def merge0(from_left, from_right):
        return jnp.where((lane16 & 15) >= 8, from_right, from_left)

    def centre0(buf, fld, h, from_left, from_right):
        for g, m in ((0, h + 1), (1, h + 18)):
            buf[fld, m, 8:24] = merge0(from_left[fld, g], from_right[fld, g])

    def open0(fld, lo, hi, put):
        for x in range(lo, hi):
            g, j = (x + 8) // 8, x % 8
            put(x, E0[fld, H0 + x], pltpu.roll(M0[fld, g], (120 - 16 * j) % 128, 1))

    def unpack0(buf, fld, h, lo, hi, put):
        for x in range(lo, hi):
            if x < 0:
                main, m, j = x + h, h, x + 8
            elif x < 16:
                main, m, j = h + 2 + x, (h + 1 if x < 8 else h + 18), x % 8
            else:
                main, m, j = h + 20 + x - 16, h + 19, x - 16
            put(x, buf[fld, main], pltpu.roll(buf[fld, m], (120 - 16 * j) % 128, 1))

    def pack1(v):
        acc = None
        for j in range(8):
            t = v[8 * j:8 * j + 8]
            low = pltpu.roll(t, 8 * j, 1) if j else t
            high = pltpu.roll(t, 8 * j + 8, 1)
            acc = low if acc is None else jnp.where((lane8 >> 3) == j, low, acc)
            acc = jnp.where((lane8 >> 3) == 8 + j, high, acc)
        return acc

    def corner_copies(pack, from_left, from_right):
        out = []
        for dz, buf in ((1, from_left), (-1, from_right)):
            for dx in (-1, 0, 1):
                for dy in (-1, 0, 1):
                    out.append(remote(pack, buf.at[pl.ds(1 - dx, 1), pl.ds(8 - 8 * dy, 8)], at(dx, dy, dz)))
        return out

    def double1(v):
        n = v.shape[0]
        return jnp.where(iota((n, 128), 1) < 64, v, pltpu.roll(v, 64, 1))

    def centre1(buf, fld, own, left, right, i):
        lane = iota((64, 128), 1)
        t = jnp.where(lane < 64, flat(own[i]), jnp.where(lane < 96, flat(right[i]), flat(left[i])))
        buf[fld, 6:14, 8:16] = t.reshape(8, 8, 128)

    def inside(n_rows, n_lanes, row0, lane_of, ny, nz):
        y = iota((n_rows, n_lanes), 0) + row0
        z = lane_of(iota((n_rows, n_lanes), 1))
        return jnp.where((y >= 0) & (y < ny) & (z >= 0) & (z < nz), 1.0, 0.0).astype(F32)

    def xin(x, n):
        return jnp.where((x >= 0) & (x < n), 1.0, 0.0).astype(F32)

    L0 = {n: S[n + "0"] for n in ("K", "WX", "WY", "WZ", "DG", "IV", "Va", "Vb")}
    L1 = {n: S[n + "1"] for n in ("WX", "WY", "WZ", "DG", "IV", "Va", "Vb")}
    L1["K"] = S["K1"].at[0]
    L2 = {n: S[n + "2"] for n in ("WX", "WY", "WZ", "DG", "IV", "Va", "Vb")}
    L2["K"] = S["K2"].at[0]
    L3 = {n: S[n + "3"] for n in ("K", "WX", "WY", "WZ", "DG", "IV", "Va", "Vb")}
    R0, X0 = S["R0"], S["X0"]
    F1, X1 = S["F1"].at[0], S["X1"]
    F2, X2 = S["F2"].at[0], S["X2"]
    F3, X3 = S["F3"], S["X3"]

    for c in loads:
        c.wait()
    E0r, M0 = S["E0r"], S["M0"]
    for fld in (0, 1):
        for g, t in enumerate(pack0(lambda x: E0[fld, H0 + x, 8:24])):
            S["P0"][fld, g] = t
    pl.semaphore_wait(barrier, len(greeted))
    z0 = begin(z_copies(S["P0"], S["P0L"], S["P0R"]))
    xy0 = begin(xy_copies(E0, H0, 16, H0, 16))
    pass_on(0)
    finish(z0)
    for fld in (0, 1):
        for g in (0, 1):
            M0[fld, 1 + g, 8:24] = merge0(S["P0L"][fld, g], S["P0R"][fld, g])
    xy0 += begin(xy_copies(M0, 1, 2, 1, 16))

    k1 = coarse_0(E0[1, H0:H0 + 16, 8:24].reshape(256, 128))
    S["T1k"][0] = k1.reshape(8, 8, 128)
    S["B2k"][...] = coarse_1(k1)
    z1k = begin(z_copies(S["T1k"], S["T1kL"], S["T1kR"]))
    p2k = begin(pair_copies(S["B2k"], S["B2kS"]))
    heard(0)
    pass_on(1)

    def pair_rows(own, slots):
        blocks = [[] for _ in range(NGZ)]
        blocks[0].append(own[...])
        for i, (_, dz) in enumerate(pair_peers):
            blocks[dz].append(slots[i])
        rows = [jnp.zeros((8, 128), F32)] * 4
        for dz in range(NGZ):
            g = (gz - dz + NGZ) % NGZ
            t = pltpu.roll(sum(blocks[dz][1:], blocks[dz][0]), 32 * g, 1)
            here = (lane8 >> 5) == g
            for x in range(4):
                rows[x] = jnp.where(here, t if x == 0 else pltpu.roll(t, 128 - 32 * x, 1), rows[x])
        return rows

    def put_rows(buf, rows):
        for x in range(4):
            buf[0, 7 + x, my_rows] = rows[x]

    my_rows = pl.ds(pl.multiple_of(chip * 8, 8), 8)
    my_half = pl.ds(pl.multiple_of(core * 8, 8), 8)

    def gather_start(v, buf):
        S["C3"][...] = v
        buf[gx, my_half] = S["C3"][my_half]
        mine = buf.at[gx, my_half]
        return begin([remote(mine, mine, at(dx=d)) for d in range(1, NGX)])

    def swap_start(buf):
        mine = buf.at[:, my_half]
        return begin([remote(mine, mine, pair_dev(1, 0))])

    finish(z1k)
    centre1(S["K1"], 0, S["T1k"], S["T1kL"], S["T1kR"], 0)
    finish(p2k)
    put_rows(S["K2"], pair_rows(S["B2k"], S["B2kS"]))

    finish(xy0)
    xy1k = begin(xy_copies(S["K1"], 6, 8, H1K, 8))
    c2k = begin(column_copies(S["K2"]))
    heard(1)
    pass_on(2)

    def lane0(l):
        return 128 * gz + jnp.where(l < 192, l, l - 256)

    in0 = inside(32, 256, 16 * gy - 8, lane0, NY0, NZ0)

    def put_k(x, main, halo):
        w = xin(16 * gx + x, NX0)
        L0["K"][x + 5, :, 0:128] = main * (in0[:, 0:128] * w)
        L0["K"][x + 5, :, 128:256] = halo * (in0[:, 128:256] * w)

    def put_r(x, main, halo):
        R0[x + 5, :, 0:128] = main
        R0[x + 5, :, 128:256] = halo

    open0(1, -5, 21, put_k)
    open0(0, -4, 20, put_r)
    weights(L0, 1, 25, 0.5, False, 1)

    presmooth(L0, R0, X0, (3, 2, 1, 0), 5, 16, G0, part=OWN0)

    own0 = R0[5:21, 8:24, 0:128]
    f1 = coarse_0(own0.reshape(256, 128))
    S["F1"][0, 6:14, 8:16] = f1.reshape(8, 8, 128)
    S["P1"][0] = pack1(f1)
    xy1f = begin(xy_copies(S["F1"], 6, 8, H1F, 8) + corner_copies(S["P1"], S["Z1L"], S["Z1R"]))
    for g, t in enumerate(pack0(lambda x: R0[5 + x, 8:24, 0:128])):
        S["P0r"][0, g] = t
    E0r[0, H0R + 2:H0R + 18, 8:24] = own0
    finish(c2k)
    xx2k = begin(x_copies(S["K2"], 0, 3))
    finish(xy1k)

    def lane1(l):
        return 64 * gz + jnp.where(l < 96, l, l - 128)

    in1 = inside(24, 128, 8 * gy - 8, lane1, NY1, NZ1)
    for p in range(20):
        L1["K"][p] = L1["K"][p] * (in1 * xin(8 * gx + p - 6, NX1))
    weights(L1, 1, 19, 0.5 * 0.25, False, 2)

    z0r = begin(z_copies(S["P0r"], S["P0rL"], S["P0rR"]))
    finish(xy1f)
    edges = [jnp.where(iota((24, 128), 1) < 64, S["Z1R"][g], S["Z1L"][g]) for g in range(3)]
    lane24 = iota((24, 128), 1)
    for x in range(-H1F, 8 + H1F):
        g, j = (x + 8) // 8, x % 8
        right = pltpu.roll(edges[g], (64 - 8 * j) % 128, 1)
        left = pltpu.roll(edges[g], (56 - 8 * j) % 128, 1)
        F1[6 + x] = jnp.where(lane24 < 64, F1[6 + x], jnp.where(lane24 < 96, right, left))
    finish(z0r)
    centre0(E0r, 0, H0R, S["P0rL"], S["P0rR"])
    xy0r = begin(xy_copies(E0r, H0R + 1, 18, H0R + 1, 16))
    heard(2)
    g3k = gather_start(coarse_2(S["K2"][0, 7:11].reshape(128, 128)), S["G3k"])
    presmooth(L1, F1, X1, (3, 2, 1, 0), 6, 8, G1)

    r1 = F1[6:14, 8:16]
    S["B2f"][...] = coarse_1(r1.reshape(64, 128))
    p2f = begin(pair_copies(S["B2f"], S["B2fS"]))
    S["T1r"][0] = double1(r1.reshape(64, 128)).reshape(8, 8, 128)
    S["T1r"][1] = double1(X1[6:14, 8:16].reshape(64, 128)).reshape(8, 8, 128)
    z1r = begin(z_copies(S["T1r"], S["T1rL"], S["T1rR"]))

    finish(xx2k)
    for p in range(18):
        if p < 7 or p > 10:
            L2["K"][p] = L2["K"][p] * xin(4 * gx + p - 7, NX1 // 2)
    weights(L2, 1, 17, 0.5 * 0.25 ** 2, True, 2)

    finish(p2f)
    put_rows(S["F2"], pair_rows(S["B2f"], S["B2fS"]))
    c2f = begin(column_copies(S["F2"]))
    finish(z1r)
    for i in (0, 1):
        centre1(S["RX1"], i, S["T1r"], S["T1rL"], S["T1rR"], i)

    finish(c2f)
    presmooth(L2, F2, X2, (3, 2, 1, 0), 7, 4, G2)

    g3f = gather_start(coarse_2(F2[7:11].reshape(128, 128)), S["G3f"])
    S["RX2"][0, 7:11] = F2[7:11]
    S["RX2"][1, 7:11] = X2[7:11]

    finish(g3k)
    finish(swap_start(S["G3k"]))

    def unpack3(slots, dst):
        for s in range(NGX):
            t = slots[s]
            dst[5 + 2 * s] = jnp.where(lane16 < 64, t, 0.0)
            dst[6 + 2 * s] = jnp.where(lane16 < 64, pltpu.roll(t, 64, 1), 0.0)

    unpack3(S["G3k"], L3["K"])
    zero3 = jnp.zeros((5, 16, 128), F32)
    for ref in (L3["K"], L3["Va"], L3["Vb"], X3):
        ref[0:5] = zero3
        ref[5 + NX3:10 + NX3] = zero3
    weights(L3, 5, 5 + NX3, 0.5 * 0.25 ** 3, True, 4)


    def compact4(v):
        v = v.reshape(4, 32, 128)
        return (v[0] + pltpu.roll(v[1], 32, 1)) + (pltpu.roll(v[2], 64, 1) + pltpu.roll(v[3], 96, 1))

    def spread4(v):
        return jnp.concatenate([v] + [pltpu.roll(v, 128 - 32 * c, 1) for c in (1, 2, 3)], axis=0)

    h4 = 0.5 * 0.25 ** 4
    k4 = coarse_3(L3["K"][5:5 + NX3].reshape(16 * NX3, 128))
    k4 = compact4(k4)
    row4, lane4 = iota((32, 128), 0), iota((32, 128), 1)
    x_first, x_last = (row4 < 8) & (lane4 < 32), (row4 >= 24) & (lane4 >= 96)
    y_first, y_last = (row4 & 7) == 0, (row4 & 7) == 7
    z_first, z_last = (lane4 & 31) == 0, (lane4 & 31) == 31

    def xup(v):
        return jnp.concatenate([v[8:32], pltpu.roll(v[0:8], 96, 1)], axis=0)

    def xdown(v):
        return jnp.concatenate([pltpu.roll(v[24:32], 32, 1), v[0:24]], axis=0)

    k4xu, k4xd = jnp.where(x_last, 0.0, xup(k4)), jnp.where(x_first, 0.0, xdown(k4))
    k4yu, k4yd = jnp.where(y_last, 0.0, up(k4, 0)), jnp.where(y_first, 0.0, down(k4, 0))
    k4zu, k4zd = jnp.where(z_last, 0.0, up(k4, 1)), jnp.where(z_first, 0.0, down(k4, 1))
    wx4 = jnp.where(x_last, 0.0, h4 * (k4 + k4xu))
    wy4 = jnp.where(y_last, 0.0, h4 * (k4 + k4yu))
    wz4 = jnp.where(z_last, 0.0, h4 * (k4 + k4zu))
    dg4 = h4 * (6.0 * k4 + ((k4xu + k4xd) + (k4yu + k4yd) + (k4zu + k4zd)))

    finish(g3f)
    xx2r = begin(x_copies(S["RX2"], 4, 2))
    xy1r = begin(xy_copies(S["RX1"], 6, 8, H1R, 8))
    finish(swap_start(S["G3f"]))
    unpack3(S["G3f"], F3)
    presmooth(L3, F3, X3, (0, 0, 0, 0), 5, NX3, G3, whole=True)

    f4 = coarse_3(F3[5:5 + NX3].reshape(16 * NX3, 128))
    f4 = compact4(f4)
    x4 = jnp.zeros_like(f4)
    r4 = p4 = f4

    def total4(v):
        t = (v[0:8] + v[8:16]) + (v[16:24] + v[24:32])
        t = jnp.broadcast_to(jnp.sum(t, axis=1, keepdims=True), (8, 128))
        for step in (4, 2, 1):
            t = t + pltpu.roll(t, step, 0)
        return t

    def times4(c, v):
        return (c[None] * v.reshape(4, 8, 128)).reshape(32, 128)

    rr = total4(r4 * r4)
    for _ in range(CG_ITERS):
        q4 = dg4 * p4 - (
            (wx4 * xup(p4) + xdown(wx4 * p4))
            + (wy4 * up(p4, 0) + down(wy4 * p4, 0))
            + (wz4 * up(p4, 1) + down(wz4 * p4, 1)))
        alpha = rr / total4(p4 * q4)
        x4 = x4 + times4(alpha, p4)
        r4 = r4 - times4(alpha, q4)
        rn = total4(r4 * r4)
        p4 = r4 + times4(rn / rr, p4)
        rr = rn

    L3["Va"][5:5 + NX3] = fine_3(spread4(x4)).reshape(NX3, 16, 128)
    postsmooth(L3, F3, X3, (0, 0, 0, 0), 5, NX3, G3)

    finish(xx2r)
    z3 = sel((128, 128), lambda c, l: (l >> 1) == c, 1.0)
    y3 = sel((32, 16), lambda r, c: (r >> 1) == c, 1.0)
    t = mmr(X3[pl.ds(2 * gx + 1, 10)].reshape(160, 128), z3)
    for q in range(10):
        e = mml(y3, t[16 * q:16 * q + 16])
        for p in (2 * q - 1, 2 * q):
            if 0 <= p < 18:
                L2["Va"][p] = e
    R2b, X2b = S["RX2"].at[0], S["RX2"].at[1]
    postsmooth(L2, R2b, X2b, (6, 5, 4, 3), 7, 4, G2)

    finish(xy1r)
    z2 = sel((128, 128), lambda c, l: ((lane1(l) >> 1) == c) & (lane1(l) >= 0) & (lane1(l) < NZ1), 1.0)

    def yrow(r):
        return 8 * gy + r - 8

    y2 = sel((24, 32), lambda r, c: ((yrow(r) >> 1) == c) & (yrow(r) >= 0) & (yrow(r) < NY1), 1.0)
    t = mmr(X2b[4:14].reshape(320, 128), z2)
    for q in range(10):
        e = mml(y2, t[32 * q:32 * q + 32])
        e = e * xin(4 * gx + q - 3, NX1 // 2)
        L1["Va"][2 * q] = e
        L1["Va"][2 * q + 1] = e
    R1b, X1b = S["RX1"].at[0], S["RX1"].at[1]
    postsmooth(L1, R1b, X1b, (5, 4, 3, 2), 6, 8, G1)

    finish(xy0r)
    unpack0(E0r, 0, H0R, -3, 19, put_r)

    def zfine(c, l):
        z = jnp.where(l < 192, l, l - 256)
        g = 128 * gz + z
        return (((z >> 1) & 127) == c) & (g >= 0) & (g < NZ0)

    def yfine(r, c):
        g = 16 * gy + r - 8
        return (((r - 8) >> 1) + 8 == c) & (g >= 0) & (g < NY0)

    z1 = sel((128, 256), zfine, 1.0)
    y1 = sel((32, 24), yfine, 1.0)
    t = mmr(X1b[4:16].reshape(288, 128), z1)
    for q in range(12):
        e = mml(y1, t[24 * q:24 * q + 24])
        e = e * xin(8 * gx + q - 2, NX1)
        L0["Va"][1 + 2 * q] = e
        L0["Va"][2 + 2 * q] = e
    postsmooth(L0, R0, X0, (3, 2, 1, 0), 5, 16, G0, part=OWN0, out=out_ref)


def scratch(sizes):
    ngx, ngy, ngz = sizes
    n_pair = 2 * ngz - 1
    shapes = {
        "C3": (16, 128), "M0": (2, 4, 32, 128),
        "P1": (1, 8, 128), "Z1L": (3, 24, 128), "Z1R": (3, 24, 128),
        "P0": (2, 2, 16, 128), "P0L": (2, 2, 16, 128), "P0R": (2, 2, 16, 128),
        "E0": (2, 16 + 2 * H0, 32, 128),
        "P0r": (1, 2, 16, 128), "P0rL": (1, 2, 16, 128), "P0rR": (1, 2, 16, 128),
        "E0r": (1, 18 + 2 * (H0R + 1), 32, 128),
        "R0": (26, 32, 256), "X0": (26, 16, 128), "K0": (26, 32, 256),
        "T1r": (2, 8, 8, 128), "T1rL": (2, 8, 8, 128), "T1rR": (2, 8, 8, 128),
        "K1": (1, 20, 24, 128), "F1": (1, 20, 24, 128), "RX1": (2, 20, 24, 128), "X1": (20, 24, 128),
        "K2": (1, 18, 32, 128), "F2": (1, 18, 32, 128), "RX2": (2, 18, 32, 128), "X2": (18, 32, 128),
        "B2k": (8, 128), "B2kS": (n_pair, 8, 128),
        "B2f": (8, 128), "B2fS": (n_pair, 8, 128),
        "G3k": (ngx, 16, 128), "G3f": (ngx, 16, 128),
        "K3": (2 * ngx + 10, 16, 128), "F3": (2 * ngx + 10, 16, 128), "X3": (2 * ngx + 10, 16, 128),
    }
    for n in ("T1k", "T1f"):
        for side in ("", "L", "R"):
            shapes[n + side] = (1, 8, 8, 128)
    for n in ("WX", "WY", "WZ", "DG", "IV", "Va", "Vb"):
        shapes[n + "0"] = (26, 32, 256)
        shapes[n + "1"] = (20, 24, 128)
        shapes[n + "2"] = (18, 32, 128)
        shapes[n + "3"] = (2 * ngx + 10, 16, 128)
    names = list(shapes) + ["ss", "rs", "ls", "dis"]
    n_sem = 74 + 2 * (n_pair + 3 * (ngy // 2) - 1) + 2 + 4 + 2 * ngx
    kinds = [pltpu.VMEM(shapes[n], F32) for n in shapes]
    kinds += [pltpu.SemaphoreType.DMA((n_sem,)), pltpu.SemaphoreType.DMA((n_sem,))]
    kinds += [pltpu.SemaphoreType.DMA((2,)), pltpu.SemaphoreType.REGULAR((3,))]
    return names, kinds


def solution(mesh):
    sizes = (mesh.shape["gx"], mesh.shape["gy"], mesh.shape["gz"])
    names, kinds = scratch(sizes)
    spec = P("gx", "gy", "gz")

    def local(right_side, conductivity):
        return pl.pallas_call(
            functools.partial(kernel, sizes, names),
            out_shape=jax.ShapeDtypeStruct(right_side.shape, F32),
            in_specs=[pl.BlockSpec(memory_space=pl.ANY)] * 2,
            out_specs=pl.BlockSpec(memory_space=pltpu.VMEM),
            scratch_shapes=kinds,
            compiler_params=pltpu.CompilerParams(
                collective_id=0, has_side_effects=True, vmem_limit_bytes=57 * 1024 * 1024
            ),
        )(right_side, conductivity)

    return jax.shard_map(local, mesh=mesh, in_specs=(spec, spec), out_specs=spec, check_vma=False)
```

```python
import functools

import jax
import jax.numpy as jnp
from jax import lax
from jax.experimental import pallas as pl
from jax.experimental.pallas import tpu as pltpu
from jax.sharding import PartitionSpec as P

F32 = jnp.float32
MESH = pl.DeviceIdType.MESH
CG_ITERS = 8
THETA = 1.125
DELTA = 0.875

H0, H0R = 5, 3
H1K, H1F, H1R = 6, 4, 5

G0, G1, G2, G3 = 8, 20, 20, 32
OWN0 = (slice(8, 24), slice(0, 128))


def cheb_table():
    sigma = THETA / DELTA
    rho_now = 1.0 / sigma
    table = []
    for _ in range(3):
        rho_next = 1.0 / (2.0 * sigma - rho_now)
        table.append((rho_next * rho_now, 2.0 * rho_next / DELTA))
        rho_now = rho_next
    return table


TABLE = cheb_table()


def parts_of(v):
    high = v.astype(jnp.bfloat16)
    rest = v - high.astype(F32)
    mid = rest.astype(jnp.bfloat16)
    return high, mid, (rest - mid.astype(F32)).astype(jnp.bfloat16)


def dot(a, b):
    return jnp.dot(a, b, preferred_element_type=F32)


def mml(m, v):
    m = m.astype(jnp.bfloat16)
    return dot(jnp.concatenate([m, m, m], axis=1), jnp.concatenate(parts_of(v), axis=0))


def mmr(v, m):
    m = m.astype(jnp.bfloat16)
    return dot(jnp.concatenate(parts_of(v), axis=1), jnp.concatenate([m, m, m], axis=0))


def iota(shape, dim):
    return lax.broadcasted_iota(jnp.int32, shape, dim)


def flat(v):
    return v.reshape(v.shape[0] * v.shape[1], v.shape[2])


def up(v, dim, step=1):
    return pltpu.roll(v, v.shape[dim] - step, dim)


def down(v, dim, step=1):
    return pltpu.roll(v, step, dim)


def planes_loop(lo, hi, group, fn):
    count = (hi - lo) // group
    if count > 1:
        def body(i, carry):
            fn(lo + i * group, group)
            return carry

        lax.fori_loop(0, count, body, 0)
    elif count == 1:
        fn(lo, group)
    rest = hi - lo - count * group
    if rest:
        fn(lo + count * group, rest)


def weights(lev, lo, hi, h, whole, group):
    K = lev["K"]
    rows, lanes = K.shape[1], K.shape[2]

    def one(p, g):
        n = g * rows
        k = flat(K[pl.ds(p, g)])
        kxu = flat(K[pl.ds(p + 1, g)])
        kxd = flat(K[pl.ds(p - 1, g)])
        kyu, kyd, kzu, kzd = up(k, 0), down(k, 0), up(k, 1), down(k, 1)
        if whole:
            row = iota((n, lanes), 0) & (rows - 1)
            lane = iota((n, lanes), 1)
            kyu = jnp.where(row == rows - 1, 0.0, kyu)
            kyd = jnp.where(row == 0, 0.0, kyd)
            kzu = jnp.where(lane == lanes - 1, 0.0, kzu)
            kzd = jnp.where(lane == 0, 0.0, kzd)
        wy, wz = h * (k + kyu), h * (k + kzu)
        diag = h * (6.0 * k + ((kxu + kxd) + (kyu + kyd) + (kzu + kzd)))
        if whole:
            wy = jnp.where(row == rows - 1, 0.0, wy)
            wz = jnp.where(lane == lanes - 1, 0.0, wz)
        shape = (g, rows, lanes)
        lev["WX"][pl.ds(p, g)] = (h * (k + kxu)).reshape(shape)
        lev["WY"][pl.ds(p, g)] = wy.reshape(shape)
        lev["WZ"][pl.ds(p, g)] = wz.reshape(shape)
        lev["DG"][pl.ds(p, g)] = diag.reshape(shape)
        lev["IV"][pl.ds(p, g)] = jnp.where(k > 0.0, 1.0 / diag, 0.0).reshape(shape)

    lev["WX"][lo - 1] = h * (K[lo - 1] + K[lo])
    planes_loop(lo, hi, group, one)


def sweep(lev, R, X, src, dst, lo, hi, a, b, group, first=False, want_dir=True, part=None,
          fold=False, out=None):
    Vi, Vo = lev[src], lev[dst]

    def one(p, g):
        v = [Vi[p - 1 + i] for i in range(g + 2)]
        wx = [lev["WX"][p - 1 + i] for i in range(g + 1)]
        for i in range(g):
            c = v[i + 1]
            wy, wz = lev["WY"][p + i], lev["WZ"][p + i]
            total = wx[i + 1] * v[i + 2] + wx[i] * v[i]
            total = total + (wy * up(c, 0) + down(wy * c, 0))
            total = total + (wz * up(c, 1) + down(wz * c, 1))
            r = R[p + i] - (lev["DG"][p + i] * c - total)
            if want_dir:
                d = b * (lev["IV"][p + i] * r)
                d = d + a * c if a else d
            step = c + d if fold else c
            own = step if part is None else step[part[0], part[1]]
            x = own if first else X[p + i] + own
            if out is None:
                X[p + i] = x
            else:
                out[p + i - lo] = x
            if not fold:
                R[p + i] = r
            if want_dir and not fold:
                Vo[p + i] = d

    planes_loop(lo, hi, group, one)


def presmooth(lev, R, X, halos, base, own, group, whole=False, part=None, after=None):
    h = 0 if whole else halos[0] + 1
    lo, hi = base - h, base + own + h

    def start(p, g):
        here = pl.ds(p, g)
        lev["Va"][here] = (lev["IV"][here] * R[here]) * (1.0 / THETA)

    planes_loop(lo, hi, group, start)
    names = ("Va", "Vb")
    for j in range(4):
        a, b = TABLE[j] if j < 3 else (0.0, 0.0)
        lo, hi = base - halos[j], base + own + halos[j]
        sweep(lev, R, X, names[j % 2], names[1 - j % 2], lo, hi, a, b, group,
              first=(j == 0), want_dir=(j < 3), part=part)
        if after:
            after(j)


def postsmooth(lev, R, X, halos, base, own, group, part=None, out=None):
    names = ("Va", "Vb")
    for j in range(4):
        a, b = TABLE[j - 1] if j > 0 else (0.0, 1.0 / THETA)
        lo, hi = base - halos[j], base + own + halos[j]
        sweep(lev, R, X, names[j % 2], names[1 - j % 2], lo, hi, a, b, group, part=part,
              fold=(j == 3), out=out if j == 3 else None)


def kernel(sizes, names, *refs):
    f_hbm, k_hbm, out_ref = refs[:3]
    S = dict(zip(names, refs[3:]))
    E0 = S["E0"]
    loads = [pltpu.make_async_copy(src, E0.at[i, pl.ds(H0, 16), pl.ds(8, 16)], S["ls"].at[i])
             for i, src in enumerate((f_hbm, k_hbm))]
    for c in loads:
        c.start()
    ss, rs = S["ss"], S["rs"]
    NGX, NGY, NGZ = sizes
    NYC = NGY // 2
    NX0, NY0, NZ0 = 16 * NGX, 16 * NGY, 128 * NGZ
    NX1, NY1, NZ1 = NX0 // 2, NY0 // 2, NZ0 // 2
    NX3 = 2 * NGX
    gx, gy, gz = lax.axis_index("gx"), lax.axis_index("gy"), lax.axis_index("gz")
    core, chip = gy % 2, gy // 2

    def at(dx=0, dy=0, dz=0):
        return ((gx + dx + NGX) % NGX, (gy + dy + NGY) % NGY, (gz + dz + NGZ) % NGZ)

    pair_peers = [(c, dz) for c in (0, 1) for dz in range(NGZ) if (c, dz) != (0, 0)]

    def pair_dev(c, dz):
        return (gx, chip * 2 + (core + c) % 2, (gz + dz) % NGZ)

    def chip_dev(dy, dx=0):
        return ((gx + dx + NGX) % NGX, ((chip + dy) % NYC) * 2 + core, gz)

    sides = [(dx, dy) for dx in (-1, 0, 1) for dy in (-1, 0, 1) if (dx, dy) != (0, 0)]

    barrier = pltpu.get_barrier_semaphore()
    greeted = [pair_dev(c, dz) for c, dz in pair_peers]
    greeted += [chip_dev(dy, dx) for dx in (-1, 0, 1) for dy in range(1, NYC)]
    greeted += [at(dx=dx, dy=dy) for dx, dy in sides]
    for dev in greeted:
        pl.semaphore_signal(barrier, inc=1, device_id=dev, device_id_type=MESH)

    def pass_on(i):
        for d in (2 ** i, -(2 ** i)):
            pl.semaphore_signal(S["dis"].at[i], inc=1, device_id=at(dx=d), device_id_type=MESH)

    def heard(i):
        pl.semaphore_wait(S["dis"].at[i], 2)

    counter = [0]

    def remote(src, dst, dev):
        i = counter[0]
        counter[0] += 1
        return pltpu.make_async_remote_copy(
            src_ref=src, dst_ref=dst, send_sem=ss.at[i], recv_sem=rs.at[i],
            device_id=dev, device_id_type=MESH,
        )

    def begin(copies):
        for c in copies:
            c.start()
        return copies

    def finish(copies):
        for c in copies:
            c.wait()

    def z_copies(buf, from_left, from_right):
        return [remote(buf, from_left, at(dz=1)), remote(buf, from_right, at(dz=-1))]

    def xy_copies(buf, base, own, h, rows):
        fields = slice(None)
        xs = {1: (base + own - h, base - h, h), -1: (base, base + own, h), 0: (base, base, own)}
        ys = {1: (rows, 0, 8), -1: (8, 8 + rows, 8), 0: (8, 8, rows)}
        out = []
        for dx, dy in sides:
            (sx, tx, nx), (sy, ty, ny) = xs[dx], ys[dy]
            out.append(remote(
                buf.at[fields, pl.ds(sx, nx), pl.ds(sy, ny)],
                buf.at[fields, pl.ds(tx, nx), pl.ds(ty, ny)],
                at(dx=dx, dy=dy)))
        return out

    def x_copies(buf, n1, n2):
        out = []
        for d, n in ((1, n1), (2, n2)):
            if n:
                fld = slice(None) if d == 1 else slice(0, 1)
                out.append(remote(buf.at[fld, pl.ds(11 - n, n)],
                                  buf.at[fld, pl.ds(7 - 4 * (d - 1) - n, n)], at(dx=d)))
                out.append(remote(buf.at[fld, pl.ds(7, n)],
                                  buf.at[fld, pl.ds(11 + 4 * (d - 1), n)], at(dx=-d)))
        return out

    def pair_copies(buf, slots):
        return [remote(buf, slots.at[i], pair_dev(c, dz)) for i, (c, dz) in enumerate(pair_peers)]

    column = [(dx, dy) for dx in (-1, 0, 1) for dy in range(NYC) if (dx, dy) != (0, 0)]

    def column_copies(buf):
        rows = pl.ds(pl.multiple_of(chip * 8, 8), 8)
        mine = buf.at[0, pl.ds(7, 4), rows]
        return [remote(mine, buf.at[0, pl.ds(7 - 4 * dx, 4), rows], chip_dev(dy, dx)) for dx, dy in column]

    lane16 = iota((16, 128), 1)
    lane8 = iota((8, 128), 1)

    def sel(shape, cond, value):
        return jnp.where(cond(iota(shape, 0), iota(shape, 1)), value, 0.0).astype(F32)

    def coarse_0(r):
        c = sel((64, 256), lambda r, c: ((c >> 5) == (r >> 3)) & (((c & 15) >> 1) == (r & 7)), 0.25)
        z = sel((128, 128), lambda l, c: (l >> 1) == (c & 63), 0.5)
        return mmr(mml(c, r), z)

    def coarse_1(r):
        c = sel((32, 64), lambda r, c: ((c >> 4) == (r >> 3)) & (((c & 7) >> 1) == (r & 7) - 4 * core), 0.25)
        z = sel((128, 128), lambda l, c: (l < 64) & (c == (l >> 1)), 0.5)
        t = mmr(mml(c, r), z)
        return (t[0:8] + pltpu.roll(t[8:16], 32, 1)) + (pltpu.roll(t[16:24], 64, 1) + pltpu.roll(t[24:32], 96, 1))

    def coarse_2(r):
        c = sel((32, 128), lambda r, c: ((c >> 6) == (r >> 4)) & (((c & 31) >> 1) == (r & 15)), 0.25)
        z = sel((128, 128), lambda l, c: (l >> 1) == (c & 63), 0.5)
        t = mmr(mml(c, r), z)
        return jnp.where(lane16 < 64, t[0:16], t[16:32])

    def coarse_3(r):
        n = r.shape[0]
        c = sel((n // 4, n), lambda r, c: ((c >> 5) == (r >> 3)) & (((c & 15) >> 1) == (r & 7)), 0.25)
        z = sel((128, 128), lambda l, c: (l < 64) & ((l >> 1) == c), 0.5)
        return mmr(mml(c, r), z)

    def fine_3(e):
        n = e.shape[0]
        u = sel((4 * n, n), lambda r, c: ((r >> 5) == (c >> 3)) & (((r & 15) >> 1) == (c & 7)), 1.0)
        z = sel((128, 128), lambda c, l: (l < 64) & ((l >> 1) == c), 1.0)
        return mml(u, mmr(e, z))

    def pack0(field):
        out = []
        for g in range(2):
            acc = None
            for j in range(8):
                t = pltpu.roll(field(8 * g + j), 16 * j + 8, 1)
                acc = t if acc is None else jnp.where((lane16 >> 4) == j, t, acc)
            out.append(acc)
        return out

    def merge0(from_left, from_right):
        return jnp.where((lane16 & 15) >= 8, from_right, from_left)

    def centre0(buf, fld, h, from_left, from_right):
        for g, m in ((0, h + 1), (1, h + 18)):
            buf[fld, m, 8:24] = merge0(from_left[fld, g], from_right[fld, g])

    def open0(fld, lo, hi, put):
        for x in range(lo, hi):
            g, j = (x + 8) // 8, x % 8
            put(x, E0[fld, H0 + x], pltpu.roll(M0[fld, g], (120 - 16 * j) % 128, 1))

    def unpack0(buf, fld, h, lo, hi, put):
        for x in range(lo, hi):
            if x < 0:
                main, m, j = x + h, h, x + 8
            elif x < 16:
                main, m, j = h + 2 + x, (h + 1 if x < 8 else h + 18), x % 8
            else:
                main, m, j = h + 20 + x - 16, h + 19, x - 16
            put(x, buf[fld, main], pltpu.roll(buf[fld, m], (120 - 16 * j) % 128, 1))

    def pack1(v):
        acc = None
        for j in range(8):
            t = v[8 * j:8 * j + 8]
            low = pltpu.roll(t, 8 * j, 1) if j else t
            high = pltpu.roll(t, 8 * j + 8, 1)
            acc = low if acc is None else jnp.where((lane8 >> 3) == j, low, acc)
            acc = jnp.where((lane8 >> 3) == 8 + j, high, acc)
        return acc

    def corner_copies(pack, from_left, from_right):
        out = []
        for dz, buf in ((1, from_left), (-1, from_right)):
            for dx in (-1, 0, 1):
                for dy in (-1, 0, 1):
                    out.append(remote(pack, buf.at[pl.ds(1 - dx, 1), pl.ds(8 - 8 * dy, 8)], at(dx, dy, dz)))
        return out

    def double1(v):
        n = v.shape[0]
        return jnp.where(iota((n, 128), 1) < 64, v, pltpu.roll(v, 64, 1))

    def centre1(buf, fld, own, left, right, i):
        lane = iota((64, 128), 1)
        t = jnp.where(lane < 64, flat(own[i]), jnp.where(lane < 96, flat(right[i]), flat(left[i])))
        buf[fld, 6:14, 8:16] = t.reshape(8, 8, 128)

    def inside(n_rows, n_lanes, row0, lane_of, ny, nz):
        y = iota((n_rows, n_lanes), 0) + row0
        z = lane_of(iota((n_rows, n_lanes), 1))
        return jnp.where((y >= 0) & (y < ny) & (z >= 0) & (z < nz), 1.0, 0.0).astype(F32)

    def xin(x, n):
        return jnp.where((x >= 0) & (x < n), 1.0, 0.0).astype(F32)

    L0 = {n: S[n + "0"] for n in ("K", "WX", "WY", "WZ", "DG", "IV", "Va", "Vb")}
    L1 = {n: S[n + "1"] for n in ("WX", "WY", "WZ", "DG", "IV", "Va", "Vb")}
    L1["K"] = S["K1"].at[0]
    L2 = {n: S[n + "2"] for n in ("WX", "WY", "WZ", "DG", "IV", "Va", "Vb")}
    L2["K"] = S["K2"].at[0]
    L3 = {n: S[n + "3"] for n in ("K", "WX", "WY", "WZ", "DG", "IV", "Va", "Vb")}
    R0, X0 = S["R0"], S["X0"]
    F1, X1 = S["F1"].at[0], S["X1"]
    F2, X2 = S["F2"].at[0], S["X2"]
    F3, X3 = S["F3"], S["X3"]

    for c in loads:
        c.wait()
    E0r, M0 = S["E0r"], S["M0"]
    for fld in (0, 1):
        for g, t in enumerate(pack0(lambda x: E0[fld, H0 + x, 8:24])):
            S["P0"][fld, g] = t
    pl.semaphore_wait(barrier, len(greeted))
    z0 = begin(z_copies(S["P0"], S["P0L"], S["P0R"]))
    xy0 = begin(xy_copies(E0, H0, 16, H0, 16))
    pass_on(0)
    finish(z0)
    for fld in (0, 1):
        for g in (0, 1):
            M0[fld, 1 + g, 8:24] = merge0(S["P0L"][fld, g], S["P0R"][fld, g])
    xy0 += begin(xy_copies(M0, 1, 2, 1, 16))

    k1 = coarse_0(E0[1, H0:H0 + 16, 8:24].reshape(256, 128))
    S["T1k"][0] = k1.reshape(8, 8, 128)
    S["B2k"][...] = coarse_1(k1)
    z1k = begin(z_copies(S["T1k"], S["T1kL"], S["T1kR"]))
    p2k = begin(pair_copies(S["B2k"], S["B2kS"]))
    heard(0)
    pass_on(1)

    def pair_rows(own, slots):
        blocks = [[] for _ in range(NGZ)]
        blocks[0].append(own[...])
        for i, (_, dz) in enumerate(pair_peers):
            blocks[dz].append(slots[i])
        rows = [jnp.zeros((8, 128), F32)] * 4
        for dz in range(NGZ):
            g = (gz - dz + NGZ) % NGZ
            t = pltpu.roll(sum(blocks[dz][1:], blocks[dz][0]), 32 * g, 1)
            here = (lane8 >> 5) == g
            for x in range(4):
                rows[x] = jnp.where(here, t if x == 0 else pltpu.roll(t, 128 - 32 * x, 1), rows[x])
        return rows

    def put_rows(buf, rows):
        for x in range(4):
            buf[0, 7 + x, my_rows] = rows[x]

    my_rows = pl.ds(pl.multiple_of(chip * 8, 8), 8)
    my_half = pl.ds(pl.multiple_of(core * 8, 8), 8)

    def gather_start(v, buf):
        S["C3"][...] = v
        buf[gx, my_half] = S["C3"][my_half]
        mine = buf.at[gx, my_half]
        return begin([remote(mine, mine, at(dx=d)) for d in range(1, NGX)])

    def swap_start(buf):
        mine = buf.at[:, my_half]
        return begin([remote(mine, mine, pair_dev(1, 0))])

    finish(z1k)
    centre1(S["K1"], 0, S["T1k"], S["T1kL"], S["T1kR"], 0)
    finish(p2k)
    put_rows(S["K2"], pair_rows(S["B2k"], S["B2kS"]))

    finish(xy0)
    xy1k = begin(xy_copies(S["K1"], 6, 8, H1K, 8))
    c2k = begin(column_copies(S["K2"]))
    heard(1)
    pass_on(2)

    def lane0(l):
        return 128 * gz + jnp.where(l < 192, l, l - 256)

    in0 = inside(32, 256, 16 * gy - 8, lane0, NY0, NZ0)

    def put_k(x, main, halo):
        w = xin(16 * gx + x, NX0)
        L0["K"][x + 5, :, 0:128] = main * (in0[:, 0:128] * w)
        L0["K"][x + 5, :, 128:256] = halo * (in0[:, 128:256] * w)

    def put_r(x, main, halo):
        R0[x + 5, :, 0:128] = main
        R0[x + 5, :, 128:256] = halo

    open0(1, -5, 21, put_k)
    open0(0, -4, 20, put_r)
    weights(L0, 1, 25, 0.5, False, 1)

    presmooth(L0, R0, X0, (3, 2, 1, 0), 5, 16, G0, part=OWN0)

    own0 = R0[5:21, 8:24, 0:128]
    f1 = coarse_0(own0.reshape(256, 128))
    S["F1"][0, 6:14, 8:16] = f1.reshape(8, 8, 128)
    S["P1"][0] = pack1(f1)
    xy1f = begin(xy_copies(S["F1"], 6, 8, H1F, 8) + corner_copies(S["P1"], S["Z1L"], S["Z1R"]))
    for g, t in enumerate(pack0(lambda x: R0[5 + x, 8:24, 0:128])):
        S["P0r"][0, g] = t
    E0r[0, H0R + 2:H0R + 18, 8:24] = own0
    finish(c2k)
    xx2k = begin(x_copies(S["K2"], 0, 3))
    finish(xy1k)

    def lane1(l):
        return 64 * gz + jnp.where(l < 96, l, l - 128)

    in1 = inside(24, 128, 8 * gy - 8, lane1, NY1, NZ1)
    for p in range(20):
        L1["K"][p] = L1["K"][p] * (in1 * xin(8 * gx + p - 6, NX1))
    weights(L1, 1, 19, 0.5 * 0.25, False, 2)

    z0r = begin(z_copies(S["P0r"], S["P0rL"], S["P0rR"]))
    finish(xy1f)
    edges = [jnp.where(iota((24, 128), 1) < 64, S["Z1R"][g], S["Z1L"][g]) for g in range(3)]
    lane24 = iota((24, 128), 1)
    for x in range(-H1F, 8 + H1F):
        g, j = (x + 8) // 8, x % 8
        right = pltpu.roll(edges[g], (64 - 8 * j) % 128, 1)
        left = pltpu.roll(edges[g], (56 - 8 * j) % 128, 1)
        F1[6 + x] = jnp.where(lane24 < 64, F1[6 + x], jnp.where(lane24 < 96, right, left))
    finish(z0r)
    centre0(E0r, 0, H0R, S["P0rL"], S["P0rR"])
    xy0r = begin(xy_copies(E0r, H0R + 1, 18, H0R + 1, 16))
    heard(2)
    g3k = gather_start(coarse_2(S["K2"][0, 7:11].reshape(128, 128)), S["G3k"])
    presmooth(L1, F1, X1, (3, 2, 1, 0), 6, 8, G1)

    r1 = F1[6:14, 8:16]
    S["B2f"][...] = coarse_1(r1.reshape(64, 128))
    p2f = begin(pair_copies(S["B2f"], S["B2fS"]))
    S["T1r"][0] = double1(r1.reshape(64, 128)).reshape(8, 8, 128)
    S["T1r"][1] = double1(X1[6:14, 8:16].reshape(64, 128)).reshape(8, 8, 128)
    z1r = begin(z_copies(S["T1r"], S["T1rL"], S["T1rR"]))

    finish(xx2k)
    for p in range(18):
        if p < 7 or p > 10:
            L2["K"][p] = L2["K"][p] * xin(4 * gx + p - 7, NX1 // 2)
    weights(L2, 1, 17, 0.5 * 0.25 ** 2, True, 2)

    finish(p2f)
    put_rows(S["F2"], pair_rows(S["B2f"], S["B2fS"]))
    c2f = begin(column_copies(S["F2"]))
    finish(z1r)
    for i in (0, 1):
        centre1(S["RX1"], i, S["T1r"], S["T1rL"], S["T1rR"], i)

    finish(c2f)
    presmooth(L2, F2, X2, (3, 2, 1, 0), 7, 4, G2)

    g3f = gather_start(coarse_2(F2[7:11].reshape(128, 128)), S["G3f"])
    S["RX2"][0, 7:11] = F2[7:11]
    S["RX2"][1, 7:11] = X2[7:11]

    finish(g3k)
    finish(swap_start(S["G3k"]))

    def unpack3(slots, dst):
        for s in range(NGX):
            t = slots[s]
            dst[5 + 2 * s] = jnp.where(lane16 < 64, t, 0.0)
            dst[6 + 2 * s] = jnp.where(lane16 < 64, pltpu.roll(t, 64, 1), 0.0)

    unpack3(S["G3k"], L3["K"])
    zero3 = jnp.zeros((5, 16, 128), F32)
    for ref in (L3["K"], L3["Va"], L3["Vb"], X3):
        ref[0:5] = zero3
        ref[5 + NX3:10 + NX3] = zero3
    weights(L3, 5, 5 + NX3, 0.5 * 0.25 ** 3, True, 4)


    def compact4(v):
        v = v.reshape(4, 32, 128)
        return (v[0] + pltpu.roll(v[1], 32, 1)) + (pltpu.roll(v[2], 64, 1) + pltpu.roll(v[3], 96, 1))

    def spread4(v):
        return jnp.concatenate([v] + [pltpu.roll(v, 128 - 32 * c, 1) for c in (1, 2, 3)], axis=0)

    h4 = 0.5 * 0.25 ** 4
    k4 = coarse_3(L3["K"][5:5 + NX3].reshape(16 * NX3, 128))
    k4 = compact4(k4)
    row4, lane4 = iota((32, 128), 0), iota((32, 128), 1)
    x_first, x_last = (row4 < 8) & (lane4 < 32), (row4 >= 24) & (lane4 >= 96)
    y_first, y_last = (row4 & 7) == 0, (row4 & 7) == 7
    z_first, z_last = (lane4 & 31) == 0, (lane4 & 31) == 31

    def xup(v):
        return jnp.concatenate([v[8:32], pltpu.roll(v[0:8], 96, 1)], axis=0)

    def xdown(v):
        return jnp.concatenate([pltpu.roll(v[24:32], 32, 1), v[0:24]], axis=0)

    k4xu, k4xd = jnp.where(x_last, 0.0, xup(k4)), jnp.where(x_first, 0.0, xdown(k4))
    k4yu, k4yd = jnp.where(y_last, 0.0, up(k4, 0)), jnp.where(y_first, 0.0, down(k4, 0))
    k4zu, k4zd = jnp.where(z_last, 0.0, up(k4, 1)), jnp.where(z_first, 0.0, down(k4, 1))
    wx4 = jnp.where(x_last, 0.0, h4 * (k4 + k4xu))
    wy4 = jnp.where(y_last, 0.0, h4 * (k4 + k4yu))
    wz4 = jnp.where(z_last, 0.0, h4 * (k4 + k4zu))
    dg4 = h4 * (6.0 * k4 + ((k4xu + k4xd) + (k4yu + k4yd) + (k4zu + k4zd)))

    finish(g3f)
    xx2r = begin(x_copies(S["RX2"], 4, 2))
    xy1r = begin(xy_copies(S["RX1"], 6, 8, H1R, 8))
    finish(swap_start(S["G3f"]))
    unpack3(S["G3f"], F3)
    presmooth(L3, F3, X3, (0, 0, 0, 0), 5, NX3, G3, whole=True)

    f4 = coarse_3(F3[5:5 + NX3].reshape(16 * NX3, 128))
    f4 = compact4(f4)
    x4 = jnp.zeros_like(f4)
    r4 = p4 = f4

    def total4(v):
        t = (v[0:8] + v[8:16]) + (v[16:24] + v[24:32])
        t = jnp.broadcast_to(jnp.sum(t, axis=1, keepdims=True), (8, 128))
        for step in (4, 2, 1):
            t = t + pltpu.roll(t, step, 0)
        return t

    def times4(c, v):
        return (c[None] * v.reshape(4, 8, 128)).reshape(32, 128)

    rr = total4(r4 * r4)
    for _ in range(CG_ITERS):
        q4 = dg4 * p4 - (
            (wx4 * xup(p4) + xdown(wx4 * p4))
            + (wy4 * up(p4, 0) + down(wy4 * p4, 0))
            + (wz4 * up(p4, 1) + down(wz4 * p4, 1)))
        alpha = rr / total4(p4 * q4)
        x4 = x4 + times4(alpha, p4)
        r4 = r4 - times4(alpha, q4)
        rn = total4(r4 * r4)
        p4 = r4 + times4(rn / rr, p4)
        rr = rn

    L3["Va"][5:5 + NX3] = fine_3(spread4(x4)).reshape(NX3, 16, 128)
    postsmooth(L3, F3, X3, (0, 0, 0, 0), 5, NX3, G3)

    finish(xx2r)
    z3 = sel((128, 128), lambda c, l: (l >> 1) == c, 1.0)
    y3 = sel((32, 16), lambda r, c: (r >> 1) == c, 1.0)
    t = mmr(X3[pl.ds(2 * gx + 1, 10)].reshape(160, 128), z3)
    for q in range(10):
        e = mml(y3, t[16 * q:16 * q + 16])
        for p in (2 * q - 1, 2 * q):
            if 0 <= p < 18:
                L2["Va"][p] = e
    R2b, X2b = S["RX2"].at[0], S["RX2"].at[1]
    postsmooth(L2, R2b, X2b, (6, 5, 4, 3), 7, 4, G2)

    finish(xy1r)
    z2 = sel((128, 128), lambda c, l: ((lane1(l) >> 1) == c) & (lane1(l) >= 0) & (lane1(l) < NZ1), 1.0)

    def yrow(r):
        return 8 * gy + r - 8

    y2 = sel((24, 32), lambda r, c: ((yrow(r) >> 1) == c) & (yrow(r) >= 0) & (yrow(r) < NY1), 1.0)
    t = mmr(X2b[4:14].reshape(320, 128), z2)
    for q in range(10):
        e = mml(y2, t[32 * q:32 * q + 32])
        e = e * xin(4 * gx + q - 3, NX1 // 2)
        L1["Va"][2 * q] = e
        L1["Va"][2 * q + 1] = e
    R1b, X1b = S["RX1"].at[0], S["RX1"].at[1]
    postsmooth(L1, R1b, X1b, (5, 4, 3, 2), 6, 8, G1)

    finish(xy0r)
    unpack0(E0r, 0, H0R, -3, 19, put_r)

    def zfine(c, l):
        z = jnp.where(l < 192, l, l - 256)
        g = 128 * gz + z
        return (((z >> 1) & 127) == c) & (g >= 0) & (g < NZ0)

    def yfine(r, c):
        g = 16 * gy + r - 8
        return (((r - 8) >> 1) + 8 == c) & (g >= 0) & (g < NY0)

    z1 = sel((128, 256), zfine, 1.0)
    y1 = sel((32, 24), yfine, 1.0)
    t = mmr(X1b[4:16].reshape(288, 128), z1)
    for q in range(12):
        e = mml(y1, t[24 * q:24 * q + 24])
        e = e * xin(8 * gx + q - 2, NX1)
        L0["Va"][1 + 2 * q] = e
        L0["Va"][2 + 2 * q] = e
    postsmooth(L0, R0, X0, (3, 2, 1, 0), 5, 16, G0, part=OWN0, out=out_ref)


def scratch(sizes):
    ngx, ngy, ngz = sizes
    n_pair = 2 * ngz - 1
    shapes = {
        "C3": (16, 128), "M0": (2, 4, 32, 128),
        "P1": (1, 8, 128), "Z1L": (3, 24, 128), "Z1R": (3, 24, 128),
        "P0": (2, 2, 16, 128), "P0L": (2, 2, 16, 128), "P0R": (2, 2, 16, 128),
        "E0": (2, 16 + 2 * H0, 32, 128),
        "P0r": (1, 2, 16, 128), "P0rL": (1, 2, 16, 128), "P0rR": (1, 2, 16, 128),
        "E0r": (1, 18 + 2 * (H0R + 1), 32, 128),
        "R0": (26, 32, 256), "X0": (26, 16, 128), "K0": (26, 32, 256),
        "T1r": (2, 8, 8, 128), "T1rL": (2, 8, 8, 128), "T1rR": (2, 8, 8, 128),
        "K1": (1, 20, 24, 128), "F1": (1, 20, 24, 128), "RX1": (2, 20, 24, 128), "X1": (20, 24, 128),
        "K2": (1, 18, 32, 128), "F2": (1, 18, 32, 128), "RX2": (2, 18, 32, 128), "X2": (18, 32, 128),
        "B2k": (8, 128), "B2kS": (n_pair, 8, 128),
        "B2f": (8, 128), "B2fS": (n_pair, 8, 128),
        "G3k": (ngx, 16, 128), "G3f": (ngx, 16, 128),
        "K3": (2 * ngx + 10, 16, 128), "F3": (2 * ngx + 10, 16, 128), "X3": (2 * ngx + 10, 16, 128),
    }
    for n in ("T1k", "T1f"):
        for side in ("", "L", "R"):
            shapes[n + side] = (1, 8, 8, 128)
    for n in ("WX", "WY", "WZ", "DG", "IV", "Va", "Vb"):
        shapes[n + "0"] = (26, 32, 256)
        shapes[n + "1"] = (20, 24, 128)
        shapes[n + "2"] = (18, 32, 128)
        shapes[n + "3"] = (2 * ngx + 10, 16, 128)
    names = list(shapes) + ["ss", "rs", "ls", "dis"]
    n_sem = 74 + 2 * (n_pair + 3 * (ngy // 2) - 1) + 2 + 4 + 2 * ngx
    kinds = [pltpu.VMEM(shapes[n], F32) for n in shapes]
    kinds += [pltpu.SemaphoreType.DMA((n_sem,)), pltpu.SemaphoreType.DMA((n_sem,))]
    kinds += [pltpu.SemaphoreType.DMA((2,)), pltpu.SemaphoreType.REGULAR((3,))]
    return names, kinds


def solution(mesh):
    sizes = (mesh.shape["gx"], mesh.shape["gy"], mesh.shape["gz"])
    names, kinds = scratch(sizes)
    spec = P("gx", "gy", "gz")

    def local(right_side, conductivity):
        return pl.pallas_call(
            functools.partial(kernel, sizes, names),
            out_shape=jax.ShapeDtypeStruct(right_side.shape, F32),
            in_specs=[pl.BlockSpec(memory_space=pl.ANY)] * 2,
            out_specs=pl.BlockSpec(memory_space=pltpu.VMEM),
            scratch_shapes=kinds,
            compiler_params=pltpu.CompilerParams(
                collective_id=0, has_side_effects=True, vmem_limit_bytes=57 * 1024 * 1024
            ),
        )(right_side, conductivity)

    return jax.shard_map(local, mesh=mesh, in_specs=(spec, spec), out_specs=spec, check_vma=False)
```

```python
import functools

import jax
import jax.numpy as jnp
from jax import lax
from jax.experimental import pallas as pl
from jax.experimental.pallas import tpu as pltpu
from jax.sharding import PartitionSpec as P

F32 = jnp.float32
MESH = pl.DeviceIdType.MESH
CG_ITERS = 8
THETA = 1.125
DELTA = 0.875

H0, H0R = 5, 3
H1K, H1F, H1R = 6, 4, 5

G0, G1, G2, G3 = 10, 20, 20, 32
OWN0 = (slice(8, 24), slice(0, 128))


def cheb_table():
    sigma = THETA / DELTA
    rho_now = 1.0 / sigma
    table = []
    for _ in range(3):
        rho_next = 1.0 / (2.0 * sigma - rho_now)
        table.append((rho_next * rho_now, 2.0 * rho_next / DELTA))
        rho_now = rho_next
    return table


TABLE = cheb_table()


def parts_of(v):
    high = v.astype(jnp.bfloat16)
    rest = v - high.astype(F32)
    mid = rest.astype(jnp.bfloat16)
    return high, mid, (rest - mid.astype(F32)).astype(jnp.bfloat16)


def dot(a, b):
    return jnp.dot(a, b, preferred_element_type=F32)


def mml(m, v):
    m = m.astype(jnp.bfloat16)
    return dot(jnp.concatenate([m, m, m], axis=1), jnp.concatenate(parts_of(v), axis=0))


def mmr(v, m):
    m = m.astype(jnp.bfloat16)
    return dot(jnp.concatenate(parts_of(v), axis=1), jnp.concatenate([m, m, m], axis=0))


def iota(shape, dim):
    return lax.broadcasted_iota(jnp.int32, shape, dim)


def flat(v):
    return v.reshape(v.shape[0] * v.shape[1], v.shape[2])


def up(v, dim, step=1):
    return pltpu.roll(v, v.shape[dim] - step, dim)


def down(v, dim, step=1):
    return pltpu.roll(v, step, dim)


def planes_loop(lo, hi, group, fn):
    count = (hi - lo) // group
    if count > 1:
        def body(i, carry):
            fn(lo + i * group, group)
            return carry

        lax.fori_loop(0, count, body, 0)
    elif count == 1:
        fn(lo, group)
    rest = hi - lo - count * group
    if rest:
        fn(lo + count * group, rest)


def weights(lev, lo, hi, h, whole, group):
    K = lev["K"]
    rows, lanes = K.shape[1], K.shape[2]

    def one(p, g):
        n = g * rows
        k = flat(K[pl.ds(p, g)])
        kxu = flat(K[pl.ds(p + 1, g)])
        kxd = flat(K[pl.ds(p - 1, g)])
        kyu, kyd, kzu, kzd = up(k, 0), down(k, 0), up(k, 1), down(k, 1)
        if whole:
            row = iota((n, lanes), 0) & (rows - 1)
            lane = iota((n, lanes), 1)
            kyu = jnp.where(row == rows - 1, 0.0, kyu)
            kyd = jnp.where(row == 0, 0.0, kyd)
            kzu = jnp.where(lane == lanes - 1, 0.0, kzu)
            kzd = jnp.where(lane == 0, 0.0, kzd)
        wy, wz = h * (k + kyu), h * (k + kzu)
        diag = h * (6.0 * k + ((kxu + kxd) + (kyu + kyd) + (kzu + kzd)))
        if whole:
            wy = jnp.where(row == rows - 1, 0.0, wy)
            wz = jnp.where(lane == lanes - 1, 0.0, wz)
        shape = (g, rows, lanes)
        lev["WX"][pl.ds(p, g)] = (h * (k + kxu)).reshape(shape)
        lev["WY"][pl.ds(p, g)] = wy.reshape(shape)
        lev["WZ"][pl.ds(p, g)] = wz.reshape(shape)
        lev["DG"][pl.ds(p, g)] = diag.reshape(shape)
        lev["IV"][pl.ds(p, g)] = jnp.where(k > 0.0, 1.0 / diag, 0.0).reshape(shape)

    lev["WX"][lo - 1] = h * (K[lo - 1] + K[lo])
    planes_loop(lo, hi, group, one)


def sweep(lev, R, X, src, dst, lo, hi, a, b, group, first=False, want_dir=True, part=None,
          fold=False, out=None):
    Vi, Vo = lev[src], lev[dst]

    def one(p, g):
        v = [Vi[p - 1 + i] for i in range(g + 2)]
        wx = [lev["WX"][p - 1 + i] for i in range(g + 1)]
        for i in range(g):
            c = v[i + 1]
            wy, wz = lev["WY"][p + i], lev["WZ"][p + i]
            total = wx[i + 1] * v[i + 2] + wx[i] * v[i]
            total = total + (wy * up(c, 0) + down(wy * c, 0))
            total = total + (wz * up(c, 1) + down(wz * c, 1))
            r = R[p + i] - (lev["DG"][p + i] * c - total)
            if want_dir:
                d = b * (lev["IV"][p + i] * r)
                d = d + a * c if a else d
            step = c + d if fold else c
            own = step if part is None else step[part[0], part[1]]
            x = own if first else X[p + i] + own
            if out is None:
                X[p + i] = x
            else:
                out[p + i - lo] = x
            if not fold:
                R[p + i] = r
            if want_dir and not fold:
                Vo[p + i] = d

    planes_loop(lo, hi, group, one)


def presmooth(lev, R, X, halos, base, own, group, whole=False, part=None, after=None):
    h = 0 if whole else halos[0] + 1
    lo, hi = base - h, base + own + h

    def start(p, g):
        here = pl.ds(p, g)
        lev["Va"][here] = (lev["IV"][here] * R[here]) * (1.0 / THETA)

    planes_loop(lo, hi, group, start)
    names = ("Va", "Vb")
    for j in range(4):
        a, b = TABLE[j] if j < 3 else (0.0, 0.0)
        lo, hi = base - halos[j], base + own + halos[j]
        sweep(lev, R, X, names[j % 2], names[1 - j % 2], lo, hi, a, b, group,
              first=(j == 0), want_dir=(j < 3), part=part)
        if after:
            after(j)


def postsmooth(lev, R, X, halos, base, own, group, part=None, out=None):
    names = ("Va", "Vb")
    for j in range(4):
        a, b = TABLE[j - 1] if j > 0 else (0.0, 1.0 / THETA)
        lo, hi = base - halos[j], base + own + halos[j]
        sweep(lev, R, X, names[j % 2], names[1 - j % 2], lo, hi, a, b, group, part=part,
              fold=(j == 3), out=out if j == 3 else None)


def kernel(sizes, names, *refs):
    f_hbm, k_hbm, out_ref = refs[:3]
    S = dict(zip(names, refs[3:]))
    E0 = S["E0"]
    loads = [pltpu.make_async_copy(src, E0.at[i, pl.ds(H0, 16), pl.ds(8, 16)], S["ls"].at[i])
             for i, src in enumerate((f_hbm, k_hbm))]
    for c in loads:
        c.start()
    ss, rs = S["ss"], S["rs"]
    NGX, NGY, NGZ = sizes
    NYC = NGY // 2
    NX0, NY0, NZ0 = 16 * NGX, 16 * NGY, 128 * NGZ
    NX1, NY1, NZ1 = NX0 // 2, NY0 // 2, NZ0 // 2
    NX3 = 2 * NGX
    gx, gy, gz = lax.axis_index("gx"), lax.axis_index("gy"), lax.axis_index("gz")
    core, chip = gy % 2, gy // 2

    def at(dx=0, dy=0, dz=0):
        return ((gx + dx + NGX) % NGX, (gy + dy + NGY) % NGY, (gz + dz + NGZ) % NGZ)

    pair_peers = [(c, dz) for c in (0, 1) for dz in range(NGZ) if (c, dz) != (0, 0)]

    def pair_dev(c, dz):
        return (gx, chip * 2 + (core + c) % 2, (gz + dz) % NGZ)

    def chip_dev(dy, dx=0):
        return ((gx + dx + NGX) % NGX, ((chip + dy) % NYC) * 2 + core, gz)

    sides = [(dx, dy) for dx in (-1, 0, 1) for dy in (-1, 0, 1) if (dx, dy) != (0, 0)]

    barrier = pltpu.get_barrier_semaphore()
    greeted = [pair_dev(c, dz) for c, dz in pair_peers]
    greeted += [chip_dev(dy, dx) for dx in (-1, 0, 1) for dy in range(1, NYC)]
    greeted += [at(dx=dx, dy=dy) for dx, dy in sides]
    for dev in greeted:
        pl.semaphore_signal(barrier, inc=1, device_id=dev, device_id_type=MESH)

    def pass_on(i):
        for d in (2 ** i, -(2 ** i)):
            pl.semaphore_signal(S["dis"].at[i], inc=1, device_id=at(dx=d), device_id_type=MESH)

    def heard(i):
        pl.semaphore_wait(S["dis"].at[i], 2)

    counter = [0]

    def remote(src, dst, dev):
        i = counter[0]
        counter[0] += 1
        return pltpu.make_async_remote_copy(
            src_ref=src, dst_ref=dst, send_sem=ss.at[i], recv_sem=rs.at[i],
            device_id=dev, device_id_type=MESH,
        )

    def begin(copies):
        for c in copies:
            c.start()
        return copies

    def finish(copies):
        for c in copies:
            c.wait()

    def z_copies(buf, from_left, from_right):
        return [remote(buf, from_left, at(dz=1)), remote(buf, from_right, at(dz=-1))]

    def xy_copies(buf, base, own, h, rows):
        fields = slice(None)
        xs = {1: (base + own - h, base - h, h), -1: (base, base + own, h), 0: (base, base, own)}
        ys = {1: (rows, 0, 8), -1: (8, 8 + rows, 8), 0: (8, 8, rows)}
        out = []
        for dx, dy in sides:
            (sx, tx, nx), (sy, ty, ny) = xs[dx], ys[dy]
            out.append(remote(
                buf.at[fields, pl.ds(sx, nx), pl.ds(sy, ny)],
                buf.at[fields, pl.ds(tx, nx), pl.ds(ty, ny)],
                at(dx=dx, dy=dy)))
        return out

    def x_copies(buf, n1, n2):
        out = []
        for d, n in ((1, n1), (2, n2)):
            if n:
                fld = slice(None) if d == 1 else slice(0, 1)
                out.append(remote(buf.at[fld, pl.ds(11 - n, n)],
                                  buf.at[fld, pl.ds(7 - 4 * (d - 1) - n, n)], at(dx=d)))
                out.append(remote(buf.at[fld, pl.ds(7, n)],
                                  buf.at[fld, pl.ds(11 + 4 * (d - 1), n)], at(dx=-d)))
        return out

    def pair_copies(buf, slots):
        return [remote(buf, slots.at[i], pair_dev(c, dz)) for i, (c, dz) in enumerate(pair_peers)]

    column = [(dx, dy) for dx in (-1, 0, 1) for dy in range(NYC) if (dx, dy) != (0, 0)]

    def column_copies(buf):
        rows = pl.ds(pl.multiple_of(chip * 8, 8), 8)
        mine = buf.at[0, pl.ds(7, 4), rows]
        return [remote(mine, buf.at[0, pl.ds(7 - 4 * dx, 4), rows], chip_dev(dy, dx)) for dx, dy in column]

    lane16 = iota((16, 128), 1)
    lane8 = iota((8, 128), 1)

    def sel(shape, cond, value):
        return jnp.where(cond(iota(shape, 0), iota(shape, 1)), value, 0.0).astype(F32)

    def coarse_0(r):
        c = sel((64, 256), lambda r, c: ((c >> 5) == (r >> 3)) & (((c & 15) >> 1) == (r & 7)), 0.25)
        z = sel((128, 128), lambda l, c: (l >> 1) == (c & 63), 0.5)
        return mmr(mml(c, r), z)

    def coarse_1(r):
        c = sel((32, 64), lambda r, c: ((c >> 4) == (r >> 3)) & (((c & 7) >> 1) == (r & 7) - 4 * core), 0.25)
        z = sel((128, 128), lambda l, c: (l < 64) & (c == (l >> 1)), 0.5)
        t = mmr(mml(c, r), z)
        return (t[0:8] + pltpu.roll(t[8:16], 32, 1)) + (pltpu.roll(t[16:24], 64, 1) + pltpu.roll(t[24:32], 96, 1))

    def coarse_2(r):
        c = sel((32, 128), lambda r, c: ((c >> 6) == (r >> 4)) & (((c & 31) >> 1) == (r & 15)), 0.25)
        z = sel((128, 128), lambda l, c: (l >> 1) == (c & 63), 0.5)
        t = mmr(mml(c, r), z)
        return jnp.where(lane16 < 64, t[0:16], t[16:32])

    def coarse_3(r):
        n = r.shape[0]
        c = sel((n // 4, n), lambda r, c: ((c >> 5) == (r >> 3)) & (((c & 15) >> 1) == (r & 7)), 0.25)
        z = sel((128, 128), lambda l, c: (l < 64) & ((l >> 1) == c), 0.5)
        return mmr(mml(c, r), z)

    def fine_3(e):
        n = e.shape[0]
        u = sel((4 * n, n), lambda r, c: ((r >> 5) == (c >> 3)) & (((r & 15) >> 1) == (c & 7)), 1.0)
        z = sel((128, 128), lambda c, l: (l < 64) & ((l >> 1) == c), 1.0)
        return mml(u, mmr(e, z))

    def pack0(field):
        out = []
        for g in range(2):
            acc = None
            for j in range(8):
                t = pltpu.roll(field(8 * g + j), 16 * j + 8, 1)
                acc = t if acc is None else jnp.where((lane16 >> 4) == j, t, acc)
            out.append(acc)
        return out

    def merge0(from_left, from_right):
        return jnp.where((lane16 & 15) >= 8, from_right, from_left)

    def centre0(buf, fld, h, from_left, from_right):
        for g, m in ((0, h + 1), (1, h + 18)):
            buf[fld, m, 8:24] = merge0(from_left[fld, g], from_right[fld, g])

    def open0(fld, lo, hi, put):
        for x in range(lo, hi):
            g, j = (x + 8) // 8, x % 8
            put(x, E0[fld, H0 + x], pltpu.roll(M0[fld, g], (120 - 16 * j) % 128, 1))

    def unpack0(buf, fld, h, lo, hi, put):
        for x in range(lo, hi):
            if x < 0:
                main, m, j = x + h, h, x + 8
            elif x < 16:
                main, m, j = h + 2 + x, (h + 1 if x < 8 else h + 18), x % 8
            else:
                main, m, j = h + 20 + x - 16, h + 19, x - 16
            put(x, buf[fld, main], pltpu.roll(buf[fld, m], (120 - 16 * j) % 128, 1))

    def pack1(v):
        acc = None
        for j in range(8):
            t = v[8 * j:8 * j + 8]
            low = pltpu.roll(t, 8 * j, 1) if j else t
            high = pltpu.roll(t, 8 * j + 8, 1)
            acc = low if acc is None else jnp.where((lane8 >> 3) == j, low, acc)
            acc = jnp.where((lane8 >> 3) == 8 + j, high, acc)
        return acc

    def corner_copies(pack, from_left, from_right):
        out = []
        for dz, buf in ((1, from_left), (-1, from_right)):
            for dx in (-1, 0, 1):
                for dy in (-1, 0, 1):
                    out.append(remote(pack, buf.at[pl.ds(1 - dx, 1), pl.ds(8 - 8 * dy, 8)], at(dx, dy, dz)))
        return out

    def double1(v):
        n = v.shape[0]
        return jnp.where(iota((n, 128), 1) < 64, v, pltpu.roll(v, 64, 1))

    def centre1(buf, fld, own, left, right, i):
        lane = iota((64, 128), 1)
        t = jnp.where(lane < 64, flat(own[i]), jnp.where(lane < 96, flat(right[i]), flat(left[i])))
        buf[fld, 6:14, 8:16] = t.reshape(8, 8, 128)

    def inside(n_rows, n_lanes, row0, lane_of, ny, nz):
        y = iota((n_rows, n_lanes), 0) + row0
        z = lane_of(iota((n_rows, n_lanes), 1))
        return jnp.where((y >= 0) & (y < ny) & (z >= 0) & (z < nz), 1.0, 0.0).astype(F32)

    def xin(x, n):
        return jnp.where((x >= 0) & (x < n), 1.0, 0.0).astype(F32)

    L0 = {n: S[n + "0"] for n in ("K", "WX", "WY", "WZ", "DG", "IV", "Va", "Vb")}
    L1 = {n: S[n + "1"] for n in ("WX", "WY", "WZ", "DG", "IV", "Va", "Vb")}
    L1["K"] = S["K1"].at[0]
    L2 = {n: S[n + "2"] for n in ("WX", "WY", "WZ", "DG", "IV", "Va", "Vb")}
    L2["K"] = S["K2"].at[0]
    L3 = {n: S[n + "3"] for n in ("K", "WX", "WY", "WZ", "DG", "IV", "Va", "Vb")}
    R0, X0 = S["R0"], S["X0"]
    F1, X1 = S["F1"].at[0], S["X1"]
    F2, X2 = S["F2"].at[0], S["X2"]
    F3, X3 = S["F3"], S["X3"]

    for c in loads:
        c.wait()
    E0r, M0 = S["E0r"], S["M0"]
    for fld in (0, 1):
        for g, t in enumerate(pack0(lambda x: E0[fld, H0 + x, 8:24])):
            S["P0"][fld, g] = t
    pl.semaphore_wait(barrier, len(greeted))
    z0 = begin(z_copies(S["P0"], S["P0L"], S["P0R"]))
    xy0 = begin(xy_copies(E0, H0, 16, H0, 16))
    pass_on(0)
    finish(z0)
    for fld in (0, 1):
        for g in (0, 1):
            M0[fld, 1 + g, 8:24] = merge0(S["P0L"][fld, g], S["P0R"][fld, g])
    xy0 += begin(xy_copies(M0, 1, 2, 1, 16))

    k1 = coarse_0(E0[1, H0:H0 + 16, 8:24].reshape(256, 128))
    S["T1k"][0] = k1.reshape(8, 8, 128)
    S["B2k"][...] = coarse_1(k1)
    z1k = begin(z_copies(S["T1k"], S["T1kL"], S["T1kR"]))
    p2k = begin(pair_copies(S["B2k"], S["B2kS"]))
    heard(0)
    pass_on(1)

    def pair_rows(own, slots):
        blocks = [[] for _ in range(NGZ)]
        blocks[0].append(own[...])
        for i, (_, dz) in enumerate(pair_peers):
            blocks[dz].append(slots[i])
        rows = [jnp.zeros((8, 128), F32)] * 4
        for dz in range(NGZ):
            g = (gz - dz + NGZ) % NGZ
            t = pltpu.roll(sum(blocks[dz][1:], blocks[dz][0]), 32 * g, 1)
            here = (lane8 >> 5) == g
            for x in range(4):
                rows[x] = jnp.where(here, t if x == 0 else pltpu.roll(t, 128 - 32 * x, 1), rows[x])
        return rows

    def put_rows(buf, rows):
        for x in range(4):
            buf[0, 7 + x, my_rows] = rows[x]

    my_rows = pl.ds(pl.multiple_of(chip * 8, 8), 8)
    my_half = pl.ds(pl.multiple_of(core * 8, 8), 8)

    def gather_start(v, buf):
        S["C3"][...] = v
        buf[gx, my_half] = S["C3"][my_half]
        mine = buf.at[gx, my_half]
        return begin([remote(mine, mine, at(dx=d)) for d in range(1, NGX)])

    def swap_start(buf):
        mine = buf.at[:, my_half]
        return begin([remote(mine, mine, pair_dev(1, 0))])

    finish(z1k)
    centre1(S["K1"], 0, S["T1k"], S["T1kL"], S["T1kR"], 0)
    finish(p2k)
    put_rows(S["K2"], pair_rows(S["B2k"], S["B2kS"]))

    finish(xy0)
    xy1k = begin(xy_copies(S["K1"], 6, 8, H1K, 8))
    c2k = begin(column_copies(S["K2"]))
    heard(1)
    pass_on(2)

    def lane0(l):
        return 128 * gz + jnp.where(l < 192, l, l - 256)

    in0 = inside(32, 256, 16 * gy - 8, lane0, NY0, NZ0)

    def put_k(x, main, halo):
        w = xin(16 * gx + x, NX0)
        L0["K"][x + 5, :, 0:128] = main * (in0[:, 0:128] * w)
        L0["K"][x + 5, :, 128:256] = halo * (in0[:, 128:256] * w)

    def put_r(x, main, halo):
        R0[x + 5, :, 0:128] = main
        R0[x + 5, :, 128:256] = halo

    open0(1, -5, 21, put_k)
    open0(0, -4, 20, put_r)
    weights(L0, 1, 25, 0.5, False, 1)

    presmooth(L0, R0, X0, (3, 2, 1, 0), 5, 16, G0, part=OWN0)

    own0 = R0[5:21, 8:24, 0:128]
    f1 = coarse_0(own0.reshape(256, 128))
    S["F1"][0, 6:14, 8:16] = f1.reshape(8, 8, 128)
    S["P1"][0] = pack1(f1)
    xy1f = begin(xy_copies(S["F1"], 6, 8, H1F, 8) + corner_copies(S["P1"], S["Z1L"], S["Z1R"]))
    for g, t in enumerate(pack0(lambda x: R0[5 + x, 8:24, 0:128])):
        S["P0r"][0, g] = t
    E0r[0, H0R + 2:H0R + 18, 8:24] = own0
    finish(c2k)
    xx2k = begin(x_copies(S["K2"], 0, 3))
    finish(xy1k)

    def lane1(l):
        return 64 * gz + jnp.where(l < 96, l, l - 128)

    in1 = inside(24, 128, 8 * gy - 8, lane1, NY1, NZ1)
    for p in range(20):
        L1["K"][p] = L1["K"][p] * (in1 * xin(8 * gx + p - 6, NX1))
    weights(L1, 1, 19, 0.5 * 0.25, False, 2)

    z0r = begin(z_copies(S["P0r"], S["P0rL"], S["P0rR"]))
    finish(xy1f)
    edges = [jnp.where(iota((24, 128), 1) < 64, S["Z1R"][g], S["Z1L"][g]) for g in range(3)]
    lane24 = iota((24, 128), 1)
    for x in range(-H1F, 8 + H1F):
        g, j = (x + 8) // 8, x % 8
        right = pltpu.roll(edges[g], (64 - 8 * j) % 128, 1)
        left = pltpu.roll(edges[g], (56 - 8 * j) % 128, 1)
        F1[6 + x] = jnp.where(lane24 < 64, F1[6 + x], jnp.where(lane24 < 96, right, left))
    finish(z0r)
    centre0(E0r, 0, H0R, S["P0rL"], S["P0rR"])
    xy0r = begin(xy_copies(E0r, H0R + 1, 18, H0R + 1, 16))
    heard(2)
    g3k = gather_start(coarse_2(S["K2"][0, 7:11].reshape(128, 128)), S["G3k"])
    presmooth(L1, F1, X1, (3, 2, 1, 0), 6, 8, G1)

    r1 = F1[6:14, 8:16]
    S["B2f"][...] = coarse_1(r1.reshape(64, 128))
    p2f = begin(pair_copies(S["B2f"], S["B2fS"]))
    S["T1r"][0] = double1(r1.reshape(64, 128)).reshape(8, 8, 128)
    S["T1r"][1] = double1(X1[6:14, 8:16].reshape(64, 128)).reshape(8, 8, 128)
    z1r = begin(z_copies(S["T1r"], S["T1rL"], S["T1rR"]))

    finish(xx2k)
    for p in range(18):
        if p < 7 or p > 10:
            L2["K"][p] = L2["K"][p] * xin(4 * gx + p - 7, NX1 // 2)
    weights(L2, 1, 17, 0.5 * 0.25 ** 2, True, 2)

    finish(p2f)
    put_rows(S["F2"], pair_rows(S["B2f"], S["B2fS"]))
    c2f = begin(column_copies(S["F2"]))
    finish(z1r)
    for i in (0, 1):
        centre1(S["RX1"], i, S["T1r"], S["T1rL"], S["T1rR"], i)

    finish(c2f)
    presmooth(L2, F2, X2, (3, 2, 1, 0), 7, 4, G2)

    g3f = gather_start(coarse_2(F2[7:11].reshape(128, 128)), S["G3f"])
    S["RX2"][0, 7:11] = F2[7:11]
    S["RX2"][1, 7:11] = X2[7:11]

    finish(g3k)
    finish(swap_start(S["G3k"]))

    def unpack3(slots, dst):
        for s in range(NGX):
            t = slots[s]
            dst[5 + 2 * s] = jnp.where(lane16 < 64, t, 0.0)
            dst[6 + 2 * s] = jnp.where(lane16 < 64, pltpu.roll(t, 64, 1), 0.0)

    unpack3(S["G3k"], L3["K"])
    zero3 = jnp.zeros((5, 16, 128), F32)
    for ref in (L3["K"], L3["Va"], L3["Vb"], X3):
        ref[0:5] = zero3
        ref[5 + NX3:10 + NX3] = zero3
    weights(L3, 5, 5 + NX3, 0.5 * 0.25 ** 3, True, 4)


    def compact4(v):
        v = v.reshape(4, 32, 128)
        return (v[0] + pltpu.roll(v[1], 32, 1)) + (pltpu.roll(v[2], 64, 1) + pltpu.roll(v[3], 96, 1))

    def spread4(v):
        return jnp.concatenate([v] + [pltpu.roll(v, 128 - 32 * c, 1) for c in (1, 2, 3)], axis=0)

    h4 = 0.5 * 0.25 ** 4
    k4 = coarse_3(L3["K"][5:5 + NX3].reshape(16 * NX3, 128))
    k4 = compact4(k4)
    row4, lane4 = iota((32, 128), 0), iota((32, 128), 1)
    x_first, x_last = (row4 < 8) & (lane4 < 32), (row4 >= 24) & (lane4 >= 96)
    y_first, y_last = (row4 & 7) == 0, (row4 & 7) == 7
    z_first, z_last = (lane4 & 31) == 0, (lane4 & 31) == 31

    def xup(v):
        return jnp.concatenate([v[8:32], pltpu.roll(v[0:8], 96, 1)], axis=0)

    def xdown(v):
        return jnp.concatenate([pltpu.roll(v[24:32], 32, 1), v[0:24]], axis=0)

    k4xu, k4xd = jnp.where(x_last, 0.0, xup(k4)), jnp.where(x_first, 0.0, xdown(k4))
    k4yu, k4yd = jnp.where(y_last, 0.0, up(k4, 0)), jnp.where(y_first, 0.0, down(k4, 0))
    k4zu, k4zd = jnp.where(z_last, 0.0, up(k4, 1)), jnp.where(z_first, 0.0, down(k4, 1))
    wx4 = jnp.where(x_last, 0.0, h4 * (k4 + k4xu))
    wy4 = jnp.where(y_last, 0.0, h4 * (k4 + k4yu))
    wz4 = jnp.where(z_last, 0.0, h4 * (k4 + k4zu))
    dg4 = h4 * (6.0 * k4 + ((k4xu + k4xd) + (k4yu + k4yd) + (k4zu + k4zd)))

    finish(g3f)
    xx2r = begin(x_copies(S["RX2"], 4, 2))
    xy1r = begin(xy_copies(S["RX1"], 6, 8, H1R, 8))
    finish(swap_start(S["G3f"]))
    unpack3(S["G3f"], F3)
    presmooth(L3, F3, X3, (0, 0, 0, 0), 5, NX3, G3, whole=True)

    f4 = coarse_3(F3[5:5 + NX3].reshape(16 * NX3, 128))
    f4 = compact4(f4)
    x4 = jnp.zeros_like(f4)
    r4 = p4 = f4

    def total4(v):
        t = (v[0:8] + v[8:16]) + (v[16:24] + v[24:32])
        t = jnp.broadcast_to(jnp.sum(t, axis=1, keepdims=True), (8, 128))
        for step in (4, 2, 1):
            t = t + pltpu.roll(t, step, 0)
        return t

    def times4(c, v):
        return (c[None] * v.reshape(4, 8, 128)).reshape(32, 128)

    rr = total4(r4 * r4)
    for _ in range(CG_ITERS):
        q4 = dg4 * p4 - (
            (wx4 * xup(p4) + xdown(wx4 * p4))
            + (wy4 * up(p4, 0) + down(wy4 * p4, 0))
            + (wz4 * up(p4, 1) + down(wz4 * p4, 1)))
        alpha = rr / total4(p4 * q4)
        x4 = x4 + times4(alpha, p4)
        r4 = r4 - times4(alpha, q4)
        rn = total4(r4 * r4)
        p4 = r4 + times4(rn / rr, p4)
        rr = rn

    L3["Va"][5:5 + NX3] = fine_3(spread4(x4)).reshape(NX3, 16, 128)
    postsmooth(L3, F3, X3, (0, 0, 0, 0), 5, NX3, G3)

    finish(xx2r)
    z3 = sel((128, 128), lambda c, l: (l >> 1) == c, 1.0)
    y3 = sel((32, 16), lambda r, c: (r >> 1) == c, 1.0)
    t = mmr(X3[pl.ds(2 * gx + 1, 10)].reshape(160, 128), z3)
    for q in range(10):
        e = mml(y3, t[16 * q:16 * q + 16])
        for p in (2 * q - 1, 2 * q):
            if 0 <= p < 18:
                L2["Va"][p] = e
    R2b, X2b = S["RX2"].at[0], S["RX2"].at[1]
    postsmooth(L2, R2b, X2b, (6, 5, 4, 3), 7, 4, G2)

    finish(xy1r)
    z2 = sel((128, 128), lambda c, l: ((lane1(l) >> 1) == c) & (lane1(l) >= 0) & (lane1(l) < NZ1), 1.0)

    def yrow(r):
        return 8 * gy + r - 8

    y2 = sel((24, 32), lambda r, c: ((yrow(r) >> 1) == c) & (yrow(r) >= 0) & (yrow(r) < NY1), 1.0)
    t = mmr(X2b[4:14].reshape(320, 128), z2)
    for q in range(10):
        e = mml(y2, t[32 * q:32 * q + 32])
        e = e * xin(4 * gx + q - 3, NX1 // 2)
        L1["Va"][2 * q] = e
        L1["Va"][2 * q + 1] = e
    R1b, X1b = S["RX1"].at[0], S["RX1"].at[1]
    postsmooth(L1, R1b, X1b, (5, 4, 3, 2), 6, 8, G1)

    finish(xy0r)
    unpack0(E0r, 0, H0R, -3, 19, put_r)

    def zfine(c, l):
        z = jnp.where(l < 192, l, l - 256)
        g = 128 * gz + z
        return (((z >> 1) & 127) == c) & (g >= 0) & (g < NZ0)

    def yfine(r, c):
        g = 16 * gy + r - 8
        return (((r - 8) >> 1) + 8 == c) & (g >= 0) & (g < NY0)

    z1 = sel((128, 256), zfine, 1.0)
    y1 = sel((32, 24), yfine, 1.0)
    t = mmr(X1b[4:16].reshape(288, 128), z1)
    for q in range(12):
        e = mml(y1, t[24 * q:24 * q + 24])
        e = e * xin(8 * gx + q - 2, NX1)
        L0["Va"][1 + 2 * q] = e
        L0["Va"][2 + 2 * q] = e
    postsmooth(L0, R0, X0, (3, 2, 1, 0), 5, 16, G0, part=OWN0, out=out_ref)


def scratch(sizes):
    ngx, ngy, ngz = sizes
    n_pair = 2 * ngz - 1
    shapes = {
        "C3": (16, 128), "M0": (2, 4, 32, 128),
        "P1": (1, 8, 128), "Z1L": (3, 24, 128), "Z1R": (3, 24, 128),
        "P0": (2, 2, 16, 128), "P0L": (2, 2, 16, 128), "P0R": (2, 2, 16, 128),
        "E0": (2, 16 + 2 * H0, 32, 128),
        "P0r": (1, 2, 16, 128), "P0rL": (1, 2, 16, 128), "P0rR": (1, 2, 16, 128),
        "E0r": (1, 18 + 2 * (H0R + 1), 32, 128),
        "R0": (26, 32, 256), "X0": (26, 16, 128), "K0": (26, 32, 256),
        "T1r": (2, 8, 8, 128), "T1rL": (2, 8, 8, 128), "T1rR": (2, 8, 8, 128),
        "K1": (1, 20, 24, 128), "F1": (1, 20, 24, 128), "RX1": (2, 20, 24, 128), "X1": (20, 24, 128),
        "K2": (1, 18, 32, 128), "F2": (1, 18, 32, 128), "RX2": (2, 18, 32, 128), "X2": (18, 32, 128),
        "B2k": (8, 128), "B2kS": (n_pair, 8, 128),
        "B2f": (8, 128), "B2fS": (n_pair, 8, 128),
        "G3k": (ngx, 16, 128), "G3f": (ngx, 16, 128),
        "K3": (2 * ngx + 10, 16, 128), "F3": (2 * ngx + 10, 16, 128), "X3": (2 * ngx + 10, 16, 128),
    }
    for n in ("T1k", "T1f"):
        for side in ("", "L", "R"):
            shapes[n + side] = (1, 8, 8, 128)
    for n in ("WX", "WY", "WZ", "DG", "IV", "Va", "Vb"):
        shapes[n + "0"] = (26, 32, 256)
        shapes[n + "1"] = (20, 24, 128)
        shapes[n + "2"] = (18, 32, 128)
        shapes[n + "3"] = (2 * ngx + 10, 16, 128)
    names = list(shapes) + ["ss", "rs", "ls", "dis"]
    n_sem = 74 + 2 * (n_pair + 3 * (ngy // 2) - 1) + 2 + 4 + 2 * ngx
    kinds = [pltpu.VMEM(shapes[n], F32) for n in shapes]
    kinds += [pltpu.SemaphoreType.DMA((n_sem,)), pltpu.SemaphoreType.DMA((n_sem,))]
    kinds += [pltpu.SemaphoreType.DMA((2,)), pltpu.SemaphoreType.REGULAR((3,))]
    return names, kinds


def solution(mesh):
    sizes = (mesh.shape["gx"], mesh.shape["gy"], mesh.shape["gz"])
    names, kinds = scratch(sizes)
    spec = P("gx", "gy", "gz")

    def local(right_side, conductivity):
        return pl.pallas_call(
            functools.partial(kernel, sizes, names),
            out_shape=jax.ShapeDtypeStruct(right_side.shape, F32),
            in_specs=[pl.BlockSpec(memory_space=pl.ANY)] * 2,
            out_specs=pl.BlockSpec(memory_space=pltpu.VMEM),
            scratch_shapes=kinds,
            compiler_params=pltpu.CompilerParams(
                collective_id=0, has_side_effects=True, vmem_limit_bytes=57 * 1024 * 1024
            ),
        )(right_side, conductivity)

    return jax.shard_map(local, mesh=mesh, in_specs=(spec, spec), out_specs=spec, check_vma=False)
```
